256 devices in a mesh: gx: 32 (over z, y_hi, core), gy: 8 (over x, y_lo).
Axes of the slice: x: 4, y: 4 (y_hi: 2, y_lo: 2; y = y_hi * 2 + y_lo), z: 8, core: 2. Of those that a mesh axis runs over, the one named last changes fastest.
Arguments:
- populations: float32 [19, 512, 64, 128], P(None, 'gx', 'gy'), may hold values from 0.02 to 0.2
- order_pops: float32 [19, 512, 64, 128], P(None, 'gx', 'gy'), may hold values from -0.1 to 0.1
- plane_offsets: int32 [32], replicated, may hold values from 0 to 63
Outputs:
- read_flow: float32 [19, 512, 64, 128], P(None, 'gx', 'gy')
- read_order: float32 [19, 512, 64, 128], P(None, 'gx', 'gy')
The draws below stay inside these ranges and needn't reach their ends.
All inputs are finite; a program needn't handle non-finite values.
Results may differ from the reference program's by a relative error of at most 0.00002.
Values sent between devices are 32-bit elements; how exact they have to be, the bound alone decides.
No kernel may reach another device: no remote copies, remote signals or barrier semaphores. Data moves between devices by JAX's collectives and lax.ppermute only.
A program may use at most 64 MiB of HBM per device.

```python
import jax
import jax.numpy as jnp
from jax import lax

VELS = 19
CX = 16
CZ = 128
NX = 512
NY = 64
N_GX = 32


def set_ends(drawn, stream_key, low, high):
    index_at = [jax.random.randint(jax.random.fold_in(stream_key, axis), (), 0, length) for axis, length in enumerate(drawn.shape)]
    widest = drawn.shape.index(max(drawn.shape))
    next_to = index_at[:widest] + [(index_at[widest] + 1) % drawn.shape[widest]] + index_at[widest + 1:]
    return drawn.at[tuple(index_at)].set(low).at[tuple(next_to)].set(high)


def block_scale(key, dims, cuts, smallest, largest):
    level, own = 1.0, jax.random.fold_in(key, 6)
    for axis_at, shards_of in cuts:
        draws = jnp.exp(jax.random.uniform(jax.random.fold_in(own, axis_at), (shards_of,), jnp.float32, smallest / len(cuts), largest / len(cuts)))
        level = level * jnp.repeat(draws, dims[axis_at] // shards_of).reshape([-1 if axis == axis_at else 1 for axis in range(len(dims))])
    return level


def setup_inputs(seed: int = 0) -> dict:
    seeds = jax.random.split(jax.random.key(seed), 4)
    return {
        "populations": jnp.clip(0.02 + 0.18 * jax.random.uniform(seeds[0], (VELS, NX, NY, CZ), jnp.float32) ** block_scale(seeds[0], (VELS, NX, NY, CZ), ((1, 32), (2, 8)), -0.2, 0.2), 0.02, 0.2),
        "order_pops": jnp.clip(jax.random.uniform(seeds[1], (VELS, NX, NY, CZ), jnp.float32, -0.1, 0.1) * block_scale(seeds[1], (VELS, NX, NY, CZ), ((1, 32), (2, 8)), -0.4, 0.0), -0.1, 0.1),
        "plane_offsets": set_ends(jax.random.randint(seeds[2], (N_GX,), 0, NY), jax.random.fold_in(seeds[2], 1), 0, NY - 1).astype(jnp.int32),
    }


SHIFT_FRACTION = 0.375
WALL_SPEED = 0.05
RELAX_FLOW = 0.8
RELAX_ORDER = 0.9
BULK_COEFF = 0.05
SURFACE_COEFF = 0.04
MOBILITY = 1.0
VELOCITY_X = (0, 1, -1, 0, 0, 0, 0, 1, -1, 1, -1, 1, -1, 1, -1, 0, 0, 0, 0)
VELOCITY_Y = (0, 0, 0, 1, -1, 0, 0, 1, -1, -1, 1, 0, 0, 0, 0, 1, -1, 1, -1)
VELOCITY_Z = (0, 0, 0, 0, 0, 1, -1, 0, 0, 0, 0, 1, -1, -1, 1, 1, -1, -1, 1)
WEIGHT_TABLE = (1.0 / 3.0,) + (1.0 / 18.0,) * 6 + (1.0 / 36.0,) * 12


def column(values):
    return jnp.array(values, jnp.float32)[:, None, None, None]


def laplace(extended):
    center = extended[..., 1:-1, 1:-1, :]
    total = extended[..., 2:, 1:-1, :] + extended[..., :-2, 1:-1, :]
    total = total + extended[..., 1:-1, 2:, :] + extended[..., 1:-1, :-2, :]
    total = total + jnp.roll(center, 1, -1) + jnp.roll(center, -1, -1)
    return total - 6.0 * center


def gradient(extended):
    center = extended[..., 1:-1, 1:-1, :]
    along_x = 0.5 * (extended[..., 2:, 1:-1, :] - extended[..., :-2, 1:-1, :])
    along_y = 0.5 * (extended[..., 1:-1, 2:, :] - extended[..., 1:-1, :-2, :])
    along_z = 0.5 * (jnp.roll(center, -1, -1) - jnp.roll(center, 1, -1))
    return jnp.stack([along_x, along_y, along_z], -4)


def collide(flow, order, phase, potential, force):
    weights = column(WEIGHT_TABLE)
    vel_x, vel_y, vel_z = column(VELOCITY_X), column(VELOCITY_Y), column(VELOCITY_Z)
    density = jnp.sum(flow, 0)
    speed_x = (jnp.sum(vel_x * flow, 0) + 0.5 * force[0]) / density
    speed_y = (jnp.sum(vel_y * flow, 0) + 0.5 * force[1]) / density
    speed_z = (jnp.sum(vel_z * flow, 0) + 0.5 * force[2]) / density
    speed_sq = speed_x * speed_x + speed_y * speed_y + speed_z * speed_z
    along = vel_x * speed_x + vel_y * speed_y + vel_z * speed_z
    pushed = vel_x * force[0] + vel_y * force[1] + vel_z * force[2]
    work_done = speed_x * force[0] + speed_y * force[1] + speed_z * force[2]
    balance = weights * density * (1.0 + 3.0 * along + 4.5 * along * along - 1.5 * speed_sq)
    source = (1.0 - 0.5 / RELAX_FLOW) * weights * (3.0 * (pushed - work_done) + 9.0 * along * pushed)
    flow_post = flow - (flow - balance) / RELAX_FLOW + source
    order_terms = weights * (3.0 * MOBILITY * potential + 3.0 * phase * along)
    rest_term = phase - jnp.sum(order_terms[1:], 0)
    order_balance = jnp.concatenate([rest_term[None], order_terms[1:]], 0)
    order_post = order - (order - order_balance) / RELAX_ORDER
    return flow_post, order_post


def stream(widened):
    planes = widened.shape[1] - 2
    height = widened.shape[2] - 2
    moved = []
    for index_comp in range(widened.shape[0]):
        vel = index_comp % 19
        step_x, step_y, step_z = VELOCITY_X[vel], VELOCITY_Y[vel], VELOCITY_Z[vel]
        piece = widened[index_comp, 1 - step_x:1 - step_x + planes, 1 - step_y:1 - step_y + height, :]
        moved.append(jnp.roll(piece, step_z, -1))
    return jnp.stack(moved, 0)


def shear_kick(planes, speed):
    density = jnp.sum(planes[:19], 0)
    factor = jnp.array(WEIGHT_TABLE, jnp.float32) * jnp.array(VELOCITY_Y, jnp.float32) * 3.0
    kick = factor[:, None, None] * density[None] * speed
    return planes + jnp.concatenate([kick, jnp.zeros_like(kick)], 0)


def shear_rows(plane, shift, weight):
    upper = jnp.roll(plane, shift, axis=1)
    lower = jnp.roll(plane, shift + 1, axis=1)
    return weight * upper + (1.0 - weight) * lower


def ghost_pair(slabs, low_shift, high_shift, add_kick):
    below = jnp.roll(slabs[:, :, -1], 1, 0)
    above = jnp.roll(slabs[:, :, 0], -1, 0)
    shearing = jax.vmap(shear_rows, in_axes=(0, 0, None))
    below = shearing(below, low_shift, 1.0 - SHIFT_FRACTION)
    above = shearing(above, high_shift, SHIFT_FRACTION)
    if add_kick:
        below = jax.vmap(shear_kick, in_axes=(0, None))(below, WALL_SPEED)
        above = jax.vmap(shear_kick, in_axes=(0, None))(above, -WALL_SPEED)
    return below, above


def widen(slab, below, above):
    extended = jnp.concatenate([below[:, None], slab, above[:, None]], 1)
    return jnp.concatenate([extended[:, :, -1:], extended, extended[:, :, :1]], 2)


def slabs_of(array):
    return array.reshape(array.shape[0], N_GX, CX, NY, CZ).transpose(1, 0, 2, 3, 4)


def collide_slab(items):
    flow, order, phase, potential, force = items
    flow_post, order_post = collide(flow, order, phase, potential, force)
    return jnp.concatenate([flow_post, order_post], 0)


def stream_slab(items):
    slab, below, above = items
    return stream(widen(slab, below, above))


def reference(populations, order_pops, plane_offsets):
    flow_slabs = slabs_of(populations)
    order_slabs = slabs_of(order_pops)
    low_shift = plane_offsets.astype(jnp.int32)
    high_shift = (NY - 1 - jnp.roll(plane_offsets, -1)).astype(jnp.int32)
    phase = jnp.sum(order_slabs, 1)
    below, above = ghost_pair(phase[:, None], low_shift, high_shift, False)
    phase_wide = jax.vmap(widen)(phase[:, None], below, above)[:, 0]
    potential = BULK_COEFF * (phase * phase * phase - phase) - SURFACE_COEFF * laplace(phase_wide)
    below, above = ghost_pair(potential[:, None], low_shift, high_shift, False)
    potential_wide = jax.vmap(widen)(potential[:, None], below, above)[:, 0]
    force = -phase[:, None] * gradient(potential_wide)
    collided = lax.map(collide_slab, (flow_slabs, order_slabs, phase, potential, force))
    below, above = ghost_pair(collided, low_shift, high_shift, True)
    result = lax.map(stream_slab, (collided, below, above))
    result = result.transpose(1, 0, 2, 3, 4).reshape(38, NX, NY, CZ)
    return result[:19], result[19:]
```

```python
import jax
import jax.numpy as jnp
from jax import lax
from jax.experimental import pallas as pl
from jax.experimental.pallas import tpu as pltpu
from jax.sharding import PartitionSpec as P

SHIFT_FRACTION = 0.375
WALL_SPEED = 0.05
RELAX_FLOW = 0.8
RELAX_ORDER = 0.9
BULK_COEFF = 0.05
SURFACE_COEFF = 0.04
MOBILITY = 1.0
VELOCITY_X = (0, 1, -1, 0, 0, 0, 0, 1, -1, 1, -1, 1, -1, 1, -1, 0, 0, 0, 0)
VELOCITY_Y = (0, 0, 0, 1, -1, 0, 0, 1, -1, -1, 1, 0, 0, 0, 0, 1, -1, 1, -1)
VELOCITY_Z = (0, 0, 0, 0, 0, 1, -1, 0, 0, 0, 0, 1, -1, -1, 1, 1, -1, -1, 1)
WEIGHT_TABLE = (1.0 / 3.0,) + (1.0 / 18.0,) * 6 + (1.0 / 36.0,) * 12

VELS = 19
PLANES = 16
ROWS = 8
LANES = 128
UP_X = tuple(i for i in range(VELS) if VELOCITY_X[i] == 1)
DOWN_X = tuple(i for i in range(VELS) if VELOCITY_X[i] == -1)
UP_Y = tuple(i for i in range(VELS) if VELOCITY_Y[i] == 1)
DOWN_Y = tuple(i for i in range(VELS) if VELOCITY_Y[i] == -1)
PAYLOAD = 17
AT_MOMENTS = 5
AT_ORDER = 9
AT_PHASE = 14
WINDOW = 16
WINDOW_PAD = 4

VMEM_LIMIT = 40 * 1024 * 1024


def roll_rows(cells, step):
    return pltpu.roll(cells, step % cells.shape[0], 0)


def roll_lanes(cells, step):
    return pltpu.roll(cells, step % LANES, cells.ndim - 1)


def moments(flow):
    parts = [flow(i) for i in range(VELS)]
    density = parts[0]
    for part in parts[1:]:
        density = density + part
    speeds = []
    for table in (VELOCITY_X, VELOCITY_Y, VELOCITY_Z):
        plus = [parts[i] for i in range(VELS) if table[i] == 1]
        minus = [parts[i] for i in range(VELS) if table[i] == -1]
        total = plus[0] - minus[0]
        for a, b in zip(plus[1:], minus[1:]):
            total = total + (a - b)
        speeds.append(total)
    return density, speeds


def potential_of(phase, neighbours):
    around = neighbours[0]
    for cells in neighbours[1:]:
        around = around + cells
    bulk = BULK_COEFF * (phase * phase * phase - phase)
    return bulk - SURFACE_COEFF * (around - 6.0 * phase)


def dot_velocity(i, vector):
    total = None
    for sign, part in zip((VELOCITY_X[i], VELOCITY_Y[i], VELOCITY_Z[i]), vector):
        if sign == 0:
            continue
        if total is None:
            total = part if sign == 1 else -part
        else:
            total = total + part if sign == 1 else total - part
    return total


def collide(wanted, flow, order, density, momentum, phase, potential, force):
    inverse = 1.0 / density
    speed = [(momentum[d] + 0.5 * force[d]) * inverse for d in range(3)]
    source = 1.0 - 0.5 / RELAX_FLOW
    relaxed = density * (1.0 / RELAX_FLOW)
    speed_sq = speed[0] * speed[0] + speed[1] * speed[1] + speed[2] * speed[2]
    work = speed[0] * force[0] + speed[1] * force[1] + speed[2] * force[2]
    even = relaxed * (1.0 - 1.5 * speed_sq) - (3.0 * source) * work
    odd = [3.0 * (relaxed * speed[d] + source * force[d]) for d in range(3)]
    quad = [4.5 * relaxed * speed[d] + (9.0 * source) * force[d] for d in range(3)]
    order_even = (3.0 * MOBILITY / RELAX_ORDER) * potential
    carried = (3.0 / RELAX_ORDER) * phase
    order_odd = [carried * speed[d] for d in range(3)]
    flow_out, order_out = {}, {}
    keep_flow = 1.0 - 1.0 / RELAX_FLOW
    keep_order = 1.0 - 1.0 / RELAX_ORDER
    done = set()
    for i in wanted:
        if i in done:
            continue
        weight = WEIGHT_TABLE[i]
        if i == 0:
            flow_out[0] = keep_flow * flow(0) + weight * even
            rest = phase - (2.0 * MOBILITY) * potential
            order_out[0] = keep_order * order(0) + (1.0 / RELAX_ORDER) * rest
            continue
        first = i if i % 2 == 1 else i - 1
        pair_even = weight * (even + dot_velocity(first, speed) * dot_velocity(first, quad))
        pair_odd = weight * dot_velocity(first, odd)
        pair_order = weight * dot_velocity(first, order_odd)
        for member, sign in ((first, 1), (first + 1, -1)):
            if member not in wanted:
                continue
            done.add(member)
            both = pair_even + pair_odd if sign == 1 else pair_even - pair_odd
            flow_out[member] = keep_flow * flow(member) + both
            both = weight * order_even
            both = both + pair_order if sign == 1 else both - pair_order
            order_out[member] = keep_order * order(member) + both
    return flow_out, order_out


def gather_kernel(flow_ref, order_ref, phase_ref, bound_ref, low_ref, high_ref):
    for x in range(PLANES):
        total = order_ref[0, x]
        for i in range(1, VELS):
            total = total + order_ref[i, x]
        phase_ref[x] = total
    copies = bound_ref.shape[0]
    for side, (plane, inward, comps) in enumerate(((PLANES - 1, -1, UP_X), (0, 1, DOWN_X))):
        density, momentum = moments(lambda i: flow_ref[i, plane])
        parts = [flow_ref[i, plane] for i in comps] + [density] + momentum
        parts += [order_ref[i, plane] for i in comps]
        parts += [phase_ref[plane + inward * d] for d in range(3)]
        for index, part in enumerate(parts):
            for copy in range(copies):
                bound_ref[copy, side * PAYLOAD + index] = part
    for out_ref, row, inward, comps in ((high_ref, ROWS - 1, -1, UP_Y), (low_ref, 0, 1, DOWN_Y)):
        density, momentum = moments(lambda i: flow_ref[i, :, row, :])
        parts = [flow_ref[i, :, row, :] for i in comps] + [density] + momentum
        parts += [order_ref[i, :, row, :] for i in comps]
        parts += [phase_ref[:, row + inward * d, :] for d in range(3)]
        for index, part in enumerate(parts):
            out_ref[index] = part


def window_kernel(start_ref, whole_ref, up_ref, down_ref):
    blocks = whole_ref.shape[0]
    row = lax.broadcasted_iota(jnp.int32, (ROWS, LANES), 0)
    for side, out_ref in enumerate((up_ref, down_ref)):
        start = start_ref[side]
        block = start // ROWS
        inner = lax.rem(start, ROWS)
        back = lax.rem(ROWS - inner, ROWS)
        early = row < ROWS - inner
        for index in range(PAYLOAD):
            rolled = [
                pltpu.roll(whole_ref[lax.rem(block + d, blocks), side * PAYLOAD + index], back, 0)
                for d in range(3)
            ]
            out_ref[index, 0:ROWS] = jnp.where(early, rolled[0], rolled[1])
            out_ref[index, ROWS : 2 * ROWS] = jnp.where(early, rolled[1], rolled[2])


def ghost_plane(window_ref, comps, own, own_next, weight, kick_speed):
    other = 1.0 - weight

    def sheared(cells):
        return weight * cells + other * roll_rows(cells, 1)

    def seen(cells):
        return other * roll_rows(cells, -1) + weight * cells

    def sides(cells):
        return [roll_rows(cells, 1), roll_rows(cells, -1), roll_lanes(cells, 1), roll_lanes(cells, -1)]

    near, second, third = [window_ref[AT_PHASE + d] for d in range(3)]
    ghost_phase = sheared(near)
    own_potential = potential_of(own, [own_next, ghost_phase] + sides(own))
    near_potential = potential_of(near, [second, seen(own)] + sides(near))
    second_potential = potential_of(second, [third, near] + sides(second))
    beyond = seen(own_potential)
    outward = 1.0 if VELOCITY_X[comps[0]] == 1 else -1.0
    half = -0.5 * near
    force = [
        outward * half * (beyond - second_potential),
        half * (roll_rows(near_potential, -1) - roll_rows(near_potential, 1)),
        half * (roll_lanes(near_potential, -1) - roll_lanes(near_potential, 1)),
    ]
    density = window_ref[AT_MOMENTS]
    momentum = [window_ref[AT_MOMENTS + 1 + d] for d in range(3)]
    flow_out, order_out = collide(
        comps,
        lambda i: window_ref[comps.index(i)],
        lambda i: window_ref[AT_ORDER + comps.index(i)],
        density,
        momentum,
        near,
        near_potential,
        force,
    )
    flow_ghost = []
    for i in comps:
        cells = flow_out[i]
        if VELOCITY_Y[i] != 0:
            cells = cells + (WEIGHT_TABLE[i] * 3.0 * VELOCITY_Y[i] * kick_speed) * density
        flow_ghost.append(sheared(cells))
    order_ghost = [sheared(order_out[i]) for i in comps]
    return ghost_phase, own_potential, sheared(near_potential), flow_ghost, order_ghost


def main_kernel(
    flow_ref, order_ref, phase_ref, low_ref, high_ref, below_ref, above_ref, flow_out, order_out,
    wide_ref, ghost_ref, potential_ref, low_side, high_side, edge_ref,
):
    for index, plane in enumerate((0, 1, PLANES - 1, PLANES - 2)):
        wide_ref[index] = jnp.zeros((WINDOW, LANES), jnp.float32)
        for d in range(3):
            wide_ref[index, 3 - d : 4 - d, :] = low_ref[AT_PHASE + d, plane : plane + 1, :]
            wide_ref[index, 12 + d : 13 + d, :] = high_ref[AT_PHASE + d, plane : plane + 1, :]
        wide_ref[index, 4:12, :] = phase_ref[plane]
    below = ghost_plane(below_ref, UP_X, wide_ref[0], wide_ref[1], 1.0 - SHIFT_FRACTION, WALL_SPEED)
    for index in range(5):
        ghost_ref[index] = below[3][index]
        ghost_ref[5 + index] = below[4][index]
    above = ghost_plane(above_ref, DOWN_X, wide_ref[2], wide_ref[3], SHIFT_FRACTION, -WALL_SPEED)
    for index in range(5):
        ghost_ref[10 + index] = above[3][index]
        ghost_ref[15 + index] = above[4][index]

    row = lax.broadcasted_iota(jnp.int32, (ROWS, LANES), 0)
    plane_at = lax.broadcasted_iota(jnp.int32, (PLANES, LANES), 0)

    def ghosts(cells, own_row):
        return cells[own_row + WINDOW_PAD : own_row + WINDOW_PAD + 1, :]

    def across(cells, ghost_low, ghost_high):
        before = jnp.where(plane_at == 0, ghost_low, roll_rows(cells, 1))
        after = jnp.where(plane_at == PLANES - 1, ghost_high, roll_rows(cells, -1))
        return before, after

    for side_ref, out_ref, edge, beside, inward, comps in (
        (low_ref, low_side, 0, -1, 1, UP_Y),
        (high_ref, high_side, ROWS - 1, ROWS, -1, DOWN_Y),
    ):
        own = [phase_ref[:, edge + inward * d, :] for d in range(2)]
        outer = [side_ref[AT_PHASE + d] for d in range(3)]
        lines = [own[1], own[0]] + outer
        potentials = []
        for index in range(1, 4):
            cells = lines[index]
            own_row = edge + inward * (1 - index)
            around = list(across(cells, ghosts(below[0], own_row), ghosts(above[0], own_row)))
            around += [lines[index - 1], lines[index + 1], roll_lanes(cells, 1), roll_lanes(cells, -1)]
            potentials.append(potential_of(cells, around))
        inside, here, outside = potentials
        before, after = across(here, ghosts(below[2], beside), ghosts(above[2], beside))
        half = -0.5 * outer[0]
        force = [
            half * (after - before),
            (inward * half) * (inside - outside),
            half * (roll_lanes(here, -1) - roll_lanes(here, 1)),
        ]
        flow_post, order_post = collide(
            comps,
            lambda i: side_ref[comps.index(i)],
            lambda i: side_ref[AT_ORDER + comps.index(i)],
            side_ref[AT_MOMENTS],
            [side_ref[AT_MOMENTS + 1 + d] for d in range(3)],
            outer[0],
            here,
            force,
        )
        for index, i in enumerate(comps):
            out_ref[index] = flow_post[i]
            out_ref[5 + index] = order_post[i]
        edge_ref[0 if inward == 1 else 1] = here

    def above_row(cells, line):
        return jnp.where(row == 0, line, roll_rows(cells, 1))

    def below_row(cells, line):
        return jnp.where(row == ROWS - 1, line, roll_rows(cells, -1))

    wide_ref[0] = below[1]
    wide_ref[1] = below[2]
    wide_ref[2] = above[1]
    wide_ref[3] = above[2]
    potential_ref[1] = wide_ref[0, 4:12, :]
    potential_ref[0] = wide_ref[1, 4:12, :]
    potential_ref[PLANES] = wide_ref[2, 4:12, :]
    potential_ref[PLANES + 1] = wide_ref[3, 4:12, :]
    for x in range(1, PLANES - 1):
        cells = phase_ref[x]
        around = [
            phase_ref[x - 1],
            phase_ref[x + 1],
            above_row(cells, low_ref[AT_PHASE, x : x + 1, :]),
            below_row(cells, high_ref[AT_PHASE, x : x + 1, :]),
            roll_lanes(cells, 1),
            roll_lanes(cells, -1),
        ]
        potential_ref[x + 1] = potential_of(cells, around)

    def moved(i, cells, index_low, index_high, x):
        if VELOCITY_Y[i] == 1:
            cells = above_row(cells, low_side[index_low + UP_Y.index(i), pl.ds(x, 1), :])
        elif VELOCITY_Y[i] == -1:
            cells = below_row(cells, high_side[index_high + DOWN_Y.index(i), pl.ds(x, 1), :])
        if VELOCITY_Z[i] != 0:
            cells = roll_lanes(cells, VELOCITY_Z[i])
        return cells

    def one_plane(x, skip):
        here = potential_ref[x + 1]
        phase = phase_ref[x]
        half = -0.5 * phase
        force = [
            half * (potential_ref[x + 2] - potential_ref[x]),
            half
            * (
                below_row(here, edge_ref[1, pl.ds(x, 1), :])
                - above_row(here, edge_ref[0, pl.ds(x, 1), :])
            ),
            half * (roll_lanes(here, -1) - roll_lanes(here, 1)),
        ]
        density, momentum = moments(lambda i: flow_ref[i, x])
        flow_post, order_post = collide(
            tuple(i for i in range(VELS) if VELOCITY_X[i] == 0 or VELOCITY_X[i] != skip),
            lambda i: flow_ref[i, x],
            lambda i: order_ref[i, x],
            density,
            momentum,
            phase,
            here,
            force,
        )
        for i in flow_post:
            target = x + VELOCITY_X[i]
            flow_out[i, target] = moved(i, flow_post[i], 0, 0, x)
            order_out[i, target] = moved(i, order_post[i], 5, 5, x)

    one_plane(0, -1)

    def step(x, carry):
        one_plane(x, 0)
        return carry

    lax.fori_loop(1, PLANES - 1, step, 0)
    one_plane(PLANES - 1, 1)

    for comps, first, target in ((UP_X, 0, 0), (DOWN_X, 10, PLANES - 1)):
        for index, i in enumerate(comps):
            start = WINDOW_PAD - VELOCITY_Y[i]
            for out_ref, at in ((flow_out, first + index), (order_out, first + 5 + index)):
                cells = ghost_ref[at, start : start + ROWS, :]
                if VELOCITY_Z[i] != 0:
                    cells = roll_lanes(cells, VELOCITY_Z[i])
                out_ref[i, target] = cells


def vmem(count):
    return [pl.BlockSpec(memory_space=pltpu.VMEM)] * count


def params():
    return pltpu.CompilerParams(vmem_limit_bytes=VMEM_LIMIT)


def f32(*shape):
    return jax.ShapeDtypeStruct(shape, jnp.float32)


def shift_pairs(count, step):
    return [(i, (i + step) % count) for i in range(count)]


def shards(populations, order_pops, plane_offsets):
    slabs, strips = lax.axis_size("gx"), lax.axis_size("gy")
    slab, strip = lax.axis_index("gx"), lax.axis_index("gy")
    height = strips * ROWS
    first_row = strip * ROWS
    starts = jnp.stack(
        [
            (first_row - WINDOW_PAD - plane_offsets[(slab + 1) % slabs]) % height,
            (first_row - WINDOW_PAD + 1 + plane_offsets[slab]) % height,
        ]
    ).astype(jnp.int32)

    phase, bound, to_low, to_high = pl.pallas_call(
        gather_kernel,
        out_shape=(
            f32(PLANES, ROWS, LANES),
            f32(strips, 2 * PAYLOAD, ROWS, LANES),
            f32(PAYLOAD, PLANES, LANES),
            f32(PAYLOAD, PLANES, LANES),
        ),
        in_specs=vmem(2),
        out_specs=tuple(vmem(4)),
        compiler_params=params(),
        name="payloads",
    )(populations, order_pops)

    from_low = lax.ppermute(to_high, "gy", shift_pairs(strips, 1))
    from_high = lax.ppermute(to_low, "gy", shift_pairs(strips, -1))
    whole = lax.all_to_all(bound, "gy", 0, 0, tiled=True)

    up, down = pl.pallas_call(
        window_kernel,
        out_shape=(f32(PAYLOAD, WINDOW, LANES), f32(PAYLOAD, WINDOW, LANES)),
        in_specs=[pl.BlockSpec(memory_space=pltpu.SMEM)] + vmem(1),
        out_specs=tuple(vmem(2)),
        compiler_params=params(),
        name="windows",
    )(starts, whole)

    below = lax.ppermute(up, "gx", shift_pairs(slabs, 1))
    above = lax.ppermute(down, "gx", shift_pairs(slabs, -1))

    return pl.pallas_call(
        main_kernel,
        out_shape=(f32(*populations.shape), f32(*order_pops.shape)),
        in_specs=vmem(7),
        out_specs=tuple(vmem(2)),
        scratch_shapes=[
            pltpu.VMEM((4, WINDOW, LANES), jnp.float32),
            pltpu.VMEM((20, WINDOW, LANES), jnp.float32),
            pltpu.VMEM((PLANES + 2, ROWS, LANES), jnp.float32),
            pltpu.VMEM((10, PLANES, LANES), jnp.float32),
            pltpu.VMEM((10, PLANES, LANES), jnp.float32),
            pltpu.VMEM((2, PLANES, LANES), jnp.float32),
        ],
        compiler_params=params(),
        name="collide_stream",
    )(populations, order_pops, phase, from_low, from_high, below, above)


def solution(mesh):
    return jax.shard_map(
        shards,
        mesh=mesh,
        in_specs=(P(None, "gx", "gy", None), P(None, "gx", "gy", None), P()),
        out_specs=(P(None, "gx", "gy", None), P(None, "gx", "gy", None)),
        check_vma=False,
    )
```

```python
import jax
import jax.numpy as jnp
from jax import lax
from jax.experimental import pallas as pl
from jax.experimental.pallas import tpu as pltpu
from jax.sharding import PartitionSpec as P

SHIFT_FRACTION = 0.375
WALL_SPEED = 0.05
RELAX_FLOW = 0.8
RELAX_ORDER = 0.9
BULK_COEFF = 0.05
SURFACE_COEFF = 0.04
MOBILITY = 1.0
VELOCITY_X = (0, 1, -1, 0, 0, 0, 0, 1, -1, 1, -1, 1, -1, 1, -1, 0, 0, 0, 0)
VELOCITY_Y = (0, 0, 0, 1, -1, 0, 0, 1, -1, -1, 1, 0, 0, 0, 0, 1, -1, 1, -1)
VELOCITY_Z = (0, 0, 0, 0, 0, 1, -1, 0, 0, 0, 0, 1, -1, -1, 1, 1, -1, -1, 1)
WEIGHT_TABLE = (1.0 / 3.0,) + (1.0 / 18.0,) * 6 + (1.0 / 36.0,) * 12

VELS = 19
PLANES = 16
ROWS = 8
LANES = 128
UP_X = tuple(i for i in range(VELS) if VELOCITY_X[i] == 1)
DOWN_X = tuple(i for i in range(VELS) if VELOCITY_X[i] == -1)
UP_Y = tuple(i for i in range(VELS) if VELOCITY_Y[i] == 1)
DOWN_Y = tuple(i for i in range(VELS) if VELOCITY_Y[i] == -1)
PAYLOAD = 17
AT_MOMENTS = 5
AT_ORDER = 9
AT_PHASE = 14
WINDOW = 16
WINDOW_PAD = 4

VMEM_LIMIT = 40 * 1024 * 1024


def roll_rows(cells, step):
    return pltpu.roll(cells, step % cells.shape[0], 0)


def roll_lanes(cells, step):
    return pltpu.roll(cells, step % LANES, cells.ndim - 1)


def moments(flow):
    parts = [flow(i) for i in range(VELS)]
    density = parts[0]
    for part in parts[1:]:
        density = density + part
    speeds = []
    for table in (VELOCITY_X, VELOCITY_Y, VELOCITY_Z):
        plus = [parts[i] for i in range(VELS) if table[i] == 1]
        minus = [parts[i] for i in range(VELS) if table[i] == -1]
        total = plus[0] - minus[0]
        for a, b in zip(plus[1:], minus[1:]):
            total = total + (a - b)
        speeds.append(total)
    return density, speeds


def potential_of(phase, neighbours):
    around = neighbours[0]
    for cells in neighbours[1:]:
        around = around + cells
    bulk = BULK_COEFF * (phase * phase * phase - phase)
    return bulk - SURFACE_COEFF * (around - 6.0 * phase)


def dot_velocity(i, vector):
    total = None
    for sign, part in zip((VELOCITY_X[i], VELOCITY_Y[i], VELOCITY_Z[i]), vector):
        if sign == 0:
            continue
        if total is None:
            total = part if sign == 1 else -part
        else:
            total = total + part if sign == 1 else total - part
    return total


def collide(wanted, flow, order, density, momentum, phase, potential, force):
    inverse = 1.0 / density
    speed = [(momentum[d] + 0.5 * force[d]) * inverse for d in range(3)]
    source = 1.0 - 0.5 / RELAX_FLOW
    relaxed = density * (1.0 / RELAX_FLOW)
    speed_sq = speed[0] * speed[0] + speed[1] * speed[1] + speed[2] * speed[2]
    work = speed[0] * force[0] + speed[1] * force[1] + speed[2] * force[2]
    even = relaxed * (1.0 - 1.5 * speed_sq) - (3.0 * source) * work
    odd = [3.0 * (relaxed * speed[d] + source * force[d]) for d in range(3)]
    quad = [4.5 * relaxed * speed[d] + (9.0 * source) * force[d] for d in range(3)]
    order_even = (3.0 * MOBILITY / RELAX_ORDER) * potential
    carried = (3.0 / RELAX_ORDER) * phase
    order_odd = [carried * speed[d] for d in range(3)]
    flow_out, order_out = {}, {}
    keep_flow = 1.0 - 1.0 / RELAX_FLOW
    keep_order = 1.0 - 1.0 / RELAX_ORDER
    done = set()
    for i in wanted:
        if i in done:
            continue
        weight = WEIGHT_TABLE[i]
        if i == 0:
            flow_out[0] = keep_flow * flow(0) + weight * even
            rest = phase - (2.0 * MOBILITY) * potential
            order_out[0] = keep_order * order(0) + (1.0 / RELAX_ORDER) * rest
            continue
        first = i if i % 2 == 1 else i - 1
        pair_even = weight * (even + dot_velocity(first, speed) * dot_velocity(first, quad))
        pair_odd = weight * dot_velocity(first, odd)
        pair_order = weight * dot_velocity(first, order_odd)
        for member, sign in ((first, 1), (first + 1, -1)):
            if member not in wanted:
                continue
            done.add(member)
            both = pair_even + pair_odd if sign == 1 else pair_even - pair_odd
            flow_out[member] = keep_flow * flow(member) + both
            both = weight * order_even
            both = both + pair_order if sign == 1 else both - pair_order
            order_out[member] = keep_order * order(member) + both
    return flow_out, order_out


def payload_kernel(flow_ref, order_ref, phase_ref, bound_ref, low_ref, high_ref):
    for x in range(PLANES):
        total = order_ref[0, x]
        for i in range(1, VELS):
            total = total + order_ref[i, x]
        phase_ref[x] = total
    for side, (plane, inward, comps) in enumerate(((PLANES - 1, -1, UP_X), (0, 1, DOWN_X))):
        density, momentum = moments(lambda i: flow_ref[i, plane])
        parts = [flow_ref[i, plane] for i in comps] + [density] + momentum
        parts += [order_ref[i, plane] for i in comps]
        parts += [phase_ref[plane + inward * d] for d in range(3)]
        for index, part in enumerate(parts):
            bound_ref[side, index] = part
    for out_ref, row, inward, comps in ((high_ref, ROWS - 1, -1, UP_Y), (low_ref, 0, 1, DOWN_Y)):
        density, momentum = moments(lambda i: flow_ref[i, :, row, :])
        parts = [flow_ref[i, :, row, :] for i in comps] + [density] + momentum
        parts += [order_ref[i, :, row, :] for i in comps]
        parts += [phase_ref[:, row + inward * d, :] for d in range(3)]
        for index, part in enumerate(parts):
            out_ref[index] = part


def window_kernel(place_ref, before_ref, own_ref, after_ref, even_ref, odd_ref):
    row = lax.broadcasted_iota(jnp.int32, (ROWS, LANES), 0)
    parity = place_ref[0]
    for side, out_ref in ((parity, even_ref), (1 - parity, odd_ref)):
        start = place_ref[1 + side]
        inner = lax.rem(start, ROWS)
        back = lax.rem(ROWS - inner, ROWS)
        early = row < ROWS - inner
        near = start < ROWS
        for index in range(PAYLOAD):
            blocks = [pltpu.roll(ref[side, index], back, 0) for ref in (before_ref, own_ref, after_ref)]
            first = jnp.where(near, blocks[0], blocks[1])
            second = jnp.where(near, blocks[1], blocks[2])
            out_ref[index, 0:ROWS] = jnp.where(early, first, second)
            out_ref[index, ROWS : 2 * ROWS] = jnp.where(early, second, blocks[2])


def ghost_plane(window_ref, comps, own, own_next, weight, kick_speed):
    other = 1.0 - weight

    def sheared(cells):
        return weight * cells + other * roll_rows(cells, 1)

    def seen(cells):
        return other * roll_rows(cells, -1) + weight * cells

    def sides(cells):
        return [roll_rows(cells, 1), roll_rows(cells, -1), roll_lanes(cells, 1), roll_lanes(cells, -1)]

    near, second, third = [window_ref[AT_PHASE + d] for d in range(3)]
    ghost_phase = sheared(near)
    own_potential = potential_of(own, [own_next, ghost_phase] + sides(own))
    near_potential = potential_of(near, [second, seen(own)] + sides(near))
    second_potential = potential_of(second, [third, near] + sides(second))
    beyond = seen(own_potential)
    outward = 1.0 if VELOCITY_X[comps[0]] == 1 else -1.0
    half = -0.5 * near
    force = [
        outward * half * (beyond - second_potential),
        half * (roll_rows(near_potential, -1) - roll_rows(near_potential, 1)),
        half * (roll_lanes(near_potential, -1) - roll_lanes(near_potential, 1)),
    ]
    density = window_ref[AT_MOMENTS]
    momentum = [window_ref[AT_MOMENTS + 1 + d] for d in range(3)]
    flow_out, order_out = collide(
        comps,
        lambda i: window_ref[comps.index(i)],
        lambda i: window_ref[AT_ORDER + comps.index(i)],
        density,
        momentum,
        near,
        near_potential,
        force,
    )
    flow_ghost = []
    for i in comps:
        cells = flow_out[i]
        if VELOCITY_Y[i] != 0:
            cells = cells + (WEIGHT_TABLE[i] * 3.0 * VELOCITY_Y[i] * kick_speed) * density
        flow_ghost.append(sheared(cells))
    order_ghost = [sheared(order_out[i]) for i in comps]
    return ghost_phase, own_potential, sheared(near_potential), flow_ghost, order_ghost


def main_kernel(
    place_ref, flow_ref, order_ref, phase_ref, low_ref, high_ref, even_ref, odd_ref, flow_out, order_out,
    below_ref, above_ref, wide_ref, ghost_ref, potential_ref, low_side, high_side, edge_ref,
):
    is_even = place_ref[0] == 0
    for index in range(PAYLOAD):
        even, odd = even_ref[index], odd_ref[index]
        below_ref[index] = jnp.where(is_even, odd, even)
        above_ref[index] = jnp.where(is_even, even, odd)
    for index, plane in enumerate((0, 1, PLANES - 1, PLANES - 2)):
        wide_ref[index] = jnp.zeros((WINDOW, LANES), jnp.float32)
        for d in range(3):
            wide_ref[index, 3 - d : 4 - d, :] = low_ref[AT_PHASE + d, plane : plane + 1, :]
            wide_ref[index, 12 + d : 13 + d, :] = high_ref[AT_PHASE + d, plane : plane + 1, :]
        wide_ref[index, 4:12, :] = phase_ref[plane]
    below = ghost_plane(below_ref, UP_X, wide_ref[0], wide_ref[1], 1.0 - SHIFT_FRACTION, WALL_SPEED)
    for index in range(5):
        ghost_ref[index] = below[3][index]
        ghost_ref[5 + index] = below[4][index]
    above = ghost_plane(above_ref, DOWN_X, wide_ref[2], wide_ref[3], SHIFT_FRACTION, -WALL_SPEED)
    for index in range(5):
        ghost_ref[10 + index] = above[3][index]
        ghost_ref[15 + index] = above[4][index]

    row = lax.broadcasted_iota(jnp.int32, (ROWS, LANES), 0)
    plane_at = lax.broadcasted_iota(jnp.int32, (PLANES, LANES), 0)

    def ghosts(cells, own_row):
        return cells[own_row + WINDOW_PAD : own_row + WINDOW_PAD + 1, :]

    def across(cells, ghost_low, ghost_high):
        before = jnp.where(plane_at == 0, ghost_low, roll_rows(cells, 1))
        after = jnp.where(plane_at == PLANES - 1, ghost_high, roll_rows(cells, -1))
        return before, after

    for side_ref, out_ref, edge, beside, inward, comps in (
        (low_ref, low_side, 0, -1, 1, UP_Y),
        (high_ref, high_side, ROWS - 1, ROWS, -1, DOWN_Y),
    ):
        own = [phase_ref[:, edge + inward * d, :] for d in range(2)]
        outer = [side_ref[AT_PHASE + d] for d in range(3)]
        lines = [own[1], own[0]] + outer
        potentials = []
        for index in range(1, 4):
            cells = lines[index]
            own_row = edge + inward * (1 - index)
            around = list(across(cells, ghosts(below[0], own_row), ghosts(above[0], own_row)))
            around += [lines[index - 1], lines[index + 1], roll_lanes(cells, 1), roll_lanes(cells, -1)]
            potentials.append(potential_of(cells, around))
        inside, here, outside = potentials
        before, after = across(here, ghosts(below[2], beside), ghosts(above[2], beside))
        half = -0.5 * outer[0]
        force = [
            half * (after - before),
            (inward * half) * (inside - outside),
            half * (roll_lanes(here, -1) - roll_lanes(here, 1)),
        ]
        flow_post, order_post = collide(
            comps,
            lambda i: side_ref[comps.index(i)],
            lambda i: side_ref[AT_ORDER + comps.index(i)],
            side_ref[AT_MOMENTS],
            [side_ref[AT_MOMENTS + 1 + d] for d in range(3)],
            outer[0],
            here,
            force,
        )
        for index, i in enumerate(comps):
            out_ref[index] = flow_post[i]
            out_ref[5 + index] = order_post[i]
        edge_ref[0 if inward == 1 else 1] = here

    def above_row(cells, line):
        return jnp.where(row == 0, line, roll_rows(cells, 1))

    def below_row(cells, line):
        return jnp.where(row == ROWS - 1, line, roll_rows(cells, -1))

    wide_ref[0] = below[1]
    wide_ref[1] = below[2]
    wide_ref[2] = above[1]
    wide_ref[3] = above[2]
    potential_ref[1] = wide_ref[0, 4:12, :]
    potential_ref[0] = wide_ref[1, 4:12, :]
    potential_ref[PLANES] = wide_ref[2, 4:12, :]
    potential_ref[PLANES + 1] = wide_ref[3, 4:12, :]
    for x in range(1, PLANES - 1):
        cells = phase_ref[x]
        around = [
            phase_ref[x - 1],
            phase_ref[x + 1],
            above_row(cells, low_ref[AT_PHASE, x : x + 1, :]),
            below_row(cells, high_ref[AT_PHASE, x : x + 1, :]),
            roll_lanes(cells, 1),
            roll_lanes(cells, -1),
        ]
        potential_ref[x + 1] = potential_of(cells, around)

    def moved(i, cells, index_low, index_high, x):
        if VELOCITY_Y[i] == 1:
            cells = above_row(cells, low_side[index_low + UP_Y.index(i), pl.ds(x, 1), :])
        elif VELOCITY_Y[i] == -1:
            cells = below_row(cells, high_side[index_high + DOWN_Y.index(i), pl.ds(x, 1), :])
        if VELOCITY_Z[i] != 0:
            cells = roll_lanes(cells, VELOCITY_Z[i])
        return cells

    def one_plane(x, skip):
        here = potential_ref[x + 1]
        phase = phase_ref[x]
        half = -0.5 * phase
        force = [
            half * (potential_ref[x + 2] - potential_ref[x]),
            half
            * (
                below_row(here, edge_ref[1, pl.ds(x, 1), :])
                - above_row(here, edge_ref[0, pl.ds(x, 1), :])
            ),
            half * (roll_lanes(here, -1) - roll_lanes(here, 1)),
        ]
        density, momentum = moments(lambda i: flow_ref[i, x])
        flow_post, order_post = collide(
            tuple(i for i in range(VELS) if VELOCITY_X[i] == 0 or VELOCITY_X[i] != skip),
            lambda i: flow_ref[i, x],
            lambda i: order_ref[i, x],
            density,
            momentum,
            phase,
            here,
            force,
        )
        for i in flow_post:
            target = x + VELOCITY_X[i]
            flow_out[i, target] = moved(i, flow_post[i], 0, 0, x)
            order_out[i, target] = moved(i, order_post[i], 5, 5, x)

    one_plane(0, -1)

    def step(x, carry):
        one_plane(x, 0)
        return carry

    lax.fori_loop(1, PLANES - 1, step, 0)
    one_plane(PLANES - 1, 1)

    for comps, first, target in ((UP_X, 0, 0), (DOWN_X, 10, PLANES - 1)):
        for index, i in enumerate(comps):
            start = WINDOW_PAD - VELOCITY_Y[i]
            for out_ref, at in ((flow_out, first + index), (order_out, first + 5 + index)):
                cells = ghost_ref[at, start : start + ROWS, :]
                if VELOCITY_Z[i] != 0:
                    cells = roll_lanes(cells, VELOCITY_Z[i])
                out_ref[i, target] = cells


def vmem(count):
    return [pl.BlockSpec(memory_space=pltpu.VMEM)] * count


def params():
    return pltpu.CompilerParams(vmem_limit_bytes=VMEM_LIMIT)


def f32(*shape):
    return jax.ShapeDtypeStruct(shape, jnp.float32)


def shift_pairs(count, step):
    return [(i, (i + step) % count) for i in range(count)]


def swap_pairs(slabs, strips, first, step):
    pairs = []
    for low in range(first, slabs, 2):
        high = (low + 1) % slabs
        for strip in range(strips):
            other = (strip + step) % strips
            pairs.append((low * strips + strip, high * strips + other))
            pairs.append((high * strips + other, low * strips + strip))
    return pairs


def swap(window, offset, slabs, strips, first):
    def branch(step):
        return lambda cells: lax.ppermute(cells, ("gx", "gy"), swap_pairs(slabs, strips, first, step))

    step = lax.rem((offset + 5) // ROWS, strips)
    return lax.switch(step, [branch(step) for step in range(strips)], window)


def shards(populations, order_pops, plane_offsets):
    slabs, strips = lax.axis_size("gx"), lax.axis_size("gy")
    slab = lax.axis_index("gx")
    parity = slab % 2
    low_offset = plane_offsets[slab]
    high_offset = plane_offsets[(slab + 1) % slabs]
    place = jnp.stack([parity, 9 - (high_offset + 5) % ROWS, (low_offset + 5) % ROWS]).astype(jnp.int32)
    even_offset = jnp.where(parity == 0, high_offset, low_offset)
    odd_offset = jnp.where(parity == 0, low_offset, high_offset)

    phase, bound, to_low, to_high = pl.pallas_call(
        payload_kernel,
        out_shape=(
            f32(PLANES, ROWS, LANES),
            f32(2, PAYLOAD, ROWS, LANES),
            f32(PAYLOAD, PLANES, LANES),
            f32(PAYLOAD, PLANES, LANES),
        ),
        in_specs=vmem(2),
        out_specs=tuple(vmem(4)),
        compiler_params=params(),
        name="payloads",
    )(populations, order_pops)

    up, down = shift_pairs(strips, 1), shift_pairs(strips, -1)
    before = lax.ppermute(bound, "gy", up)
    after = lax.ppermute(bound, "gy", down)
    from_low = lax.ppermute(to_high, "gy", up)
    from_high = lax.ppermute(to_low, "gy", down)

    even, odd = pl.pallas_call(
        window_kernel,
        out_shape=(f32(PAYLOAD, WINDOW, LANES), f32(PAYLOAD, WINDOW, LANES)),
        in_specs=[pl.BlockSpec(memory_space=pltpu.SMEM)] + vmem(3),
        out_specs=tuple(vmem(2)),
        compiler_params=params(),
        name="windows",
    )(place, before, bound, after)

    even = swap(even, even_offset, slabs, strips, 0)
    odd = swap(odd, odd_offset, slabs, strips, 1)

    return pl.pallas_call(
        main_kernel,
        out_shape=(f32(*populations.shape), f32(*order_pops.shape)),
        in_specs=[pl.BlockSpec(memory_space=pltpu.SMEM)] + vmem(7),
        out_specs=tuple(vmem(2)),
        scratch_shapes=[
            pltpu.VMEM((PAYLOAD, WINDOW, LANES), jnp.float32),
            pltpu.VMEM((PAYLOAD, WINDOW, LANES), jnp.float32),
            pltpu.VMEM((4, WINDOW, LANES), jnp.float32),
            pltpu.VMEM((20, WINDOW, LANES), jnp.float32),
            pltpu.VMEM((PLANES + 2, ROWS, LANES), jnp.float32),
            pltpu.VMEM((10, PLANES, LANES), jnp.float32),
            pltpu.VMEM((10, PLANES, LANES), jnp.float32),
            pltpu.VMEM((2, PLANES, LANES), jnp.float32),
        ],
        compiler_params=params(),
        name="collide_stream",
    )(place, populations, order_pops, phase, from_low, from_high, even, odd)


def solution(mesh):
    return jax.shard_map(
        shards,
        mesh=mesh,
        in_specs=(P(None, "gx", "gy", None), P(None, "gx", "gy", None), P()),
        out_specs=(P(None, "gx", "gy", None), P(None, "gx", "gy", None)),
        check_vma=False,
    )
```

```python
import jax
import jax.numpy as jnp
from jax import lax
from jax.experimental import pallas as pl
from jax.experimental.pallas import tpu as pltpu
from jax.sharding import PartitionSpec as P

SHIFT_FRACTION = 0.375
WALL_SPEED = 0.05
RELAX_FLOW = 0.8
RELAX_ORDER = 0.9
BULK_COEFF = 0.05
SURFACE_COEFF = 0.04
MOBILITY = 1.0
VELOCITY_X = (0, 1, -1, 0, 0, 0, 0, 1, -1, 1, -1, 1, -1, 1, -1, 0, 0, 0, 0)
VELOCITY_Y = (0, 0, 0, 1, -1, 0, 0, 1, -1, -1, 1, 0, 0, 0, 0, 1, -1, 1, -1)
VELOCITY_Z = (0, 0, 0, 0, 0, 1, -1, 0, 0, 0, 0, 1, -1, -1, 1, 1, -1, -1, 1)
WEIGHT_TABLE = (1.0 / 3.0,) + (1.0 / 18.0,) * 6 + (1.0 / 36.0,) * 12

VELS = 19
PLANES = 16
ROWS = 8
LANES = 128
UP_X = tuple(i for i in range(VELS) if VELOCITY_X[i] == 1)
DOWN_X = tuple(i for i in range(VELS) if VELOCITY_X[i] == -1)
UP_Y = tuple(i for i in range(VELS) if VELOCITY_Y[i] == 1)
DOWN_Y = tuple(i for i in range(VELS) if VELOCITY_Y[i] == -1)
PAYLOAD = 17
AT_MOMENTS = 5
AT_ORDER = 9
AT_PHASE = 14
WINDOW = 16
WINDOW_PAD = 4

VMEM_LIMIT = 40 * 1024 * 1024
PAYLOAD_VMEM = 61500000


def roll_rows(cells, step):
    return pltpu.roll(cells, step % cells.shape[0], 0)


def roll_lanes(cells, step):
    return pltpu.roll(cells, step % LANES, cells.ndim - 1)


def moments(flow):
    parts = [flow(i) for i in range(VELS)]
    density = parts[0]
    for part in parts[1:]:
        density = density + part
    speeds = []
    for table in (VELOCITY_X, VELOCITY_Y, VELOCITY_Z):
        plus = [parts[i] for i in range(VELS) if table[i] == 1]
        minus = [parts[i] for i in range(VELS) if table[i] == -1]
        total = plus[0] - minus[0]
        for a, b in zip(plus[1:], minus[1:]):
            total = total + (a - b)
        speeds.append(total)
    return density, speeds


def potential_of(phase, neighbours):
    around = neighbours[0]
    for cells in neighbours[1:]:
        around = around + cells
    bulk = BULK_COEFF * (phase * phase * phase - phase)
    return bulk - SURFACE_COEFF * (around - 6.0 * phase)


def dot_velocity(i, vector):
    total = None
    for sign, part in zip((VELOCITY_X[i], VELOCITY_Y[i], VELOCITY_Z[i]), vector):
        if sign == 0:
            continue
        if total is None:
            total = part if sign == 1 else -part
        else:
            total = total + part if sign == 1 else total - part
    return total


def collide(wanted, flow, order, density, momentum, phase, potential, force):
    inverse = 1.0 / density
    speed = [(momentum[d] + 0.5 * force[d]) * inverse for d in range(3)]
    source = 1.0 - 0.5 / RELAX_FLOW
    relaxed = density * (1.0 / RELAX_FLOW)
    speed_sq = speed[0] * speed[0] + speed[1] * speed[1] + speed[2] * speed[2]
    work = speed[0] * force[0] + speed[1] * force[1] + speed[2] * force[2]
    even = relaxed * (1.0 - 1.5 * speed_sq) - (3.0 * source) * work
    odd = [3.0 * (relaxed * speed[d] + source * force[d]) for d in range(3)]
    quad = [4.5 * relaxed * speed[d] + (9.0 * source) * force[d] for d in range(3)]
    order_even = (3.0 * MOBILITY / RELAX_ORDER) * potential
    carried = (3.0 / RELAX_ORDER) * phase
    order_odd = [carried * speed[d] for d in range(3)]
    flow_out, order_out = {}, {}
    keep_flow = 1.0 - 1.0 / RELAX_FLOW
    keep_order = 1.0 - 1.0 / RELAX_ORDER
    done = set()
    for i in wanted:
        if i in done:
            continue
        weight = WEIGHT_TABLE[i]
        if i == 0:
            flow_out[0] = keep_flow * flow(0) + weight * even
            rest = phase - (2.0 * MOBILITY) * potential
            order_out[0] = keep_order * order(0) + (1.0 / RELAX_ORDER) * rest
            continue
        first = i if i % 2 == 1 else i - 1
        pair_even = weight * (even + dot_velocity(first, speed) * dot_velocity(first, quad))
        pair_odd = weight * dot_velocity(first, odd)
        pair_order = weight * dot_velocity(first, order_odd)
        for member, sign in ((first, 1), (first + 1, -1)):
            if member not in wanted:
                continue
            done.add(member)
            both = pair_even + pair_odd if sign == 1 else pair_even - pair_odd
            flow_out[member] = keep_flow * flow(member) + both
            both = weight * order_even
            both = both + pair_order if sign == 1 else both - pair_order
            order_out[member] = keep_order * order(member) + both
    return flow_out, order_out


def plane_copies(source, target, sems, pieces):
    return [
        pltpu.make_async_copy(source.at[:, pl.ds(first, count)], target.at[:, pl.ds(first, count)], sems.at[index])
        for index, (first, count) in enumerate(pieces)
    ]


FLOW_PIECES = ((0, 1), (PLANES - 1, 1), (1, 4), (5, 5), (10, 5))
ORDER_PIECES = ((0, 3), (PLANES - 3, 3), (3, 5), (8, 5))


def payload_kernel(
    flow_hbm, order_hbm, phase_ref, even_ref, odd_ref, low_ref, high_ref, flow_ref, order_ref, flow_sems, order_sems
):
    flow_copies = plane_copies(flow_hbm, flow_ref, flow_sems, FLOW_PIECES)
    order_copies = plane_copies(order_hbm, order_ref, order_sems, ORDER_PIECES)
    for copy in flow_copies[:2] + order_copies[:2] + order_copies[2:] + flow_copies[2:]:
        copy.start()
    is_even = lax.axis_index("gx") % 2 == 0

    def add_phase(x):
        total = order_ref[0, x]
        for i in range(1, VELS):
            total = total + order_ref[i, x]
        phase_ref[x] = total

    for copy in flow_copies[:2] + order_copies[:2]:
        copy.wait()
    for x in (0, 1, 2, PLANES - 3, PLANES - 2, PLANES - 1):
        add_phase(x)
    sides = []
    for plane, inward, comps in ((PLANES - 1, -1, UP_X), (0, 1, DOWN_X)):
        density, momentum = moments(lambda i: flow_ref[i, plane])
        parts = [flow_ref[i, plane] for i in comps] + [density] + momentum
        parts += [order_ref[i, plane] for i in comps]
        parts += [phase_ref[plane + inward * d] for d in range(3)]
        sides.append(parts)
    for index, (last, first) in enumerate(zip(*sides)):
        even_ref[index] = jnp.where(is_even, last, first)
        odd_ref[index] = jnp.where(is_even, first, last)
    for copy in order_copies[2:]:
        copy.wait()
    for x in range(3, PLANES - 3):
        add_phase(x)
    for copy in flow_copies[2:]:
        copy.wait()
    for out_ref, row, inward, comps in ((high_ref, ROWS - 1, -1, UP_Y), (low_ref, 0, 1, DOWN_Y)):
        density, momentum = moments(lambda i: flow_ref[i, :, row, :])
        parts = [flow_ref[i, :, row, :] for i in comps] + [density] + momentum
        parts += [order_ref[i, :, row, :] for i in comps]
        parts += [phase_ref[:, row + inward * d, :] for d in range(3)]
        for index, part in enumerate(parts):
            out_ref[index] = part


def cut_window(blocks, start, window_ref):
    row = lax.broadcasted_iota(jnp.int32, (ROWS, LANES), 0)
    inner = lax.rem(start, ROWS)
    back = lax.rem(ROWS - inner, ROWS)
    early = row < ROWS - inner
    near = start < ROWS
    for index in range(PAYLOAD):
        rolled = [pltpu.roll(block(index), back, 0) for block in blocks]
        first = jnp.where(near, rolled[0], rolled[1])
        second = jnp.where(near, rolled[1], rolled[2])
        window_ref[index, 0:ROWS] = jnp.where(early, first, second)
        window_ref[index, ROWS : 2 * ROWS] = jnp.where(early, second, rolled[2])


def ghost_plane(window_ref, comps, own, own_next, weight, kick_speed):
    other = 1.0 - weight

    def sheared(cells):
        return weight * cells + other * roll_rows(cells, 1)

    def seen(cells):
        return other * roll_rows(cells, -1) + weight * cells

    def sides(cells):
        return [roll_rows(cells, 1), roll_rows(cells, -1), roll_lanes(cells, 1), roll_lanes(cells, -1)]

    near, second, third = [window_ref[AT_PHASE + d] for d in range(3)]
    ghost_phase = sheared(near)
    own_potential = potential_of(own, [own_next, ghost_phase] + sides(own))
    near_potential = potential_of(near, [second, seen(own)] + sides(near))
    second_potential = potential_of(second, [third, near] + sides(second))
    beyond = seen(own_potential)
    outward = 1.0 if VELOCITY_X[comps[0]] == 1 else -1.0
    half = -0.5 * near
    force = [
        outward * half * (beyond - second_potential),
        half * (roll_rows(near_potential, -1) - roll_rows(near_potential, 1)),
        half * (roll_lanes(near_potential, -1) - roll_lanes(near_potential, 1)),
    ]
    density = window_ref[AT_MOMENTS]
    momentum = [window_ref[AT_MOMENTS + 1 + d] for d in range(3)]
    flow_out, order_out = collide(
        comps,
        lambda i: window_ref[comps.index(i)],
        lambda i: window_ref[AT_ORDER + comps.index(i)],
        density,
        momentum,
        near,
        near_potential,
        force,
    )
    flow_ghost = []
    for i in comps:
        cells = flow_out[i]
        if VELOCITY_Y[i] != 0:
            cells = cells + (WEIGHT_TABLE[i] * 3.0 * VELOCITY_Y[i] * kick_speed) * density
        flow_ghost.append(sheared(cells))
    order_ghost = [sheared(order_out[i]) for i in comps]
    return ghost_phase, own_potential, sheared(near_potential), flow_ghost, order_ghost


def main_kernel(
    offset_ref, flow_ref, order_ref, phase_ref, low_ref, high_ref,
    even_minus, even_same, even_plus, odd_minus, odd_same, odd_plus, flow_out, order_out,
    below_ref, above_ref, wide_ref, ghost_ref, potential_ref, low_side, high_side, edge_ref,
):
    slab = lax.axis_index("gx")
    is_even = slab % 2 == 0
    low_offset = offset_ref[slab]
    high_offset = offset_ref[lax.rem(slab + 1, offset_ref.shape[0])]

    def chosen(when_even, when_odd):
        return lambda index: jnp.where(is_even, when_even[index], when_odd[index])

    below_blocks = [chosen(odd_plus, even_plus), chosen(odd_same, even_same), chosen(odd_minus, even_minus)]
    above_blocks = [chosen(even_minus, odd_minus), chosen(even_same, odd_same), chosen(even_plus, odd_plus)]
    cut_window(below_blocks, 9 - lax.rem(low_offset + 5, ROWS), below_ref)
    cut_window(above_blocks, lax.rem(high_offset + 5, ROWS), above_ref)
    for index, plane in enumerate((0, 1, PLANES - 1, PLANES - 2)):
        wide_ref[index] = jnp.zeros((WINDOW, LANES), jnp.float32)
        for d in range(3):
            wide_ref[index, 3 - d : 4 - d, :] = low_ref[AT_PHASE + d, plane : plane + 1, :]
            wide_ref[index, 12 + d : 13 + d, :] = high_ref[AT_PHASE + d, plane : plane + 1, :]
        wide_ref[index, 4:12, :] = phase_ref[plane]
    below = ghost_plane(below_ref, UP_X, wide_ref[0], wide_ref[1], 1.0 - SHIFT_FRACTION, WALL_SPEED)
    for index in range(5):
        ghost_ref[index] = below[3][index]
        ghost_ref[5 + index] = below[4][index]
    above = ghost_plane(above_ref, DOWN_X, wide_ref[2], wide_ref[3], SHIFT_FRACTION, -WALL_SPEED)
    for index in range(5):
        ghost_ref[10 + index] = above[3][index]
        ghost_ref[15 + index] = above[4][index]

    row = lax.broadcasted_iota(jnp.int32, (ROWS, LANES), 0)
    plane_at = lax.broadcasted_iota(jnp.int32, (PLANES, LANES), 0)

    def ghosts(cells, own_row):
        return cells[own_row + WINDOW_PAD : own_row + WINDOW_PAD + 1, :]

    def across(cells, ghost_low, ghost_high):
        before = jnp.where(plane_at == 0, ghost_low, roll_rows(cells, 1))
        after = jnp.where(plane_at == PLANES - 1, ghost_high, roll_rows(cells, -1))
        return before, after

    for side_ref, out_ref, edge, beside, inward, comps in (
        (low_ref, low_side, 0, -1, 1, UP_Y),
        (high_ref, high_side, ROWS - 1, ROWS, -1, DOWN_Y),
    ):
        own = [phase_ref[:, edge + inward * d, :] for d in range(2)]
        outer = [side_ref[AT_PHASE + d] for d in range(3)]
        lines = [own[1], own[0]] + outer
        potentials = []
        for index in range(1, 4):
            cells = lines[index]
            own_row = edge + inward * (1 - index)
            around = list(across(cells, ghosts(below[0], own_row), ghosts(above[0], own_row)))
            around += [lines[index - 1], lines[index + 1], roll_lanes(cells, 1), roll_lanes(cells, -1)]
            potentials.append(potential_of(cells, around))
        inside, here, outside = potentials
        before, after = across(here, ghosts(below[2], beside), ghosts(above[2], beside))
        half = -0.5 * outer[0]
        force = [
            half * (after - before),
            (inward * half) * (inside - outside),
            half * (roll_lanes(here, -1) - roll_lanes(here, 1)),
        ]
        flow_post, order_post = collide(
            comps,
            lambda i: side_ref[comps.index(i)],
            lambda i: side_ref[AT_ORDER + comps.index(i)],
            side_ref[AT_MOMENTS],
            [side_ref[AT_MOMENTS + 1 + d] for d in range(3)],
            outer[0],
            here,
            force,
        )
        for index, i in enumerate(comps):
            out_ref[index] = flow_post[i]
            out_ref[5 + index] = order_post[i]
        edge_ref[0 if inward == 1 else 1] = here

    def above_row(cells, line):
        return jnp.where(row == 0, line, roll_rows(cells, 1))

    def below_row(cells, line):
        return jnp.where(row == ROWS - 1, line, roll_rows(cells, -1))

    wide_ref[0] = below[1]
    wide_ref[1] = below[2]
    wide_ref[2] = above[1]
    wide_ref[3] = above[2]
    potential_ref[1] = wide_ref[0, 4:12, :]
    potential_ref[0] = wide_ref[1, 4:12, :]
    potential_ref[PLANES] = wide_ref[2, 4:12, :]
    potential_ref[PLANES + 1] = wide_ref[3, 4:12, :]
    for x in range(1, PLANES - 1):
        cells = phase_ref[x]
        around = [
            phase_ref[x - 1],
            phase_ref[x + 1],
            above_row(cells, low_ref[AT_PHASE, x : x + 1, :]),
            below_row(cells, high_ref[AT_PHASE, x : x + 1, :]),
            roll_lanes(cells, 1),
            roll_lanes(cells, -1),
        ]
        potential_ref[x + 1] = potential_of(cells, around)

    def moved(i, cells, index_low, index_high, x):
        if VELOCITY_Y[i] == 1:
            cells = above_row(cells, low_side[index_low + UP_Y.index(i), pl.ds(x, 1), :])
        elif VELOCITY_Y[i] == -1:
            cells = below_row(cells, high_side[index_high + DOWN_Y.index(i), pl.ds(x, 1), :])
        if VELOCITY_Z[i] != 0:
            cells = roll_lanes(cells, VELOCITY_Z[i])
        return cells

    def one_plane(x, skip):
        here = potential_ref[x + 1]
        phase = phase_ref[x]
        half = -0.5 * phase
        force = [
            half * (potential_ref[x + 2] - potential_ref[x]),
            half
            * (
                below_row(here, edge_ref[1, pl.ds(x, 1), :])
                - above_row(here, edge_ref[0, pl.ds(x, 1), :])
            ),
            half * (roll_lanes(here, -1) - roll_lanes(here, 1)),
        ]
        density, momentum = moments(lambda i: flow_ref[i, x])
        flow_post, order_post = collide(
            tuple(i for i in range(VELS) if VELOCITY_X[i] == 0 or VELOCITY_X[i] != skip),
            lambda i: flow_ref[i, x],
            lambda i: order_ref[i, x],
            density,
            momentum,
            phase,
            here,
            force,
        )
        for i in flow_post:
            target = x + VELOCITY_X[i]
            flow_out[i, target] = moved(i, flow_post[i], 0, 0, x)
            order_out[i, target] = moved(i, order_post[i], 5, 5, x)

    one_plane(0, -1)

    def step(x, carry):
        one_plane(x, 0)
        return carry

    lax.fori_loop(1, PLANES - 1, step, 0)
    one_plane(PLANES - 1, 1)

    for comps, first, target in ((UP_X, 0, 0), (DOWN_X, 10, PLANES - 1)):
        for index, i in enumerate(comps):
            start = WINDOW_PAD - VELOCITY_Y[i]
            for out_ref, at in ((flow_out, first + index), (order_out, first + 5 + index)):
                cells = ghost_ref[at, start : start + ROWS, :]
                if VELOCITY_Z[i] != 0:
                    cells = roll_lanes(cells, VELOCITY_Z[i])
                out_ref[i, target] = cells


def vmem(count):
    return [pl.BlockSpec(memory_space=pltpu.VMEM)] * count


def params(limit=VMEM_LIMIT):
    return pltpu.CompilerParams(vmem_limit_bytes=limit)


def f32(*shape):
    return jax.ShapeDtypeStruct(shape, jnp.float32)


def shift_pairs(count, step):
    return [(i, (i + step) % count) for i in range(count)]


def swap_pairs(slabs, strips, first, step):
    pairs = []
    for low in range(first, slabs, 2):
        high = (low + 1) % slabs
        for strip in range(strips):
            other = (strip + step) % strips
            pairs.append((low * strips + strip, high * strips + other))
            pairs.append((high * strips + other, low * strips + strip))
    return pairs


def swap(payload, offset, slabs, strips, first):
    def branch(step):
        return lambda cells: tuple(
            lax.ppermute(cells, ("gx", "gy"), swap_pairs(slabs, strips, first, step + d)) for d in (-1, 0, 1)
        )

    step = lax.rem((offset + jnp.uint32(5)) // jnp.uint32(ROWS), jnp.uint32(strips)).astype(jnp.int32)
    return lax.switch(step, [branch(step) for step in range(strips)], payload)


def shards(populations, order_pops, plane_offsets):
    slabs, strips = lax.axis_size("gx"), lax.axis_size("gy")
    slab = lax.axis_index("gx").astype(jnp.uint32)
    even_boundary = slab | jnp.uint32(1)
    odd_boundary = lax.rem(slab + (slab & jnp.uint32(1)), jnp.uint32(slabs))
    even_offset = lax.dynamic_index_in_dim(plane_offsets, even_boundary, keepdims=False)
    odd_offset = lax.dynamic_index_in_dim(plane_offsets, odd_boundary, keepdims=False)

    phase, even, odd, to_low, to_high = pl.pallas_call(
        payload_kernel,
        out_shape=(
            f32(PLANES, ROWS, LANES),
            f32(PAYLOAD, ROWS, LANES),
            f32(PAYLOAD, ROWS, LANES),
            f32(PAYLOAD, PLANES, LANES),
            f32(PAYLOAD, PLANES, LANES),
        ),
        in_specs=[pl.BlockSpec(memory_space=pltpu.HBM)] * 2,
        out_specs=tuple(vmem(5)),
        scratch_shapes=[
            pltpu.VMEM(populations.shape, jnp.float32),
            pltpu.VMEM(order_pops.shape, jnp.float32),
            pltpu.SemaphoreType.DMA((len(FLOW_PIECES),)),
            pltpu.SemaphoreType.DMA((len(ORDER_PIECES),)),
        ],
        compiler_params=params(PAYLOAD_VMEM),
        name="payloads",
    )(populations, order_pops)

    from_low = lax.ppermute(to_high, "gy", shift_pairs(strips, 1))
    from_high = lax.ppermute(to_low, "gy", shift_pairs(strips, -1))
    even = swap(even, even_offset.astype(jnp.uint32), slabs, strips, 0)
    odd = swap(odd, odd_offset.astype(jnp.uint32), slabs, strips, 1)

    return pl.pallas_call(
        main_kernel,
        out_shape=(f32(*populations.shape), f32(*order_pops.shape)),
        in_specs=[pl.BlockSpec(memory_space=pltpu.SMEM)] + vmem(11),
        out_specs=tuple(vmem(2)),
        scratch_shapes=[
            pltpu.VMEM((PAYLOAD, WINDOW, LANES), jnp.float32),
            pltpu.VMEM((PAYLOAD, WINDOW, LANES), jnp.float32),
            pltpu.VMEM((4, WINDOW, LANES), jnp.float32),
            pltpu.VMEM((20, WINDOW, LANES), jnp.float32),
            pltpu.VMEM((PLANES + 2, ROWS, LANES), jnp.float32),
            pltpu.VMEM((10, PLANES, LANES), jnp.float32),
            pltpu.VMEM((10, PLANES, LANES), jnp.float32),
            pltpu.VMEM((2, PLANES, LANES), jnp.float32),
        ],
        compiler_params=params(),
        name="collide_stream",
    )(plane_offsets, populations, order_pops, phase, from_low, from_high, *even, *odd)


def solution(mesh):
    return jax.shard_map(
        shards,
        mesh=mesh,
        in_specs=(P(None, "gx", "gy", None), P(None, "gx", "gy", None), P()),
        out_specs=(P(None, "gx", "gy", None), P(None, "gx", "gy", None)),
        check_vma=False,
    )
```

```python
import jax
import jax.numpy as jnp
from jax import lax
from jax.experimental import pallas as pl
from jax.experimental.pallas import tpu as pltpu
from jax.sharding import PartitionSpec as P

SHIFT_FRACTION = 0.375
WALL_SPEED = 0.05
RELAX_FLOW = 0.8
RELAX_ORDER = 0.9
BULK_COEFF = 0.05
SURFACE_COEFF = 0.04
MOBILITY = 1.0
VELOCITY_X = (0, 1, -1, 0, 0, 0, 0, 1, -1, 1, -1, 1, -1, 1, -1, 0, 0, 0, 0)
VELOCITY_Y = (0, 0, 0, 1, -1, 0, 0, 1, -1, -1, 1, 0, 0, 0, 0, 1, -1, 1, -1)
VELOCITY_Z = (0, 0, 0, 0, 0, 1, -1, 0, 0, 0, 0, 1, -1, -1, 1, 1, -1, -1, 1)
WEIGHT_TABLE = (1.0 / 3.0,) + (1.0 / 18.0,) * 6 + (1.0 / 36.0,) * 12

VELS = 19
PLANES = 16
ROWS = 8
LANES = 128
UP_X = tuple(i for i in range(VELS) if VELOCITY_X[i] == 1)
DOWN_X = tuple(i for i in range(VELS) if VELOCITY_X[i] == -1)
UP_Y = tuple(i for i in range(VELS) if VELOCITY_Y[i] == 1)
DOWN_Y = tuple(i for i in range(VELS) if VELOCITY_Y[i] == -1)
PAYLOAD = 17
AT_MOMENTS = 5
AT_ORDER = 9
AT_PHASE = 14
WINDOW = 16
WINDOW_PAD = 4

VMEM_LIMIT = 61500000


def roll_rows(cells, step):
    return pltpu.roll(cells, step % cells.shape[0], 0)


def roll_lanes(cells, step):
    return pltpu.roll(cells, step % LANES, cells.ndim - 1)


def moments(flow):
    parts = [flow(i) for i in range(VELS)]
    density = parts[0]
    for part in parts[1:]:
        density = density + part
    speeds = []
    for table in (VELOCITY_X, VELOCITY_Y, VELOCITY_Z):
        plus = [parts[i] for i in range(VELS) if table[i] == 1]
        minus = [parts[i] for i in range(VELS) if table[i] == -1]
        total = plus[0] - minus[0]
        for a, b in zip(plus[1:], minus[1:]):
            total = total + (a - b)
        speeds.append(total)
    return density, speeds


def potential_of(phase, neighbours):
    around = neighbours[0]
    for cells in neighbours[1:]:
        around = around + cells
    bulk = BULK_COEFF * (phase * phase * phase - phase)
    return bulk - SURFACE_COEFF * (around - 6.0 * phase)


def dot_velocity(i, vector):
    total = None
    for sign, part in zip((VELOCITY_X[i], VELOCITY_Y[i], VELOCITY_Z[i]), vector):
        if sign == 0:
            continue
        if total is None:
            total = part if sign == 1 else -part
        else:
            total = total + part if sign == 1 else total - part
    return total


def collide(wanted, flow, order, density, momentum, phase, potential, force):
    inverse = 1.0 / density
    speed = [(momentum[d] + 0.5 * force[d]) * inverse for d in range(3)]
    source = 1.0 - 0.5 / RELAX_FLOW
    relaxed = density * (1.0 / RELAX_FLOW)
    speed_sq = speed[0] * speed[0] + speed[1] * speed[1] + speed[2] * speed[2]
    work = speed[0] * force[0] + speed[1] * force[1] + speed[2] * force[2]
    even = relaxed * (1.0 - 1.5 * speed_sq) - (3.0 * source) * work
    odd = [3.0 * (relaxed * speed[d] + source * force[d]) for d in range(3)]
    quad = [4.5 * relaxed * speed[d] + (9.0 * source) * force[d] for d in range(3)]
    order_even = (3.0 * MOBILITY / RELAX_ORDER) * potential
    carried = (3.0 / RELAX_ORDER) * phase
    order_odd = [carried * speed[d] for d in range(3)]
    flow_out, order_out = {}, {}
    keep_flow = 1.0 - 1.0 / RELAX_FLOW
    keep_order = 1.0 - 1.0 / RELAX_ORDER
    done = set()
    for i in wanted:
        if i in done:
            continue
        weight = WEIGHT_TABLE[i]
        if i == 0:
            flow_out[0] = keep_flow * flow(0) + weight * even
            rest = phase - (2.0 * MOBILITY) * potential
            order_out[0] = keep_order * order(0) + (1.0 / RELAX_ORDER) * rest
            continue
        first = i if i % 2 == 1 else i - 1
        pair_even = weight * (even + dot_velocity(first, speed) * dot_velocity(first, quad))
        pair_odd = weight * dot_velocity(first, odd)
        pair_order = weight * dot_velocity(first, order_odd)
        for member, sign in ((first, 1), (first + 1, -1)):
            if member not in wanted:
                continue
            done.add(member)
            both = pair_even + pair_odd if sign == 1 else pair_even - pair_odd
            flow_out[member] = keep_flow * flow(member) + both
            both = weight * order_even
            both = both + pair_order if sign == 1 else both - pair_order
            order_out[member] = keep_order * order(member) + both
    return flow_out, order_out


def add_phase(phase_ref, order_ref, x):
    total = order_ref[0, x]
    for i in range(1, VELS):
        total = total + order_ref[i, x]
    phase_ref[x] = total


def plane_copies(source, target, sems, pieces):
    return [
        pltpu.make_async_copy(source.at[:, pl.ds(first, count)], target.at[:, pl.ds(first, count)], sems.at[index])
        for index, (first, count) in enumerate(pieces)
    ]


FLOW_PIECES = ((0, 1), (PLANES - 1, 1), (1, 4), (5, 5), (10, 5))
ORDER_PIECES = ((0, 3), (PLANES - 3, 3), (3, 5), (8, 5))
QUARTERS = ((0, 4), (4, 4), (8, 4), (12, 4))
PACKED = PAYLOAD * (ROWS + PLANES)


def side_rows(index):
    return pl.ds(PAYLOAD * ROWS + index * PLANES, PLANES)


def payload_kernel(
    flow_hbm, order_hbm, even_ref, low_ref, high_ref, flow_ref, order_ref, phase_ref, flow_sems, order_sems
):
    flow_copies = plane_copies(flow_hbm, flow_ref, flow_sems, FLOW_PIECES)
    order_copies = plane_copies(order_hbm, order_ref, order_sems, ORDER_PIECES)
    for copy in flow_copies[:2] + order_copies[:2] + order_copies[2:] + flow_copies[2:]:
        copy.start()
    is_even = lax.axis_index("gx") % 2 == 0

    for copy in flow_copies[:2] + order_copies[:2]:
        copy.wait()
    for x in (0, 1, 2, PLANES - 3, PLANES - 2, PLANES - 1):
        add_phase(phase_ref, order_ref, x)
    sides = []
    for plane, inward, comps in ((PLANES - 1, -1, UP_X), (0, 1, DOWN_X)):
        density, momentum = moments(lambda i: flow_ref[i, plane])
        parts = [flow_ref[i, plane] for i in comps] + [density] + momentum
        parts += [order_ref[i, plane] for i in comps]
        parts += [phase_ref[plane + inward * d] for d in range(3)]
        sides.append(parts)
    for index, (last, first) in enumerate(zip(*sides)):
        even_ref[index] = jnp.where(is_even, last, first)
        odd = jnp.where(is_even, first, last)
        low_ref[index * ROWS : (index + 1) * ROWS, :] = odd
        high_ref[index * ROWS : (index + 1) * ROWS, :] = odd
    for copy in order_copies[2:]:
        copy.wait()
    for x in range(3, PLANES - 3):
        add_phase(phase_ref, order_ref, x)
    for copy in flow_copies[2:]:
        copy.wait()
    for out_ref, row, inward, comps in ((high_ref, ROWS - 1, -1, UP_Y), (low_ref, 0, 1, DOWN_Y)):
        density, momentum = moments(lambda i: flow_ref[i, :, row, :])
        parts = [flow_ref[i, :, row, :] for i in comps] + [density] + momentum
        parts += [order_ref[i, :, row, :] for i in comps]
        parts += [phase_ref[:, row + inward * d, :] for d in range(3)]
        for index, part in enumerate(parts):
            out_ref[side_rows(index), :] = part


def window_kernel(offset_ref, before_ref, own_ref, after_ref, out_ref):
    slab = lax.axis_index("gx")
    is_even = slab % 2 == 0
    offset = offset_ref[lax.rem(slab + slab % 2, offset_ref.shape[0])]
    inner = lax.rem(offset + 5, ROWS)

    def block(ref):
        return lambda index: ref[index * ROWS : (index + 1) * ROWS, :]

    cut_window([block(before_ref), block(own_ref), block(after_ref)], jnp.where(is_even, inner, 9 - inner), out_ref)


def cut_window(blocks, start, window_ref):
    row = lax.broadcasted_iota(jnp.int32, (ROWS, LANES), 0)
    inner = lax.rem(start, ROWS)
    back = lax.rem(ROWS - inner, ROWS)
    early = row < ROWS - inner
    near = start < ROWS
    for index in range(PAYLOAD):
        rolled = [pltpu.roll(block(index), back, 0) for block in blocks]
        first = jnp.where(near, rolled[0], rolled[1])
        second = jnp.where(near, rolled[1], rolled[2])
        window_ref[index, 0:ROWS] = jnp.where(early, first, second)
        window_ref[index, ROWS : 2 * ROWS] = jnp.where(early, second, rolled[2])


def ghost_plane(window_ref, comps, own, own_next, weight, kick_speed):
    other = 1.0 - weight

    def sheared(cells):
        return weight * cells + other * roll_rows(cells, 1)

    def seen(cells):
        return other * roll_rows(cells, -1) + weight * cells

    def sides(cells):
        return [roll_rows(cells, 1), roll_rows(cells, -1), roll_lanes(cells, 1), roll_lanes(cells, -1)]

    near, second, third = [window_ref[AT_PHASE + d] for d in range(3)]
    ghost_phase = sheared(near)
    own_potential = potential_of(own, [own_next, ghost_phase] + sides(own))
    near_potential = potential_of(near, [second, seen(own)] + sides(near))
    second_potential = potential_of(second, [third, near] + sides(second))
    beyond = seen(own_potential)
    outward = 1.0 if VELOCITY_X[comps[0]] == 1 else -1.0
    half = -0.5 * near
    force = [
        outward * half * (beyond - second_potential),
        half * (roll_rows(near_potential, -1) - roll_rows(near_potential, 1)),
        half * (roll_lanes(near_potential, -1) - roll_lanes(near_potential, 1)),
    ]
    density = window_ref[AT_MOMENTS]
    momentum = [window_ref[AT_MOMENTS + 1 + d] for d in range(3)]
    flow_out, order_out = collide(
        comps,
        lambda i: window_ref[comps.index(i)],
        lambda i: window_ref[AT_ORDER + comps.index(i)],
        density,
        momentum,
        near,
        near_potential,
        force,
    )
    flow_ghost = []
    for i in comps:
        cells = flow_out[i]
        if VELOCITY_Y[i] != 0:
            cells = cells + (WEIGHT_TABLE[i] * 3.0 * VELOCITY_Y[i] * kick_speed) * density
        flow_ghost.append(sheared(cells))
    order_ghost = [sheared(order_out[i]) for i in comps]
    return ghost_phase, own_potential, sheared(near_potential), flow_ghost, order_ghost


def main_kernel(
    offset_ref, flow_hbm, order_hbm, low_hbm, high_hbm, minus_hbm, same_hbm, plus_hbm, odd_hbm, flow_hbm_out, order_hbm_out,
    flow_ref, order_ref, low_ref, high_ref, even_ref, odd_ref, flow_out, order_out, phase_ref,
    below_ref, above_ref, wide_ref, ghost_ref, potential_ref, low_side, high_side, edge_ref,
    flow_sems, order_sems, extra_sems, flow_out_sems, order_out_sems,
):
    flow_copies = plane_copies(flow_hbm, flow_ref, flow_sems, QUARTERS)
    order_copies = plane_copies(order_hbm, order_ref, order_sems, QUARTERS)
    rest = pl.ds(PAYLOAD * ROWS, PAYLOAD * PLANES)
    pairs = [(minus_hbm, even_ref.at[0]), (same_hbm, even_ref.at[1]), (plus_hbm, even_ref.at[2]), (odd_hbm, odd_ref)]
    pairs += [(low_hbm.at[rest], low_ref), (high_hbm.at[rest], high_ref)]
    extra_copies = [pltpu.make_async_copy(a, b, extra_sems.at[index]) for index, (a, b) in enumerate(pairs)]
    for copy in order_copies + extra_copies + flow_copies:
        copy.start()

    slab = lax.axis_index("gx")
    is_even = slab % 2 == 0
    even_offset = offset_ref[slab + 1 - slab % 2]
    even_inner = lax.rem(even_offset + 5, ROWS)

    def arrived(index):
        return lambda at: even_ref[jnp.where(is_even, index, 2 - index), at]

    for copy in order_copies:
        copy.wait()
    for x in range(PLANES):
        add_phase(phase_ref, order_ref, x)
    for copy in extra_copies:
        copy.wait()
    cut_window([arrived(0), arrived(1), arrived(2)], jnp.where(is_even, even_inner, 9 - even_inner), above_ref)
    for index in range(PAYLOAD):
        even, odd = above_ref[index], odd_ref[index]
        below_ref[index] = jnp.where(is_even, odd, even)
        above_ref[index] = jnp.where(is_even, even, odd)

    def side_line(ref, index):
        return ref[index * PLANES : (index + 1) * PLANES, :]

    def side_at(ref, index, x):
        return ref[index * PLANES + x : index * PLANES + x + 1, :]

    for index, plane in enumerate((0, 1, PLANES - 1, PLANES - 2)):
        wide_ref[index] = jnp.zeros((WINDOW, LANES), jnp.float32)
        for d in range(3):
            wide_ref[index, 3 - d : 4 - d, :] = side_at(low_ref, AT_PHASE + d, plane)
            wide_ref[index, 12 + d : 13 + d, :] = side_at(high_ref, AT_PHASE + d, plane)
        wide_ref[index, 4:12, :] = phase_ref[plane]
    below = ghost_plane(below_ref, UP_X, wide_ref[0], wide_ref[1], 1.0 - SHIFT_FRACTION, WALL_SPEED)
    for index in range(5):
        ghost_ref[index] = below[3][index]
        ghost_ref[5 + index] = below[4][index]
    above = ghost_plane(above_ref, DOWN_X, wide_ref[2], wide_ref[3], SHIFT_FRACTION, -WALL_SPEED)
    for index in range(5):
        ghost_ref[10 + index] = above[3][index]
        ghost_ref[15 + index] = above[4][index]

    row = lax.broadcasted_iota(jnp.int32, (ROWS, LANES), 0)
    plane_at = lax.broadcasted_iota(jnp.int32, (PLANES, LANES), 0)

    def ghosts(cells, own_row):
        return cells[own_row + WINDOW_PAD : own_row + WINDOW_PAD + 1, :]

    def across(cells, ghost_low, ghost_high):
        before = jnp.where(plane_at == 0, ghost_low, roll_rows(cells, 1))
        after = jnp.where(plane_at == PLANES - 1, ghost_high, roll_rows(cells, -1))
        return before, after

    for side_ref, out_ref, edge, beside, inward, comps in (
        (low_ref, low_side, 0, -1, 1, UP_Y),
        (high_ref, high_side, ROWS - 1, ROWS, -1, DOWN_Y),
    ):
        own = [phase_ref[:, edge + inward * d, :] for d in range(2)]
        outer = [side_line(side_ref, AT_PHASE + d) for d in range(3)]
        lines = [own[1], own[0]] + outer
        potentials = []
        for index in range(1, 4):
            cells = lines[index]
            own_row = edge + inward * (1 - index)
            around = list(across(cells, ghosts(below[0], own_row), ghosts(above[0], own_row)))
            around += [lines[index - 1], lines[index + 1], roll_lanes(cells, 1), roll_lanes(cells, -1)]
            potentials.append(potential_of(cells, around))
        inside, here, outside = potentials
        before, after = across(here, ghosts(below[2], beside), ghosts(above[2], beside))
        half = -0.5 * outer[0]
        force = [
            half * (after - before),
            (inward * half) * (inside - outside),
            half * (roll_lanes(here, -1) - roll_lanes(here, 1)),
        ]
        flow_post, order_post = collide(
            comps,
            lambda i: side_line(side_ref, comps.index(i)),
            lambda i: side_line(side_ref, AT_ORDER + comps.index(i)),
            side_line(side_ref, AT_MOMENTS),
            [side_line(side_ref, AT_MOMENTS + 1 + d) for d in range(3)],
            outer[0],
            here,
            force,
        )
        for index, i in enumerate(comps):
            out_ref[index] = flow_post[i]
            out_ref[5 + index] = order_post[i]
        edge_ref[0 if inward == 1 else 1] = here

    def above_row(cells, line):
        return jnp.where(row == 0, line, roll_rows(cells, 1))

    def below_row(cells, line):
        return jnp.where(row == ROWS - 1, line, roll_rows(cells, -1))

    wide_ref[0] = below[1]
    wide_ref[1] = below[2]
    wide_ref[2] = above[1]
    wide_ref[3] = above[2]
    potential_ref[1] = wide_ref[0, 4:12, :]
    potential_ref[0] = wide_ref[1, 4:12, :]
    potential_ref[PLANES] = wide_ref[2, 4:12, :]
    potential_ref[PLANES + 1] = wide_ref[3, 4:12, :]
    for x in range(1, PLANES - 1):
        cells = phase_ref[x]
        around = [
            phase_ref[x - 1],
            phase_ref[x + 1],
            above_row(cells, side_at(low_ref, AT_PHASE, x)),
            below_row(cells, side_at(high_ref, AT_PHASE, x)),
            roll_lanes(cells, 1),
            roll_lanes(cells, -1),
        ]
        potential_ref[x + 1] = potential_of(cells, around)

    def moved(i, cells, index_low, index_high, x):
        if VELOCITY_Y[i] == 1:
            cells = above_row(cells, low_side[index_low + UP_Y.index(i), pl.ds(x, 1), :])
        elif VELOCITY_Y[i] == -1:
            cells = below_row(cells, high_side[index_high + DOWN_Y.index(i), pl.ds(x, 1), :])
        if VELOCITY_Z[i] != 0:
            cells = roll_lanes(cells, VELOCITY_Z[i])
        return cells

    def one_plane(x, skip):
        here = potential_ref[x + 1]
        phase = phase_ref[x]
        half = -0.5 * phase
        force = [
            half * (potential_ref[x + 2] - potential_ref[x]),
            half
            * (
                below_row(here, edge_ref[1, pl.ds(x, 1), :])
                - above_row(here, edge_ref[0, pl.ds(x, 1), :])
            ),
            half * (roll_lanes(here, -1) - roll_lanes(here, 1)),
        ]
        density, momentum = moments(lambda i: flow_ref[i, x])
        flow_post, order_post = collide(
            tuple(i for i in range(VELS) if VELOCITY_X[i] == 0 or VELOCITY_X[i] != skip),
            lambda i: flow_ref[i, x],
            lambda i: order_ref[i, x],
            density,
            momentum,
            phase,
            here,
            force,
        )
        for i in flow_post:
            target = x + VELOCITY_X[i]
            flow_out[i, target] = moved(i, flow_post[i], 0, 0, x)
            order_out[i, target] = moved(i, order_post[i], 5, 5, x)

    def step(x, carry):
        one_plane(x, 0)
        return carry

    for comps, first, target in ((UP_X, 0, 0), (DOWN_X, 10, PLANES - 1)):
        for index, i in enumerate(comps):
            start = WINDOW_PAD - VELOCITY_Y[i]
            for out_ref, at in ((flow_out, first + index), (order_out, first + 5 + index)):
                cells = ghost_ref[at, start : start + ROWS, :]
                if VELOCITY_Z[i] != 0:
                    cells = roll_lanes(cells, VELOCITY_Z[i])
                out_ref[i, target] = cells

    flow_writes = plane_copies(flow_out, flow_hbm_out, flow_out_sems, QUARTERS)
    order_writes = plane_copies(order_out, order_hbm_out, order_out_sems, QUARTERS)
    for quarter, (first, count) in enumerate(QUARTERS):
        flow_copies[quarter].wait()
        last = first + count
        if quarter == 0:
            one_plane(0, -1)
            first = 1
        if last == PLANES:
            last = PLANES - 1
        lax.fori_loop(first, last, step, 0)
        if last == PLANES - 1:
            one_plane(PLANES - 1, 1)
        if quarter > 0:
            flow_writes[quarter - 1].start()
            order_writes[quarter - 1].start()
    flow_writes[-1].start()
    order_writes[-1].start()
    for copy in flow_writes + order_writes:
        copy.wait()


def vmem(count):
    return [pl.BlockSpec(memory_space=pltpu.VMEM)] * count


def params(limit=VMEM_LIMIT):
    return pltpu.CompilerParams(vmem_limit_bytes=limit)


def f32(*shape):
    return jax.ShapeDtypeStruct(shape, jnp.float32)


def shift_pairs(count, step):
    return [(i, (i + step) % count) for i in range(count)]


def swap_pairs(slabs, strips, first, step):
    pairs = []
    for low in range(first, slabs, 2):
        high = (low + 1) % slabs
        for strip in range(strips):
            other = (strip + step) % strips
            pairs.append((low * strips + strip, high * strips + other))
            pairs.append((high * strips + other, low * strips + strip))
    return pairs


def boundary_switch(payload, offset, slabs, strips, first, nearby):
    def branch(step):
        return lambda cells: tuple(
            lax.ppermute(cells, ("gx", "gy"), swap_pairs(slabs, strips, first, step + d)) for d in nearby
        )

    step = lax.rem((offset + jnp.uint32(5)) // jnp.uint32(ROWS), jnp.uint32(strips)).astype(jnp.int32)
    return lax.switch(step, [branch(step) for step in range(strips)], payload)


def hbm(count):
    return [pl.BlockSpec(memory_space=pltpu.HBM)] * count


def smem():
    return [pl.BlockSpec(memory_space=pltpu.SMEM)]


def scratch(*shape):
    return pltpu.VMEM(shape, jnp.float32)


def shards(populations, order_pops, plane_offsets):
    slabs, strips = lax.axis_size("gx"), lax.axis_size("gy")
    slab = lax.axis_index("gx").astype(jnp.uint32)
    even_boundary = slab | jnp.uint32(1)
    odd_boundary = lax.rem(slab + (slab & jnp.uint32(1)), jnp.uint32(slabs))
    offsets = plane_offsets.astype(jnp.uint32)
    even_offset = lax.dynamic_index_in_dim(offsets, even_boundary, keepdims=False)
    odd_offset = lax.dynamic_index_in_dim(offsets, odd_boundary, keepdims=False)

    even, to_low, to_high = pl.pallas_call(
        payload_kernel,
        out_shape=(f32(PAYLOAD, ROWS, LANES), f32(PACKED, LANES), f32(PACKED, LANES)),
        in_specs=hbm(2),
        out_specs=tuple(vmem(3)),
        scratch_shapes=[
            scratch(*populations.shape),
            scratch(*order_pops.shape),
            scratch(PLANES, ROWS, LANES),
            pltpu.SemaphoreType.DMA((len(FLOW_PIECES),)),
            pltpu.SemaphoreType.DMA((len(ORDER_PIECES),)),
        ],
        compiler_params=params(),
        name="payloads",
    )(populations, order_pops)

    from_low = lax.ppermute(to_high, "gy", shift_pairs(strips, 1))
    from_high = lax.ppermute(to_low, "gy", shift_pairs(strips, -1))
    minus, same, plus = boundary_switch(even, even_offset, slabs, strips, 0, (-1, 0, 1))
    window = pl.pallas_call(
        window_kernel,
        out_shape=f32(PAYLOAD, WINDOW, LANES),
        in_specs=smem() + vmem(3),
        out_specs=vmem(1)[0],
        compiler_params=params(8 * 1024 * 1024),
        name="window",
    )(plane_offsets, from_low, to_low, from_high)
    (odd,) = boundary_switch(window, odd_offset, slabs, strips, 1, (0,))

    quarters = pltpu.SemaphoreType.DMA((len(QUARTERS),))
    return pl.pallas_call(
        main_kernel,
        out_shape=(f32(*populations.shape), f32(*order_pops.shape)),
        in_specs=smem() + hbm(8),
        out_specs=tuple(hbm(2)),
        scratch_shapes=[
            scratch(*populations.shape),
            scratch(*order_pops.shape),
            scratch(PAYLOAD * PLANES, LANES),
            scratch(PAYLOAD * PLANES, LANES),
            scratch(3, PAYLOAD, ROWS, LANES),
            scratch(PAYLOAD, WINDOW, LANES),
            scratch(*populations.shape),
            scratch(*order_pops.shape),
            scratch(PLANES, ROWS, LANES),
            scratch(PAYLOAD, WINDOW, LANES),
            scratch(PAYLOAD, WINDOW, LANES),
            scratch(4, WINDOW, LANES),
            scratch(20, WINDOW, LANES),
            scratch(PLANES + 2, ROWS, LANES),
            scratch(10, PLANES, LANES),
            scratch(10, PLANES, LANES),
            scratch(2, PLANES, LANES),
            quarters,
            quarters,
            pltpu.SemaphoreType.DMA((6,)),
            quarters,
            quarters,
        ],
        compiler_params=params(),
        name="collide_stream",
    )(plane_offsets, populations, order_pops, from_low, from_high, minus, same, plus, odd)


def solution(mesh):
    return jax.shard_map(
        shards,
        mesh=mesh,
        in_specs=(P(None, "gx", "gy", None), P(None, "gx", "gy", None), P()),
        out_specs=(P(None, "gx", "gy", None), P(None, "gx", "gy", None)),
        check_vma=False,
    )
```

```python
import jax
import jax.numpy as jnp
from jax import lax
from jax.experimental import pallas as pl
from jax.experimental.pallas import tpu as pltpu
from jax.sharding import PartitionSpec as P

SHIFT_FRACTION = 0.375
WALL_SPEED = 0.05
RELAX_FLOW = 0.8
RELAX_ORDER = 0.9
BULK_COEFF = 0.05
SURFACE_COEFF = 0.04
MOBILITY = 1.0
VELOCITY_X = (0, 1, -1, 0, 0, 0, 0, 1, -1, 1, -1, 1, -1, 1, -1, 0, 0, 0, 0)
VELOCITY_Y = (0, 0, 0, 1, -1, 0, 0, 1, -1, -1, 1, 0, 0, 0, 0, 1, -1, 1, -1)
VELOCITY_Z = (0, 0, 0, 0, 0, 1, -1, 0, 0, 0, 0, 1, -1, -1, 1, 1, -1, -1, 1)
WEIGHT_TABLE = (1.0 / 3.0,) + (1.0 / 18.0,) * 6 + (1.0 / 36.0,) * 12

VELS = 19
PLANES = 16
ROWS = 8
LANES = 128
UP_X = tuple(i for i in range(VELS) if VELOCITY_X[i] == 1)
DOWN_X = tuple(i for i in range(VELS) if VELOCITY_X[i] == -1)
UP_Y = tuple(i for i in range(VELS) if VELOCITY_Y[i] == 1)
DOWN_Y = tuple(i for i in range(VELS) if VELOCITY_Y[i] == -1)
PAYLOAD = 17
AT_MOMENTS = 5
AT_ORDER = 9
AT_PHASE = 14
WINDOW = 16
WINDOW_PAD = 4

VMEM_LIMIT = 61500000


def roll_rows(cells, step):
    return pltpu.roll(cells, step % cells.shape[0], 0)


def roll_lanes(cells, step):
    return pltpu.roll(cells, step % LANES, cells.ndim - 1)


def moments(flow):
    parts = [flow(i) for i in range(VELS)]
    density = parts[0]
    for part in parts[1:]:
        density = density + part
    speeds = []
    for table in (VELOCITY_X, VELOCITY_Y, VELOCITY_Z):
        plus = [parts[i] for i in range(VELS) if table[i] == 1]
        minus = [parts[i] for i in range(VELS) if table[i] == -1]
        total = plus[0] - minus[0]
        for a, b in zip(plus[1:], minus[1:]):
            total = total + (a - b)
        speeds.append(total)
    return density, speeds


def potential_of(phase, neighbours):
    around = neighbours[0]
    for cells in neighbours[1:]:
        around = around + cells
    bulk = BULK_COEFF * (phase * phase * phase - phase)
    return bulk - SURFACE_COEFF * (around - 6.0 * phase)


def dot_velocity(i, vector):
    total = None
    for sign, part in zip((VELOCITY_X[i], VELOCITY_Y[i], VELOCITY_Z[i]), vector):
        if sign == 0:
            continue
        if total is None:
            total = part if sign == 1 else -part
        else:
            total = total + part if sign == 1 else total - part
    return total


def collide(wanted, flow, order, density, momentum, phase, potential, force):
    inverse = 1.0 / density
    speed = [(momentum[d] + 0.5 * force[d]) * inverse for d in range(3)]
    source = 1.0 - 0.5 / RELAX_FLOW
    relaxed = density * (1.0 / RELAX_FLOW)
    speed_sq = speed[0] * speed[0] + speed[1] * speed[1] + speed[2] * speed[2]
    work = speed[0] * force[0] + speed[1] * force[1] + speed[2] * force[2]
    even = relaxed * (1.0 - 1.5 * speed_sq) - (3.0 * source) * work
    odd = [3.0 * (relaxed * speed[d] + source * force[d]) for d in range(3)]
    quad = [4.5 * relaxed * speed[d] + (9.0 * source) * force[d] for d in range(3)]
    order_even = (3.0 * MOBILITY / RELAX_ORDER) * potential
    carried = (3.0 / RELAX_ORDER) * phase
    order_odd = [carried * speed[d] for d in range(3)]
    flow_out, order_out = {}, {}
    keep_flow = 1.0 - 1.0 / RELAX_FLOW
    keep_order = 1.0 - 1.0 / RELAX_ORDER
    done = set()
    for i in wanted:
        if i in done:
            continue
        weight = WEIGHT_TABLE[i]
        if i == 0:
            flow_out[0] = keep_flow * flow(0) + weight * even
            rest = phase - (2.0 * MOBILITY) * potential
            order_out[0] = keep_order * order(0) + (1.0 / RELAX_ORDER) * rest
            continue
        first = i if i % 2 == 1 else i - 1
        pair_even = weight * (even + dot_velocity(first, speed) * dot_velocity(first, quad))
        pair_odd = weight * dot_velocity(first, odd)
        pair_order = weight * dot_velocity(first, order_odd)
        for member, sign in ((first, 1), (first + 1, -1)):
            if member not in wanted:
                continue
            done.add(member)
            both = pair_even + pair_odd if sign == 1 else pair_even - pair_odd
            flow_out[member] = keep_flow * flow(member) + both
            both = weight * order_even
            both = both + pair_order if sign == 1 else both - pair_order
            order_out[member] = keep_order * order(member) + both
    return flow_out, order_out


def add_phase(phase_ref, order_ref, x):
    total = order_ref[0, x]
    for i in range(1, VELS):
        total = total + order_ref[i, x]
    phase_ref[x] = total


def plane_copies(source, target, sems, pieces):
    return [
        pltpu.make_async_copy(source.at[:, pl.ds(first, count)], target.at[:, pl.ds(first, count)], sems.at[index])
        for index, (first, count) in enumerate(pieces)
    ]


FLOW_PIECES = ((0, 1), (PLANES - 1, 1), (1, 4), (5, 5), (10, 5))
ORDER_PIECES = ((0, 3), (PLANES - 3, 3), (3, 5), (8, 5))
INNER = (2, PLANES - 2)
INNER_LOADS = ((1, 4), (5, 4), (9, 3), (12, 3))
INNER_STORES = ((1, 4), (5, 4), (9, 3), (12, 3))
OUTER_LOADS = ((0, 2), (PLANES - 2, 2))
OUTER_PARTS = ((1, 2), (PLANES - 3, 2))
OUTER_STORES = ((0, 3), (PLANES - 3, 3))
PACKED = PAYLOAD * (ROWS + PLANES)


def even_boundary(slab):
    return slab + 1 - slab % 2


def odd_boundary(slab, slabs):
    return lax.rem(slab + slab % 2, slabs)


def side_rows(index):
    return pl.ds(PAYLOAD * ROWS + index * PLANES, PLANES)


def side_row(ref, index, x):
    return ref[pl.ds(PAYLOAD * ROWS + index * PLANES + x, 1), :]


def payload_kernel(
    offset_ref, flow_hbm, order_hbm, even_step, odd_step, even_ref, odd_ref, low_ref, high_ref,
    flow_ref, order_ref, phase_ref, flow_sems, order_sems,
):
    flow_copies = plane_copies(flow_hbm, flow_ref, flow_sems, FLOW_PIECES)
    order_copies = plane_copies(order_hbm, order_ref, order_sems, ORDER_PIECES)
    for copy in flow_copies[:2] + order_copies[:2] + order_copies[2:] + flow_copies[2:]:
        copy.start()
    slab = lax.axis_index("gx")
    is_even = slab % 2 == 0
    strips = lax.axis_size("gy")
    even_step[0] = lax.rem((offset_ref[even_boundary(slab)] + 5) // ROWS, strips)
    odd_step[0] = lax.rem((offset_ref[odd_boundary(slab, offset_ref.shape[0])] + 5) // ROWS, strips)

    for copy in flow_copies[:2] + order_copies[:2]:
        copy.wait()
    for x in (0, 1, 2, PLANES - 3, PLANES - 2, PLANES - 1):
        add_phase(phase_ref, order_ref, x)
    sides = []
    for plane, inward, comps in ((PLANES - 1, -1, UP_X), (0, 1, DOWN_X)):
        density, momentum = moments(lambda i: flow_ref[i, plane])
        parts = [flow_ref[i, plane] for i in comps] + [density] + momentum
        parts += [order_ref[i, plane] for i in comps]
        parts += [phase_ref[plane + inward * d] for d in range(3)]
        sides.append(parts)
    for index, (last, first) in enumerate(zip(*sides)):
        even_ref[index] = jnp.where(is_even, last, first)
        odd = jnp.where(is_even, first, last)
        odd_ref[index] = odd
        low_ref[index * ROWS : (index + 1) * ROWS, :] = odd
        high_ref[index * ROWS : (index + 1) * ROWS, :] = odd
    for copy in order_copies[2:]:
        copy.wait()
    for x in range(3, PLANES - 3):
        add_phase(phase_ref, order_ref, x)
    for copy in flow_copies[2:]:
        copy.wait()
    for out_ref, row, inward, comps in ((high_ref, ROWS - 1, -1, UP_Y), (low_ref, 0, 1, DOWN_Y)):
        density, momentum = moments(lambda i: flow_ref[i, :, row, :])
        parts = [flow_ref[i, :, row, :] for i in comps] + [density] + momentum
        parts += [order_ref[i, :, row, :] for i in comps]
        parts += [phase_ref[:, row + inward * d, :] for d in range(3)]
        for index, part in enumerate(parts):
            out_ref[side_rows(index), :] = part


def window_kernel(offset_ref, before_ref, own_ref, after_ref, out_ref):
    slab = lax.axis_index("gx")
    inner = lax.rem(offset_ref[odd_boundary(slab, offset_ref.shape[0])] + 5, ROWS)

    def block(ref):
        return lambda index: ref[index * ROWS : (index + 1) * ROWS, :]

    blocks = [block(before_ref), lambda index: own_ref[index], block(after_ref)]
    cut_window(blocks, jnp.where(slab % 2 == 0, inner, 9 - inner), out_ref)


def cut_window(blocks, start, window_ref):
    row = lax.broadcasted_iota(jnp.int32, (ROWS, LANES), 0)
    inner = lax.rem(start, ROWS)
    back = lax.rem(ROWS - inner, ROWS)
    early = row < ROWS - inner
    near = start < ROWS
    for index in range(PAYLOAD):
        rolled = [pltpu.roll(block(index), back, 0) for block in blocks]
        first = jnp.where(near, rolled[0], rolled[1])
        second = jnp.where(near, rolled[1], rolled[2])
        window_ref[index, 0:ROWS] = jnp.where(early, first, second)
        window_ref[index, ROWS : 2 * ROWS] = jnp.where(early, second, rolled[2])


def ghost_plane(window_ref, comps, own, own_next, weight, kick_speed):
    other = 1.0 - weight

    def sheared(cells):
        return weight * cells + other * roll_rows(cells, 1)

    def seen(cells):
        return other * roll_rows(cells, -1) + weight * cells

    def sides(cells):
        return [roll_rows(cells, 1), roll_rows(cells, -1), roll_lanes(cells, 1), roll_lanes(cells, -1)]

    near, second, third = [window_ref[AT_PHASE + d] for d in range(3)]
    ghost_phase = sheared(near)
    own_potential = potential_of(own, [own_next, ghost_phase] + sides(own))
    near_potential = potential_of(near, [second, seen(own)] + sides(near))
    second_potential = potential_of(second, [third, near] + sides(second))
    beyond = seen(own_potential)
    outward = 1.0 if VELOCITY_X[comps[0]] == 1 else -1.0
    half = -0.5 * near
    force = [
        outward * half * (beyond - second_potential),
        half * (roll_rows(near_potential, -1) - roll_rows(near_potential, 1)),
        half * (roll_lanes(near_potential, -1) - roll_lanes(near_potential, 1)),
    ]
    density = window_ref[AT_MOMENTS]
    momentum = [window_ref[AT_MOMENTS + 1 + d] for d in range(3)]
    flow_out, order_out = collide(
        comps,
        lambda i: window_ref[comps.index(i)],
        lambda i: window_ref[AT_ORDER + comps.index(i)],
        density,
        momentum,
        near,
        near_potential,
        force,
    )
    flow_ghost = []
    for i in comps:
        cells = flow_out[i]
        if VELOCITY_Y[i] != 0:
            cells = cells + (WEIGHT_TABLE[i] * 3.0 * VELOCITY_Y[i] * kick_speed) * density
        flow_ghost.append(sheared(cells))
    order_ghost = [sheared(order_out[i]) for i in comps]
    return ghost_phase, own_potential, sheared(near_potential), flow_ghost, order_ghost


def rows_before(cells, line):
    row = lax.broadcasted_iota(jnp.int32, (ROWS, LANES), 0)
    return jnp.where(row == 0, line, roll_rows(cells, 1))


def rows_after(cells, line):
    row = lax.broadcasted_iota(jnp.int32, (ROWS, LANES), 0)
    return jnp.where(row == ROWS - 1, line, roll_rows(cells, -1))


def collide_sides(phase_ref, low_ref, high_ref, below, above, low_side, high_side, edge_ref):
    plane_at = lax.broadcasted_iota(jnp.int32, (PLANES, LANES), 0)

    def across(cells, which, own_row):
        before, after = roll_rows(cells, 1), roll_rows(cells, -1)
        if below is not None:
            before = jnp.where(plane_at == 0, below(which, own_row), before)
            after = jnp.where(plane_at == PLANES - 1, above(which, own_row), after)
        return before, after

    for side_ref, out_ref, edge, beside, inward, comps in (
        (low_ref, low_side, 0, -1, 1, UP_Y),
        (high_ref, high_side, ROWS - 1, ROWS, -1, DOWN_Y),
    ):
        own = [phase_ref[:, edge + inward * d, :] for d in range(2)]
        outer = [side_ref[side_rows(AT_PHASE + d), :] for d in range(3)]
        lines = [own[1], own[0]] + outer
        potentials = []
        for index in range(1, 4):
            cells = lines[index]
            around = list(across(cells, 0, edge + inward * (1 - index)))
            around += [lines[index - 1], lines[index + 1], roll_lanes(cells, 1), roll_lanes(cells, -1)]
            potentials.append(potential_of(cells, around))
        inside, here, outside = potentials
        before, after = across(here, 1, beside)
        half = -0.5 * outer[0]
        force = [
            half * (after - before),
            (inward * half) * (inside - outside),
            half * (roll_lanes(here, -1) - roll_lanes(here, 1)),
        ]
        flow_post, order_post = collide(
            comps,
            lambda i: side_ref[side_rows(comps.index(i)), :],
            lambda i: side_ref[side_rows(AT_ORDER + comps.index(i)), :],
            side_ref[side_rows(AT_MOMENTS), :],
            [side_ref[side_rows(AT_MOMENTS + 1 + d), :] for d in range(3)],
            outer[0],
            here,
            force,
        )
        for index, i in enumerate(comps):
            out_ref[index] = flow_post[i]
            out_ref[5 + index] = order_post[i]
        edge_ref[0 if inward == 1 else 1] = here


def plane_potential(phase_ref, low_ref, high_ref, x):
    cells = phase_ref[x]
    around = [
        phase_ref[x - 1],
        phase_ref[x + 1],
        rows_before(cells, side_row(low_ref, AT_PHASE, x)),
        rows_after(cells, side_row(high_ref, AT_PHASE, x)),
        roll_lanes(cells, 1),
        roll_lanes(cells, -1),
    ]
    return potential_of(cells, around)


def collide_plane(x, skip, flow_ref, order_ref, phase_ref, potential_ref, edge_ref, low_side, high_side, flow_out, order_out):
    here = potential_ref[x + 1]
    phase = phase_ref[x]
    half = -0.5 * phase
    along_y = rows_after(here, edge_ref[1, pl.ds(x, 1), :]) - rows_before(here, edge_ref[0, pl.ds(x, 1), :])
    force = [
        half * (potential_ref[x + 2] - potential_ref[x]),
        half * along_y,
        half * (roll_lanes(here, -1) - roll_lanes(here, 1)),
    ]
    density, momentum = moments(lambda i: flow_ref[i, x])
    flow_post, order_post = collide(
        tuple(i for i in range(VELS) if VELOCITY_X[i] == 0 or VELOCITY_X[i] != skip),
        lambda i: flow_ref[i, x],
        lambda i: order_ref[i, x],
        density,
        momentum,
        phase,
        here,
        force,
    )

    def moved(i, cells, first):
        if VELOCITY_Y[i] == 1:
            cells = rows_before(cells, low_side[first + UP_Y.index(i), pl.ds(x, 1), :])
        elif VELOCITY_Y[i] == -1:
            cells = rows_after(cells, high_side[first + DOWN_Y.index(i), pl.ds(x, 1), :])
        if VELOCITY_Z[i] != 0:
            cells = roll_lanes(cells, VELOCITY_Z[i])
        return cells

    for i in flow_post:
        target = x + VELOCITY_X[i]
        flow_out[i, target] = moved(i, flow_post[i], 0)
        order_out[i, target] = moved(i, order_post[i], 5)


def inner_kernel(
    flow_hbm, order_hbm, low_hbm, high_hbm, phase_ref, flow_hbm_out, order_hbm_out,
    flow_ref, order_ref, low_ref, high_ref, flow_out, order_out, potential_ref, low_side, high_side, edge_ref,
    flow_sems, order_sems, side_sems, flow_out_sems, order_out_sems,
):
    whole_order = pltpu.make_async_copy(order_hbm, order_ref, order_sems.at[0])
    sides = [
        pltpu.make_async_copy(low_hbm, low_ref, side_sems.at[0]),
        pltpu.make_async_copy(high_hbm, high_ref, side_sems.at[1]),
    ]
    flow_copies = plane_copies(flow_hbm, flow_ref, flow_sems, INNER_LOADS)
    for copy in [whole_order] + sides + flow_copies:
        copy.start()
    whole_order.wait()
    for x in range(PLANES):
        add_phase(phase_ref, order_ref, x)
    for copy in sides:
        copy.wait()
    collide_sides(phase_ref, low_ref, high_ref, None, None, low_side, high_side, edge_ref)
    for x in range(1, PLANES - 1):
        potential_ref[x + 1] = plane_potential(phase_ref, low_ref, high_ref, x)

    def step(x, carry):
        collide_plane(
            x, 0, flow_ref, order_ref, phase_ref, potential_ref, edge_ref, low_side, high_side, flow_out, order_out
        )
        return carry

    flow_writes = plane_copies(flow_out, flow_hbm_out, flow_out_sems, INNER_STORES)
    order_writes = plane_copies(order_out, order_hbm_out, order_out_sems, INNER_STORES)
    for part, (first, count) in enumerate(INNER_LOADS):
        flow_copies[part].wait()
        lax.fori_loop(max(first, INNER[0]), min(first + count, INNER[1]), step, 0)
        if part > 0:
            flow_writes[part - 1].start()
            order_writes[part - 1].start()
    flow_writes[-1].start()
    order_writes[-1].start()
    for copy in flow_writes + order_writes:
        copy.wait()


def outer_kernel(
    offset_ref, flow_hbm, order_hbm, phase_ref, low_ref, high_ref, minus_ref, same_ref, plus_ref, odd_ref,
    flow_part, order_part, flow_hbm_out, order_hbm_out,
    flow_ref, order_ref, flow_out, order_out,
    below_ref, above_ref, wide_ref, ghost_ref, potential_ref, low_side, high_side, edge_ref,
    flow_sems, order_sems, flow_part_sems, order_part_sems, flow_out_sems, order_out_sems,
):
    loads = plane_copies(order_hbm, order_ref, order_sems, OUTER_LOADS)
    loads += plane_copies(flow_hbm, flow_ref, flow_sems, OUTER_LOADS)
    loads += plane_copies(flow_part, flow_out, flow_part_sems, OUTER_PARTS)
    loads += plane_copies(order_part, order_out, order_part_sems, OUTER_PARTS)
    for copy in loads:
        copy.start()

    slab = lax.axis_index("gx")
    is_even = slab % 2 == 0
    inner = lax.rem(offset_ref[even_boundary(slab)] + 5, ROWS)
    blocks = [
        lambda at: jnp.where(is_even, minus_ref[at], plus_ref[at]),
        lambda at: same_ref[at],
        lambda at: jnp.where(is_even, plus_ref[at], minus_ref[at]),
    ]
    cut_window(blocks, jnp.where(is_even, inner, 9 - inner), above_ref)
    for index in range(PAYLOAD):
        even, odd = above_ref[index], odd_ref[index]
        below_ref[index] = jnp.where(is_even, odd, even)
        above_ref[index] = jnp.where(is_even, even, odd)

    for index, plane in enumerate((0, 1, PLANES - 1, PLANES - 2)):
        wide_ref[index] = jnp.zeros((WINDOW, LANES), jnp.float32)
        for d in range(3):
            wide_ref[index, 3 - d : 4 - d, :] = side_row(low_ref, AT_PHASE + d, plane)
            wide_ref[index, 12 + d : 13 + d, :] = side_row(high_ref, AT_PHASE + d, plane)
        wide_ref[index, 4:12, :] = phase_ref[plane]
    below = ghost_plane(below_ref, UP_X, wide_ref[0], wide_ref[1], 1.0 - SHIFT_FRACTION, WALL_SPEED)
    above = ghost_plane(above_ref, DOWN_X, wide_ref[2], wide_ref[3], SHIFT_FRACTION, -WALL_SPEED)
    for index in range(5):
        ghost_ref[index] = below[3][index]
        ghost_ref[5 + index] = below[4][index]
        ghost_ref[10 + index] = above[3][index]
        ghost_ref[15 + index] = above[4][index]

    def ghost_row(ghost):
        return lambda which, own_row: ghost[2 * which][own_row + WINDOW_PAD : own_row + WINDOW_PAD + 1, :]

    collide_sides(
        phase_ref, low_ref, high_ref, ghost_row(below), ghost_row(above), low_side, high_side, edge_ref
    )
    wide_ref[0] = below[1]
    wide_ref[1] = below[2]
    wide_ref[2] = above[1]
    wide_ref[3] = above[2]
    potential_ref[1] = wide_ref[0, 4:12, :]
    potential_ref[0] = wide_ref[1, 4:12, :]
    potential_ref[PLANES] = wide_ref[2, 4:12, :]
    potential_ref[PLANES + 1] = wide_ref[3, 4:12, :]
    for x in (1, 2, PLANES - 3, PLANES - 2):
        potential_ref[x + 1] = plane_potential(phase_ref, low_ref, high_ref, x)
    for copy in loads:
        copy.wait()
    for comps, first, target in ((UP_X, 0, 0), (DOWN_X, 10, PLANES - 1)):
        for index, i in enumerate(comps):
            start = WINDOW_PAD - VELOCITY_Y[i]
            for out_ref, at in ((flow_out, first + index), (order_out, first + 5 + index)):
                cells = ghost_ref[at, start : start + ROWS, :]
                if VELOCITY_Z[i] != 0:
                    cells = roll_lanes(cells, VELOCITY_Z[i])
                out_ref[i, target] = cells
    flow_writes = plane_copies(flow_out, flow_hbm_out, flow_out_sems, OUTER_STORES)
    order_writes = plane_copies(order_out, order_hbm_out, order_out_sems, OUTER_STORES)
    for end, planes in enumerate((((0, -1), (1, 0)), ((PLANES - 2, 0), (PLANES - 1, 1)))):
        for x, skip in planes:
            collide_plane(
                x, skip, flow_ref, order_ref, phase_ref, potential_ref, edge_ref, low_side, high_side, flow_out, order_out
            )
        flow_writes[end].start()
        order_writes[end].start()
    for copy in flow_writes + order_writes:
        copy.wait()


def vmem(count):
    return [pl.BlockSpec(memory_space=pltpu.VMEM)] * count


def params(limit=VMEM_LIMIT):
    return pltpu.CompilerParams(vmem_limit_bytes=limit)


def f32(*shape):
    return jax.ShapeDtypeStruct(shape, jnp.float32)


def shift_pairs(count, step):
    return [(i, (i + step) % count) for i in range(count)]


def swap_pairs(slabs, strips, first, step):
    pairs = []
    for low in range(first, slabs, 2):
        high = (low + 1) % slabs
        for strip in range(strips):
            other = (strip + step) % strips
            pairs.append((low * strips + strip, high * strips + other))
            pairs.append((high * strips + other, low * strips + strip))
    return pairs


def hbm(count):
    return [pl.BlockSpec(memory_space=pltpu.HBM)] * count


def smem():
    return [pl.BlockSpec(memory_space=pltpu.SMEM)]


def scratch(*shape):
    return pltpu.VMEM(shape, jnp.float32)


def sems(count):
    return pltpu.SemaphoreType.DMA((count,))


def inner_planes(populations, order_pops, from_low, from_high):
    return pl.pallas_call(
        inner_kernel,
        out_shape=(f32(PLANES, ROWS, LANES), f32(*populations.shape), f32(*order_pops.shape)),
        in_specs=hbm(4),
        out_specs=tuple(vmem(1) + hbm(2)),
        scratch_shapes=[
            scratch(*populations.shape),
            scratch(*order_pops.shape),
            scratch(PACKED, LANES),
            scratch(PACKED, LANES),
            scratch(*populations.shape),
            scratch(*order_pops.shape),
            scratch(PLANES + 2, ROWS, LANES),
            scratch(10, PLANES, LANES),
            scratch(10, PLANES, LANES),
            scratch(2, PLANES, LANES),
            sems(len(INNER_LOADS)),
            sems(1),
            sems(2),
            sems(len(INNER_STORES)),
            sems(len(INNER_STORES)),
        ],
        compiler_params=params(),
        name="inner_planes",
    )(populations, order_pops, from_low, from_high)


def outer_planes(plane_offsets, populations, order_pops, phase, from_low, from_high, blocks, odd, flow_part, order_part):
    return pl.pallas_call(
        outer_kernel,
        out_shape=(f32(*populations.shape), f32(*order_pops.shape)),
        in_specs=smem() + hbm(2) + vmem(7) + hbm(2),
        out_specs=tuple(hbm(2)),
        input_output_aliases={10: 0, 11: 1},
        scratch_shapes=[
            scratch(*populations.shape),
            scratch(*order_pops.shape),
            scratch(*populations.shape),
            scratch(*order_pops.shape),
            scratch(PAYLOAD, WINDOW, LANES),
            scratch(PAYLOAD, WINDOW, LANES),
            scratch(4, WINDOW, LANES),
            scratch(20, WINDOW, LANES),
            scratch(PLANES + 2, ROWS, LANES),
            scratch(10, PLANES, LANES),
            scratch(10, PLANES, LANES),
            scratch(2, PLANES, LANES),
            sems(2),
            sems(2),
            sems(2),
            sems(2),
            sems(2),
            sems(2),
        ],
        compiler_params=params(),
        name="outer_planes",
    )(plane_offsets, populations, order_pops, phase, from_low, from_high, *blocks, odd, flow_part, order_part)


def shards(populations, order_pops, plane_offsets):
    slabs, strips = lax.axis_size("gx"), lax.axis_size("gy")
    even_step, odd_step, even, own_odd, to_low, to_high = pl.pallas_call(
        payload_kernel,
        out_shape=(
            jax.ShapeDtypeStruct((1,), jnp.int32),
            jax.ShapeDtypeStruct((1,), jnp.int32),
            f32(PAYLOAD, ROWS, LANES),
            f32(PAYLOAD, ROWS, LANES),
            f32(PACKED, LANES),
            f32(PACKED, LANES),
        ),
        in_specs=smem() + hbm(2),
        out_specs=tuple(smem() * 2 + vmem(4)),
        scratch_shapes=[
            scratch(*populations.shape),
            scratch(*order_pops.shape),
            scratch(PLANES, ROWS, LANES),
            sems(len(FLOW_PIECES)),
            sems(len(ORDER_PIECES)),
        ],
        compiler_params=params(),
        name="payloads",
    )(plane_offsets, populations, order_pops)

    from_low = lax.ppermute(to_high, "gy", shift_pairs(strips, 1))
    from_high = lax.ppermute(to_low, "gy", shift_pairs(strips, -1))

    def even_branch(step):
        def run(payload):
            return tuple(
                lax.ppermute(payload, ("gx", "gy"), swap_pairs(slabs, strips, 0, step + d)) for d in (-1, 0, 1)
            )

        return run

    blocks = lax.switch(even_step.reshape(()), [even_branch(step) for step in range(strips)], even)
    window = pl.pallas_call(
        window_kernel,
        out_shape=f32(PAYLOAD, WINDOW, LANES),
        in_specs=smem() + vmem(3),
        out_specs=vmem(1)[0],
        compiler_params=params(8 * 1024 * 1024),
        name="window",
    )(plane_offsets, from_low, own_odd, from_high)

    def odd_branch(step):
        def run(offsets, flow, order, low, high, near, mine):
            odd = lax.ppermute(mine, ("gx", "gy"), swap_pairs(slabs, strips, 1, step))
            phase, flow_part, order_part = inner_planes(flow, order, low, high)
            return outer_planes(offsets, flow, order, phase, low, high, near, odd, flow_part, order_part)

        return run

    branches = [odd_branch(step) for step in range(strips)]
    return lax.switch(
        odd_step.reshape(()), branches, plane_offsets, populations, order_pops, from_low, from_high, blocks, window
    )


def solution(mesh):
    return jax.shard_map(
        shards,
        mesh=mesh,
        in_specs=(P(None, "gx", "gy", None), P(None, "gx", "gy", None), P()),
        out_specs=(P(None, "gx", "gy", None), P(None, "gx", "gy", None)),
        check_vma=False,
    )
```

```python
import jax
import jax.numpy as jnp
from jax import lax
from jax.experimental import pallas as pl
from jax.experimental.pallas import tpu as pltpu
from jax.sharding import PartitionSpec as P

SHIFT_FRACTION = 0.375
WALL_SPEED = 0.05
RELAX_FLOW = 0.8
RELAX_ORDER = 0.9
BULK_COEFF = 0.05
SURFACE_COEFF = 0.04
MOBILITY = 1.0
VELOCITY_X = (0, 1, -1, 0, 0, 0, 0, 1, -1, 1, -1, 1, -1, 1, -1, 0, 0, 0, 0)
VELOCITY_Y = (0, 0, 0, 1, -1, 0, 0, 1, -1, -1, 1, 0, 0, 0, 0, 1, -1, 1, -1)
VELOCITY_Z = (0, 0, 0, 0, 0, 1, -1, 0, 0, 0, 0, 1, -1, -1, 1, 1, -1, -1, 1)
WEIGHT_TABLE = (1.0 / 3.0,) + (1.0 / 18.0,) * 6 + (1.0 / 36.0,) * 12

VELS = 19
PLANES = 16
ROWS = 8
LANES = 128
UP_X = tuple(i for i in range(VELS) if VELOCITY_X[i] == 1)
DOWN_X = tuple(i for i in range(VELS) if VELOCITY_X[i] == -1)
UP_Y = tuple(i for i in range(VELS) if VELOCITY_Y[i] == 1)
DOWN_Y = tuple(i for i in range(VELS) if VELOCITY_Y[i] == -1)
PAYLOAD = 17
AT_MOMENTS = 5
AT_ORDER = 9
AT_PHASE = 14
WINDOW = 16
WINDOW_PAD = 4

VMEM_LIMIT = 61500000
SMALL_VMEM = 16 * 1024 * 1024


def roll_rows(cells, step):
    return pltpu.roll(cells, step % cells.shape[0], 0)


def roll_lanes(cells, step):
    return pltpu.roll(cells, step % LANES, cells.ndim - 1)


def moments(flow):
    parts = [flow(i) for i in range(VELS)]
    density = parts[0]
    for part in parts[1:]:
        density = density + part
    speeds = []
    for table in (VELOCITY_X, VELOCITY_Y, VELOCITY_Z):
        plus = [parts[i] for i in range(VELS) if table[i] == 1]
        minus = [parts[i] for i in range(VELS) if table[i] == -1]
        total = plus[0] - minus[0]
        for a, b in zip(plus[1:], minus[1:]):
            total = total + (a - b)
        speeds.append(total)
    return density, speeds


def potential_of(phase, neighbours):
    around = neighbours[0]
    for cells in neighbours[1:]:
        around = around + cells
    bulk = BULK_COEFF * (phase * phase * phase - phase)
    return bulk - SURFACE_COEFF * (around - 6.0 * phase)


def dot_velocity(i, vector):
    total = None
    for sign, part in zip((VELOCITY_X[i], VELOCITY_Y[i], VELOCITY_Z[i]), vector):
        if sign == 0:
            continue
        if total is None:
            total = part if sign == 1 else -part
        else:
            total = total + part if sign == 1 else total - part
    return total


def collide(wanted, flow, order, density, momentum, phase, potential, force):
    inverse = 1.0 / density
    speed = [(momentum[d] + 0.5 * force[d]) * inverse for d in range(3)]
    source = 1.0 - 0.5 / RELAX_FLOW
    relaxed = density * (1.0 / RELAX_FLOW)
    speed_sq = speed[0] * speed[0] + speed[1] * speed[1] + speed[2] * speed[2]
    work = speed[0] * force[0] + speed[1] * force[1] + speed[2] * force[2]
    even = relaxed * (1.0 - 1.5 * speed_sq) - (3.0 * source) * work
    odd = [3.0 * (relaxed * speed[d] + source * force[d]) for d in range(3)]
    quad = [4.5 * relaxed * speed[d] + (9.0 * source) * force[d] for d in range(3)]
    order_even = (3.0 * MOBILITY / RELAX_ORDER) * potential
    carried = (3.0 / RELAX_ORDER) * phase
    order_odd = [carried * speed[d] for d in range(3)]
    flow_out, order_out = {}, {}
    keep_flow = 1.0 - 1.0 / RELAX_FLOW
    keep_order = 1.0 - 1.0 / RELAX_ORDER
    done = set()
    for i in wanted:
        if i in done:
            continue
        weight = WEIGHT_TABLE[i]
        if i == 0:
            flow_out[0] = keep_flow * flow(0) + weight * even
            rest = phase - (2.0 * MOBILITY) * potential
            order_out[0] = keep_order * order(0) + (1.0 / RELAX_ORDER) * rest
            continue
        first = i if i % 2 == 1 else i - 1
        pair_even = weight * (even + dot_velocity(first, speed) * dot_velocity(first, quad))
        pair_odd = weight * dot_velocity(first, odd)
        pair_order = weight * dot_velocity(first, order_odd)
        for member, sign in ((first, 1), (first + 1, -1)):
            if member not in wanted:
                continue
            done.add(member)
            both = pair_even + pair_odd if sign == 1 else pair_even - pair_odd
            flow_out[member] = keep_flow * flow(member) + both
            both = weight * order_even
            both = both + pair_order if sign == 1 else both - pair_order
            order_out[member] = keep_order * order(member) + both
    return flow_out, order_out


def add_phase(phase_ref, order_ref, x):
    total = order_ref[0, x]
    for i in range(1, VELS):
        total = total + order_ref[i, x]
    phase_ref[x] = total


def plane_copies(source, target, sems, pieces):
    return [
        pltpu.make_async_copy(source.at[:, pl.ds(first, count)], target.at[:, pl.ds(first, count)], sems.at[index])
        for index, (first, count) in enumerate(pieces)
    ]


FLOW_PIECES = ((0, 1), (PLANES - 1, 1), (1, 4), (5, 5), (10, 5))
ORDER_PIECES = ((0, 3), (PLANES - 3, 3), (3, 5), (8, 5))
INNER = (2, PLANES - 2)
INNER_LOADS = ((1, 4), (5, 4), (9, 3), (12, 3))
INNER_STORES = ((1, 4), (5, 4), (9, 3), (12, 3))
OUTER_LOADS = ((0, 2), (PLANES - 2, 2))
OUTER_PARTS = ((1, 2), (PLANES - 3, 2))
OUTER_STORES = ((0, 3), (PLANES - 3, 3))
PACKED = PAYLOAD * (ROWS + PLANES)


def even_boundary(slab):
    return slab + 1 - slab % 2


def odd_boundary(slab, slabs):
    return lax.rem(slab + slab % 2, slabs)


def side_rows(index):
    return pl.ds(PAYLOAD * ROWS + index * PLANES, PLANES)


def side_row(ref, index, x):
    return ref[pl.ds(PAYLOAD * ROWS + index * PLANES + x, 1), :]


def payload_kernel(
    offset_ref, flow_hbm, order_hbm, even_step, odd_step, even_ref, odd_ref, low_ref, high_ref,
    flow_ref, order_ref, phase_ref, flow_sems, order_sems,
):
    flow_copies = plane_copies(flow_hbm, flow_ref, flow_sems, FLOW_PIECES)
    order_copies = plane_copies(order_hbm, order_ref, order_sems, ORDER_PIECES)
    for copy in flow_copies[:2] + order_copies[:2] + order_copies[2:] + flow_copies[2:]:
        copy.start()
    slab = lax.axis_index("gx")
    is_even = slab % 2 == 0
    strips = lax.axis_size("gy")
    even_step[0] = lax.rem((offset_ref[even_boundary(slab)] + 5) // ROWS, strips)
    odd_step[0] = lax.rem((offset_ref[odd_boundary(slab, offset_ref.shape[0])] + 5) // ROWS, strips)

    for copy in flow_copies[:2] + order_copies[:2]:
        copy.wait()
    for x in (0, 1, 2, PLANES - 3, PLANES - 2, PLANES - 1):
        add_phase(phase_ref, order_ref, x)
    sides = []
    for plane, inward, comps in ((PLANES - 1, -1, UP_X), (0, 1, DOWN_X)):
        density, momentum = moments(lambda i: flow_ref[i, plane])
        parts = [flow_ref[i, plane] for i in comps] + [density] + momentum
        parts += [order_ref[i, plane] for i in comps]
        parts += [phase_ref[plane + inward * d] for d in range(3)]
        sides.append(parts)
    for index, (last, first) in enumerate(zip(*sides)):
        even_ref[index] = jnp.where(is_even, last, first)
        odd = jnp.where(is_even, first, last)
        odd_ref[index] = odd
        low_ref[index * ROWS : (index + 1) * ROWS, :] = odd
        high_ref[index * ROWS : (index + 1) * ROWS, :] = odd
    for copy in order_copies[2:]:
        copy.wait()
    for x in range(3, PLANES - 3):
        add_phase(phase_ref, order_ref, x)
    for copy in flow_copies[2:]:
        copy.wait()
    for out_ref, row, inward, comps in ((high_ref, ROWS - 1, -1, UP_Y), (low_ref, 0, 1, DOWN_Y)):
        density, momentum = moments(lambda i: flow_ref[i, :, row, :])
        parts = [flow_ref[i, :, row, :] for i in comps] + [density] + momentum
        parts += [order_ref[i, :, row, :] for i in comps]
        parts += [phase_ref[:, row + inward * d, :] for d in range(3)]
        for index, part in enumerate(parts):
            out_ref[side_rows(index), :] = part


def window_kernel(offset_ref, before_ref, own_ref, after_ref, out_ref):
    slab = lax.axis_index("gx")
    inner = lax.rem(offset_ref[odd_boundary(slab, offset_ref.shape[0])] + 5, ROWS)

    def block(ref):
        return lambda index: ref[index * ROWS : (index + 1) * ROWS, :]

    blocks = [block(before_ref), lambda index: own_ref[index], block(after_ref)]
    cut_window(blocks, jnp.where(slab % 2 == 0, inner, 9 - inner), out_ref)


def cut_window(blocks, start, window_ref):
    row = lax.broadcasted_iota(jnp.int32, (ROWS, LANES), 0)
    inner = lax.rem(start, ROWS)
    back = lax.rem(ROWS - inner, ROWS)
    early = row < ROWS - inner
    near = start < ROWS
    for index in range(PAYLOAD):
        rolled = [pltpu.roll(block(index), back, 0) for block in blocks]
        first = jnp.where(near, rolled[0], rolled[1])
        second = jnp.where(near, rolled[1], rolled[2])
        window_ref[index, 0:ROWS] = jnp.where(early, first, second)
        window_ref[index, ROWS : 2 * ROWS] = jnp.where(early, second, rolled[2])


def ghost_plane(window_ref, comps, own, own_next, weight, kick_speed):
    other = 1.0 - weight

    def sheared(cells):
        return weight * cells + other * roll_rows(cells, 1)

    def seen(cells):
        return other * roll_rows(cells, -1) + weight * cells

    def sides(cells):
        return [roll_rows(cells, 1), roll_rows(cells, -1), roll_lanes(cells, 1), roll_lanes(cells, -1)]

    near, second, third = [window_ref[AT_PHASE + d] for d in range(3)]
    ghost_phase = sheared(near)
    own_potential = potential_of(own, [own_next, ghost_phase] + sides(own))
    near_potential = potential_of(near, [second, seen(own)] + sides(near))
    second_potential = potential_of(second, [third, near] + sides(second))
    beyond = seen(own_potential)
    outward = 1.0 if VELOCITY_X[comps[0]] == 1 else -1.0
    half = -0.5 * near
    force = [
        outward * half * (beyond - second_potential),
        half * (roll_rows(near_potential, -1) - roll_rows(near_potential, 1)),
        half * (roll_lanes(near_potential, -1) - roll_lanes(near_potential, 1)),
    ]
    density = window_ref[AT_MOMENTS]
    momentum = [window_ref[AT_MOMENTS + 1 + d] for d in range(3)]
    flow_out, order_out = collide(
        comps,
        lambda i: window_ref[comps.index(i)],
        lambda i: window_ref[AT_ORDER + comps.index(i)],
        density,
        momentum,
        near,
        near_potential,
        force,
    )
    flow_ghost = []
    for i in comps:
        cells = flow_out[i]
        if VELOCITY_Y[i] != 0:
            cells = cells + (WEIGHT_TABLE[i] * 3.0 * VELOCITY_Y[i] * kick_speed) * density
        flow_ghost.append(sheared(cells))
    order_ghost = [sheared(order_out[i]) for i in comps]
    return ghost_phase, own_potential, sheared(near_potential), flow_ghost, order_ghost


def rows_before(cells, line):
    row = lax.broadcasted_iota(jnp.int32, (ROWS, LANES), 0)
    return jnp.where(row == 0, line, roll_rows(cells, 1))


def rows_after(cells, line):
    row = lax.broadcasted_iota(jnp.int32, (ROWS, LANES), 0)
    return jnp.where(row == ROWS - 1, line, roll_rows(cells, -1))


def collide_sides(phase_ref, low_ref, high_ref, below, above, low_side, high_side, edge_ref):
    plane_at = lax.broadcasted_iota(jnp.int32, (PLANES, LANES), 0)

    def across(cells, which, own_row):
        before, after = roll_rows(cells, 1), roll_rows(cells, -1)
        if below is not None:
            before = jnp.where(plane_at == 0, below(which, own_row), before)
            after = jnp.where(plane_at == PLANES - 1, above(which, own_row), after)
        return before, after

    for side_ref, out_ref, edge, beside, inward, comps in (
        (low_ref, low_side, 0, -1, 1, UP_Y),
        (high_ref, high_side, ROWS - 1, ROWS, -1, DOWN_Y),
    ):
        own = [phase_ref[:, edge + inward * d, :] for d in range(2)]
        outer = [side_ref[side_rows(AT_PHASE + d), :] for d in range(3)]
        lines = [own[1], own[0]] + outer
        potentials = []
        for index in range(1, 4):
            cells = lines[index]
            around = list(across(cells, 0, edge + inward * (1 - index)))
            around += [lines[index - 1], lines[index + 1], roll_lanes(cells, 1), roll_lanes(cells, -1)]
            potentials.append(potential_of(cells, around))
        inside, here, outside = potentials
        before, after = across(here, 1, beside)
        half = -0.5 * outer[0]
        force = [
            half * (after - before),
            (inward * half) * (inside - outside),
            half * (roll_lanes(here, -1) - roll_lanes(here, 1)),
        ]
        flow_post, order_post = collide(
            comps,
            lambda i: side_ref[side_rows(comps.index(i)), :],
            lambda i: side_ref[side_rows(AT_ORDER + comps.index(i)), :],
            side_ref[side_rows(AT_MOMENTS), :],
            [side_ref[side_rows(AT_MOMENTS + 1 + d), :] for d in range(3)],
            outer[0],
            here,
            force,
        )
        for index, i in enumerate(comps):
            out_ref[index] = flow_post[i]
            out_ref[5 + index] = order_post[i]
        edge_ref[0 if inward == 1 else 1] = here


def plane_potential(phase_ref, low_ref, high_ref, x):
    cells = phase_ref[x]
    around = [
        phase_ref[x - 1],
        phase_ref[x + 1],
        rows_before(cells, side_row(low_ref, AT_PHASE, x)),
        rows_after(cells, side_row(high_ref, AT_PHASE, x)),
        roll_lanes(cells, 1),
        roll_lanes(cells, -1),
    ]
    return potential_of(cells, around)


def collide_plane(x, skip, flow_ref, order_ref, phase_ref, potential_ref, edge_ref, low_side, high_side, flow_out, order_out):
    here = potential_ref[x + 1]
    phase = phase_ref[x]
    half = -0.5 * phase
    along_y = rows_after(here, edge_ref[1, pl.ds(x, 1), :]) - rows_before(here, edge_ref[0, pl.ds(x, 1), :])
    force = [
        half * (potential_ref[x + 2] - potential_ref[x]),
        half * along_y,
        half * (roll_lanes(here, -1) - roll_lanes(here, 1)),
    ]
    density, momentum = moments(lambda i: flow_ref[i, x])
    flow_post, order_post = collide(
        tuple(i for i in range(VELS) if VELOCITY_X[i] == 0 or VELOCITY_X[i] != skip),
        lambda i: flow_ref[i, x],
        lambda i: order_ref[i, x],
        density,
        momentum,
        phase,
        here,
        force,
    )

    def moved(i, cells, first):
        if VELOCITY_Y[i] == 1:
            cells = rows_before(cells, low_side[first + UP_Y.index(i), pl.ds(x, 1), :])
        elif VELOCITY_Y[i] == -1:
            cells = rows_after(cells, high_side[first + DOWN_Y.index(i), pl.ds(x, 1), :])
        if VELOCITY_Z[i] != 0:
            cells = roll_lanes(cells, VELOCITY_Z[i])
        return cells

    for i in flow_post:
        target = x + VELOCITY_X[i]
        flow_out[i, target] = moved(i, flow_post[i], 0)
        order_out[i, target] = moved(i, order_post[i], 5)


def inner_kernel(
    flow_hbm, order_hbm, low_hbm, high_hbm, phase_ref, flow_hbm_out, order_hbm_out,
    flow_ref, order_ref, low_ref, high_ref, flow_out, order_out, potential_ref, low_side, high_side, edge_ref,
    flow_sems, order_sems, side_sems, flow_out_sems, order_out_sems,
):
    whole_order = pltpu.make_async_copy(order_hbm, order_ref, order_sems.at[0])
    sides = [
        pltpu.make_async_copy(low_hbm, low_ref, side_sems.at[0]),
        pltpu.make_async_copy(high_hbm, high_ref, side_sems.at[1]),
    ]
    flow_copies = plane_copies(flow_hbm, flow_ref, flow_sems, INNER_LOADS)
    for copy in [whole_order] + sides + flow_copies:
        copy.start()
    whole_order.wait()
    for x in range(PLANES):
        add_phase(phase_ref, order_ref, x)
    for copy in sides:
        copy.wait()
    collide_sides(phase_ref, low_ref, high_ref, None, None, low_side, high_side, edge_ref)
    for x in range(1, PLANES - 1):
        potential_ref[x + 1] = plane_potential(phase_ref, low_ref, high_ref, x)

    def step(x, carry):
        collide_plane(
            x, 0, flow_ref, order_ref, phase_ref, potential_ref, edge_ref, low_side, high_side, flow_out, order_out
        )
        return carry

    flow_writes = plane_copies(flow_out, flow_hbm_out, flow_out_sems, INNER_STORES)
    order_writes = plane_copies(order_out, order_hbm_out, order_out_sems, INNER_STORES)
    for part, (first, count) in enumerate(INNER_LOADS):
        flow_copies[part].wait()
        lax.fori_loop(max(first, INNER[0]), min(first + count, INNER[1]), step, 0)
        if part > 0:
            flow_writes[part - 1].start()
            order_writes[part - 1].start()
    flow_writes[-1].start()
    order_writes[-1].start()
    for copy in flow_writes + order_writes:
        copy.wait()


def outer_kernel(
    offset_ref, flow_hbm, order_hbm, phase_ref, low_ref, high_ref, minus_ref, same_ref, plus_ref, odd_ref,
    flow_part, order_part, flow_hbm_out, order_hbm_out,
    flow_ref, order_ref, flow_out, order_out,
    below_ref, above_ref, wide_ref, ghost_ref, potential_ref, low_side, high_side, edge_ref,
    flow_sems, order_sems, flow_part_sems, order_part_sems, flow_out_sems, order_out_sems,
):
    loads = plane_copies(order_hbm, order_ref, order_sems, OUTER_LOADS)
    loads += plane_copies(flow_hbm, flow_ref, flow_sems, OUTER_LOADS)
    loads += plane_copies(flow_part, flow_out, flow_part_sems, OUTER_PARTS)
    loads += plane_copies(order_part, order_out, order_part_sems, OUTER_PARTS)
    for copy in loads:
        copy.start()

    slab = lax.axis_index("gx")
    is_even = slab % 2 == 0
    inner = lax.rem(offset_ref[even_boundary(slab)] + 5, ROWS)
    blocks = [
        lambda at: jnp.where(is_even, minus_ref[at], plus_ref[at]),
        lambda at: same_ref[at],
        lambda at: jnp.where(is_even, plus_ref[at], minus_ref[at]),
    ]
    cut_window(blocks, jnp.where(is_even, inner, 9 - inner), above_ref)
    for index in range(PAYLOAD):
        even, odd = above_ref[index], odd_ref[index]
        below_ref[index] = jnp.where(is_even, odd, even)
        above_ref[index] = jnp.where(is_even, even, odd)

    for index, plane in enumerate((0, 1, PLANES - 1, PLANES - 2)):
        wide_ref[index] = jnp.zeros((WINDOW, LANES), jnp.float32)
        for d in range(3):
            wide_ref[index, 3 - d : 4 - d, :] = side_row(low_ref, AT_PHASE + d, plane)
            wide_ref[index, 12 + d : 13 + d, :] = side_row(high_ref, AT_PHASE + d, plane)
        wide_ref[index, 4:12, :] = phase_ref[plane]
    below = ghost_plane(below_ref, UP_X, wide_ref[0], wide_ref[1], 1.0 - SHIFT_FRACTION, WALL_SPEED)
    above = ghost_plane(above_ref, DOWN_X, wide_ref[2], wide_ref[3], SHIFT_FRACTION, -WALL_SPEED)
    for index in range(5):
        ghost_ref[index] = below[3][index]
        ghost_ref[5 + index] = below[4][index]
        ghost_ref[10 + index] = above[3][index]
        ghost_ref[15 + index] = above[4][index]

    def ghost_row(ghost):
        return lambda which, own_row: ghost[2 * which][own_row + WINDOW_PAD : own_row + WINDOW_PAD + 1, :]

    collide_sides(
        phase_ref, low_ref, high_ref, ghost_row(below), ghost_row(above), low_side, high_side, edge_ref
    )
    wide_ref[0] = below[1]
    wide_ref[1] = below[2]
    wide_ref[2] = above[1]
    wide_ref[3] = above[2]
    potential_ref[1] = wide_ref[0, 4:12, :]
    potential_ref[0] = wide_ref[1, 4:12, :]
    potential_ref[PLANES] = wide_ref[2, 4:12, :]
    potential_ref[PLANES + 1] = wide_ref[3, 4:12, :]
    for x in (1, 2, PLANES - 3, PLANES - 2):
        potential_ref[x + 1] = plane_potential(phase_ref, low_ref, high_ref, x)
    for copy in loads:
        copy.wait()
    for comps, first, target in ((UP_X, 0, 0), (DOWN_X, 10, PLANES - 1)):
        for index, i in enumerate(comps):
            start = WINDOW_PAD - VELOCITY_Y[i]
            for out_ref, at in ((flow_out, first + index), (order_out, first + 5 + index)):
                cells = ghost_ref[at, start : start + ROWS, :]
                if VELOCITY_Z[i] != 0:
                    cells = roll_lanes(cells, VELOCITY_Z[i])
                out_ref[i, target] = cells
    flow_writes = plane_copies(flow_out, flow_hbm_out, flow_out_sems, OUTER_STORES)
    order_writes = plane_copies(order_out, order_hbm_out, order_out_sems, OUTER_STORES)
    for end, planes in enumerate((((0, -1), (1, 0)), ((PLANES - 2, 0), (PLANES - 1, 1)))):
        for x, skip in planes:
            collide_plane(
                x, skip, flow_ref, order_ref, phase_ref, potential_ref, edge_ref, low_side, high_side, flow_out, order_out
            )
        flow_writes[end].start()
        order_writes[end].start()
    for copy in flow_writes + order_writes:
        copy.wait()


def vmem(count):
    return [pl.BlockSpec(memory_space=pltpu.VMEM)] * count


def params(limit=VMEM_LIMIT):
    return pltpu.CompilerParams(vmem_limit_bytes=limit)


def f32(*shape):
    return jax.ShapeDtypeStruct(shape, jnp.float32)


def shift_pairs(count, step):
    return [(i, (i + step) % count) for i in range(count)]


def swap_pairs(slabs, strips, first, step):
    pairs = []
    for low in range(first, slabs, 2):
        high = (low + 1) % slabs
        for strip in range(strips):
            other = (strip + step) % strips
            pairs.append((low * strips + strip, high * strips + other))
            pairs.append((high * strips + other, low * strips + strip))
    return pairs


def hbm(count):
    return [pl.BlockSpec(memory_space=pltpu.HBM)] * count


def smem():
    return [pl.BlockSpec(memory_space=pltpu.SMEM)]


def scratch(*shape):
    return pltpu.VMEM(shape, jnp.float32)


def sems(count):
    return pltpu.SemaphoreType.DMA((count,))


def inner_planes(populations, order_pops, from_low, from_high):
    return pl.pallas_call(
        inner_kernel,
        out_shape=(f32(PLANES, ROWS, LANES), f32(*populations.shape), f32(*order_pops.shape)),
        in_specs=hbm(4),
        out_specs=tuple(vmem(1) + hbm(2)),
        scratch_shapes=[
            scratch(*populations.shape),
            scratch(*order_pops.shape),
            scratch(PACKED, LANES),
            scratch(PACKED, LANES),
            scratch(*populations.shape),
            scratch(*order_pops.shape),
            scratch(PLANES + 2, ROWS, LANES),
            scratch(10, PLANES, LANES),
            scratch(10, PLANES, LANES),
            scratch(2, PLANES, LANES),
            sems(len(INNER_LOADS)),
            sems(1),
            sems(2),
            sems(len(INNER_STORES)),
            sems(len(INNER_STORES)),
        ],
        compiler_params=params(),
        name="inner_planes",
    )(populations, order_pops, from_low, from_high)


def odd_window(plane_offsets, from_low, own, from_high):
    return pl.pallas_call(
        window_kernel,
        out_shape=f32(PAYLOAD, WINDOW, LANES),
        in_specs=smem() + vmem(3),
        out_specs=vmem(1)[0],
        compiler_params=params(SMALL_VMEM),
        name="window",
    )(plane_offsets, from_low, own, from_high)


def outer_planes(odd, plane_offsets, populations, order_pops, phase, from_low, from_high, blocks, flow_part, order_part):
    return pl.pallas_call(
        outer_kernel,
        out_shape=(f32(*populations.shape), f32(*order_pops.shape)),
        in_specs=smem() + hbm(2) + vmem(7) + hbm(2),
        out_specs=tuple(hbm(2)),
        input_output_aliases={10: 0, 11: 1},
        scratch_shapes=[
            scratch(*populations.shape),
            scratch(*order_pops.shape),
            scratch(*populations.shape),
            scratch(*order_pops.shape),
            scratch(PAYLOAD, WINDOW, LANES),
            scratch(PAYLOAD, WINDOW, LANES),
            scratch(4, WINDOW, LANES),
            scratch(20, WINDOW, LANES),
            scratch(PLANES + 2, ROWS, LANES),
            scratch(10, PLANES, LANES),
            scratch(10, PLANES, LANES),
            scratch(2, PLANES, LANES),
            sems(2),
            sems(2),
            sems(2),
            sems(2),
            sems(2),
            sems(2),
        ],
        compiler_params=params(SMALL_VMEM),
        name="outer_planes",
    )(plane_offsets, populations, order_pops, phase, from_low, from_high, *blocks, odd, flow_part, order_part)


def shards(populations, order_pops, plane_offsets):
    slabs, strips = lax.axis_size("gx"), lax.axis_size("gy")
    even_step, odd_step, even, own_odd, to_low, to_high = pl.pallas_call(
        payload_kernel,
        out_shape=(
            jax.ShapeDtypeStruct((1,), jnp.int32),
            jax.ShapeDtypeStruct((1,), jnp.int32),
            f32(PAYLOAD, ROWS, LANES),
            f32(PAYLOAD, ROWS, LANES),
            f32(PACKED, LANES),
            f32(PACKED, LANES),
        ),
        in_specs=smem() + hbm(2),
        out_specs=tuple(smem() * 2 + vmem(4)),
        scratch_shapes=[
            scratch(*populations.shape),
            scratch(*order_pops.shape),
            scratch(PLANES, ROWS, LANES),
            sems(len(FLOW_PIECES)),
            sems(len(ORDER_PIECES)),
        ],
        compiler_params=params(),
        name="payloads",
    )(plane_offsets, populations, order_pops)

    def even_branch(step):
        def run(offsets, flow, order, mine, own, low, high):
            from_low = lax.ppermute(high, "gy", shift_pairs(strips, 1))
            from_high = lax.ppermute(low, "gy", shift_pairs(strips, -1))
            blocks = tuple(
                lax.ppermute(mine, ("gx", "gy"), swap_pairs(slabs, strips, 0, step + d)) for d in (-1, 0, 1)
            )
            window = odd_window(offsets, from_low, own, from_high)
            return from_low, from_high, blocks, window, *inner_planes(flow, order, from_low, from_high)

        return run

    from_low, from_high, blocks, window, phase, flow_part, order_part = lax.switch(
        even_step.reshape(()),
        [even_branch(step) for step in range(strips)],
        plane_offsets, populations, order_pops, even, own_odd, to_low, to_high,
    )

    def odd_branch(step):
        def run(mine, *others):
            odd = lax.ppermute(mine, ("gx", "gy"), swap_pairs(slabs, strips, 1, step))
            return outer_planes(odd, *others)

        return run

    return lax.switch(
        odd_step.reshape(()),
        [odd_branch(step) for step in range(strips)],
        window, plane_offsets, populations, order_pops, phase, from_low, from_high, blocks, flow_part, order_part,
    )


def solution(mesh):
    return jax.shard_map(
        shards,
        mesh=mesh,
        in_specs=(P(None, "gx", "gy", None), P(None, "gx", "gy", None), P()),
        out_specs=(P(None, "gx", "gy", None), P(None, "gx", "gy", None)),
        check_vma=False,
    )
```

```python
import jax
import jax.numpy as jnp
from jax import lax
from jax.experimental import pallas as pl
from jax.experimental.pallas import tpu as pltpu
from jax.sharding import PartitionSpec as P

SHIFT_FRACTION = 0.375
WALL_SPEED = 0.05
RELAX_FLOW = 0.8
RELAX_ORDER = 0.9
BULK_COEFF = 0.05
SURFACE_COEFF = 0.04
MOBILITY = 1.0
VELOCITY_X = (0, 1, -1, 0, 0, 0, 0, 1, -1, 1, -1, 1, -1, 1, -1, 0, 0, 0, 0)
VELOCITY_Y = (0, 0, 0, 1, -1, 0, 0, 1, -1, -1, 1, 0, 0, 0, 0, 1, -1, 1, -1)
VELOCITY_Z = (0, 0, 0, 0, 0, 1, -1, 0, 0, 0, 0, 1, -1, -1, 1, 1, -1, -1, 1)
WEIGHT_TABLE = (1.0 / 3.0,) + (1.0 / 18.0,) * 6 + (1.0 / 36.0,) * 12

VELS = 19
PLANES = 16
ROWS = 8
LANES = 128
UP_X = tuple(i for i in range(VELS) if VELOCITY_X[i] == 1)
DOWN_X = tuple(i for i in range(VELS) if VELOCITY_X[i] == -1)
UP_Y = tuple(i for i in range(VELS) if VELOCITY_Y[i] == 1)
DOWN_Y = tuple(i for i in range(VELS) if VELOCITY_Y[i] == -1)
PAYLOAD = 17
AT_MOMENTS = 5
AT_ORDER = 9
AT_PHASE = 14
WINDOW = 16
WINDOW_PAD = 4

VMEM_LIMIT = 61500000
SMALL_VMEM = 16 * 1024 * 1024


def roll_rows(cells, step):
    return pltpu.roll(cells, step % cells.shape[0], 0)


def roll_lanes(cells, step):
    return pltpu.roll(cells, step % LANES, cells.ndim - 1)


def moments(flow):
    parts = [flow(i) for i in range(VELS)]
    density = parts[0]
    for part in parts[1:]:
        density = density + part
    speeds = []
    for table in (VELOCITY_X, VELOCITY_Y, VELOCITY_Z):
        plus = [parts[i] for i in range(VELS) if table[i] == 1]
        minus = [parts[i] for i in range(VELS) if table[i] == -1]
        total = plus[0] - minus[0]
        for a, b in zip(plus[1:], minus[1:]):
            total = total + (a - b)
        speeds.append(total)
    return density, speeds


def potential_of(phase, neighbours):
    around = neighbours[0]
    for cells in neighbours[1:]:
        around = around + cells
    bulk = BULK_COEFF * (phase * phase * phase - phase)
    return bulk - SURFACE_COEFF * (around - 6.0 * phase)


def dot_velocity(i, vector):
    total = None
    for sign, part in zip((VELOCITY_X[i], VELOCITY_Y[i], VELOCITY_Z[i]), vector):
        if sign == 0:
            continue
        if total is None:
            total = part if sign == 1 else -part
        else:
            total = total + part if sign == 1 else total - part
    return total


def collide(wanted, flow, order, density, momentum, phase, potential, force):
    inverse = 1.0 / density
    speed = [(momentum[d] + 0.5 * force[d]) * inverse for d in range(3)]
    source = 1.0 - 0.5 / RELAX_FLOW
    relaxed = density * (1.0 / RELAX_FLOW)
    speed_sq = speed[0] * speed[0] + speed[1] * speed[1] + speed[2] * speed[2]
    work = speed[0] * force[0] + speed[1] * force[1] + speed[2] * force[2]
    even = relaxed * (1.0 - 1.5 * speed_sq) - (3.0 * source) * work
    odd = [3.0 * (relaxed * speed[d] + source * force[d]) for d in range(3)]
    quad = [4.5 * relaxed * speed[d] + (9.0 * source) * force[d] for d in range(3)]
    order_even = (3.0 * MOBILITY / RELAX_ORDER) * potential
    carried = (3.0 / RELAX_ORDER) * phase
    order_odd = [carried * speed[d] for d in range(3)]
    flow_out, order_out = {}, {}
    keep_flow = 1.0 - 1.0 / RELAX_FLOW
    keep_order = 1.0 - 1.0 / RELAX_ORDER
    done = set()
    for i in wanted:
        if i in done:
            continue
        weight = WEIGHT_TABLE[i]
        if i == 0:
            flow_out[0] = keep_flow * flow(0) + weight * even
            rest = phase - (2.0 * MOBILITY) * potential
            order_out[0] = keep_order * order(0) + (1.0 / RELAX_ORDER) * rest
            continue
        first = i if i % 2 == 1 else i - 1
        pair_even = weight * (even + dot_velocity(first, speed) * dot_velocity(first, quad))
        pair_odd = weight * dot_velocity(first, odd)
        pair_order = weight * dot_velocity(first, order_odd)
        for member, sign in ((first, 1), (first + 1, -1)):
            if member not in wanted:
                continue
            done.add(member)
            both = pair_even + pair_odd if sign == 1 else pair_even - pair_odd
            flow_out[member] = keep_flow * flow(member) + both
            both = weight * order_even
            both = both + pair_order if sign == 1 else both - pair_order
            order_out[member] = keep_order * order(member) + both
    return flow_out, order_out


def add_phase(phase_ref, order_ref, x):
    total = order_ref[0, x]
    for i in range(1, VELS):
        total = total + order_ref[i, x]
    phase_ref[x] = total


def plane_copies(source, target, sems, pieces):
    return [
        pltpu.make_async_copy(source.at[:, pl.ds(first, count)], target.at[:, pl.ds(first, count)], sems.at[index])
        for index, (first, count) in enumerate(pieces)
    ]


FLOW_PIECES = ((0, 1), (PLANES - 1, 1), (1, 4), (5, 5), (10, 5))
ORDER_PIECES = ((0, 3), (PLANES - 3, 3), (3, 5), (8, 5))
INNER = (2, PLANES - 2)
INNER_LOADS = ((1, 4), (5, 4), (9, 3), (12, 3))
INNER_STORES = ((1, 4), (5, 4), (9, 3), (12, 3))
OUTER_LOADS = ((0, 2), (PLANES - 2, 2))
OUTER_PARTS = ((1, 2), (PLANES - 3, 2))
OUTER_STORES = ((0, 3), (PLANES - 3, 3))
PACKED = PAYLOAD * (ROWS + PLANES)


def even_boundary(slab):
    return slab + 1 - slab % 2


def odd_boundary(slab, slabs):
    return lax.rem(slab + slab % 2, slabs)


def side_rows(index):
    return pl.ds(PAYLOAD * ROWS + index * PLANES, PLANES)


def side_row(ref, index, x):
    return ref[pl.ds(PAYLOAD * ROWS + index * PLANES + x, 1), :]


def payload_kernel(
    offset_ref, flow_hbm, order_hbm, even_step, odd_step, even_ref, odd_ref, low_ref, high_ref,
    flow_ref, order_ref, phase_ref, flow_sems, order_sems,
):
    flow_copies = plane_copies(flow_hbm, flow_ref, flow_sems, FLOW_PIECES)
    order_copies = plane_copies(order_hbm, order_ref, order_sems, ORDER_PIECES)
    for copy in flow_copies[:2] + order_copies[:2] + order_copies[2:] + flow_copies[2:]:
        copy.start()
    slab = lax.axis_index("gx")
    is_even = slab % 2 == 0
    strips = lax.axis_size("gy")
    even_step[0] = lax.rem((offset_ref[even_boundary(slab)] + 5) // ROWS, strips)
    odd_step[0] = lax.rem((offset_ref[odd_boundary(slab, offset_ref.shape[0])] + 5) // ROWS, strips)

    for copy in flow_copies[:2] + order_copies[:2]:
        copy.wait()
    for x in (0, 1, 2, PLANES - 3, PLANES - 2, PLANES - 1):
        add_phase(phase_ref, order_ref, x)
    sides = []
    for plane, inward, comps in ((PLANES - 1, -1, UP_X), (0, 1, DOWN_X)):
        density, momentum = moments(lambda i: flow_ref[i, plane])
        parts = [flow_ref[i, plane] for i in comps] + [density] + momentum
        parts += [order_ref[i, plane] for i in comps]
        parts += [phase_ref[plane + inward * d] for d in range(3)]
        sides.append(parts)
    for index, (last, first) in enumerate(zip(*sides)):
        even_ref[index] = jnp.where(is_even, last, first)
        odd = jnp.where(is_even, first, last)
        odd_ref[index] = odd
        low_ref[index * ROWS : (index + 1) * ROWS, :] = odd
        high_ref[index * ROWS : (index + 1) * ROWS, :] = odd
    for copy in order_copies[2:]:
        copy.wait()
    for x in range(3, PLANES - 3):
        add_phase(phase_ref, order_ref, x)
    for copy in flow_copies[2:]:
        copy.wait()
    for out_ref, row, inward, comps in ((high_ref, ROWS - 1, -1, UP_Y), (low_ref, 0, 1, DOWN_Y)):
        density, momentum = moments(lambda i: flow_ref[i, :, row, :])
        parts = [flow_ref[i, :, row, :] for i in comps] + [density] + momentum
        parts += [order_ref[i, :, row, :] for i in comps]
        parts += [phase_ref[:, row + inward * d, :] for d in range(3)]
        for index, part in enumerate(parts):
            out_ref[side_rows(index), :] = part


def window_kernel(offset_ref, before_ref, own_ref, after_ref, out_ref):
    slab = lax.axis_index("gx")
    inner = lax.rem(offset_ref[odd_boundary(slab, offset_ref.shape[0])] + 5, ROWS)

    def block(ref):
        return lambda index: ref[index * ROWS : (index + 1) * ROWS, :]

    blocks = [block(before_ref), lambda index: own_ref[index], block(after_ref)]
    cut_window(blocks, jnp.where(slab % 2 == 0, inner, 9 - inner), out_ref)


def cut_window(blocks, start, window_ref):
    row = lax.broadcasted_iota(jnp.int32, (ROWS, LANES), 0)
    inner = lax.rem(start, ROWS)
    back = lax.rem(ROWS - inner, ROWS)
    early = row < ROWS - inner
    near = start < ROWS
    for index in range(PAYLOAD):
        rolled = [pltpu.roll(block(index), back, 0) for block in blocks]
        first = jnp.where(near, rolled[0], rolled[1])
        second = jnp.where(near, rolled[1], rolled[2])
        window_ref[index, 0:ROWS] = jnp.where(early, first, second)
        window_ref[index, ROWS : 2 * ROWS] = jnp.where(early, second, rolled[2])


def ghost_plane(window_ref, comps, own, own_next, weight, kick_speed):
    other = 1.0 - weight

    def sheared(cells):
        return weight * cells + other * roll_rows(cells, 1)

    def seen(cells):
        return other * roll_rows(cells, -1) + weight * cells

    def sides(cells):
        return [roll_rows(cells, 1), roll_rows(cells, -1), roll_lanes(cells, 1), roll_lanes(cells, -1)]

    near, second, third = [window_ref[AT_PHASE + d] for d in range(3)]
    ghost_phase = sheared(near)
    own_potential = potential_of(own, [own_next, ghost_phase] + sides(own))
    near_potential = potential_of(near, [second, seen(own)] + sides(near))
    second_potential = potential_of(second, [third, near] + sides(second))
    beyond = seen(own_potential)
    outward = 1.0 if VELOCITY_X[comps[0]] == 1 else -1.0
    half = -0.5 * near
    force = [
        outward * half * (beyond - second_potential),
        half * (roll_rows(near_potential, -1) - roll_rows(near_potential, 1)),
        half * (roll_lanes(near_potential, -1) - roll_lanes(near_potential, 1)),
    ]
    density = window_ref[AT_MOMENTS]
    momentum = [window_ref[AT_MOMENTS + 1 + d] for d in range(3)]
    flow_out, order_out = collide(
        comps,
        lambda i: window_ref[comps.index(i)],
        lambda i: window_ref[AT_ORDER + comps.index(i)],
        density,
        momentum,
        near,
        near_potential,
        force,
    )
    flow_ghost = []
    for i in comps:
        cells = flow_out[i]
        if VELOCITY_Y[i] != 0:
            cells = cells + (WEIGHT_TABLE[i] * 3.0 * VELOCITY_Y[i] * kick_speed) * density
        flow_ghost.append(sheared(cells))
    order_ghost = [sheared(order_out[i]) for i in comps]
    return ghost_phase, own_potential, sheared(near_potential), flow_ghost, order_ghost


def rows_before(cells, line):
    row = lax.broadcasted_iota(jnp.int32, (ROWS, LANES), 0)
    return jnp.where(row == 0, line, roll_rows(cells, 1))


def rows_after(cells, line):
    row = lax.broadcasted_iota(jnp.int32, (ROWS, LANES), 0)
    return jnp.where(row == ROWS - 1, line, roll_rows(cells, -1))


def collide_sides(phase_ref, low_ref, high_ref, below, above, low_side, high_side, edge_ref):
    plane_at = lax.broadcasted_iota(jnp.int32, (PLANES, LANES), 0)

    def across(cells, which, own_row):
        before, after = roll_rows(cells, 1), roll_rows(cells, -1)
        if below is not None:
            before = jnp.where(plane_at == 0, below(which, own_row), before)
            after = jnp.where(plane_at == PLANES - 1, above(which, own_row), after)
        return before, after

    for side_ref, out_ref, edge, beside, inward, comps in (
        (low_ref, low_side, 0, -1, 1, UP_Y),
        (high_ref, high_side, ROWS - 1, ROWS, -1, DOWN_Y),
    ):
        own = [phase_ref[:, edge + inward * d, :] for d in range(2)]
        outer = [side_ref[side_rows(AT_PHASE + d), :] for d in range(3)]
        lines = [own[1], own[0]] + outer
        potentials = []
        for index in range(1, 4):
            cells = lines[index]
            around = list(across(cells, 0, edge + inward * (1 - index)))
            around += [lines[index - 1], lines[index + 1], roll_lanes(cells, 1), roll_lanes(cells, -1)]
            potentials.append(potential_of(cells, around))
        inside, here, outside = potentials
        before, after = across(here, 1, beside)
        half = -0.5 * outer[0]
        force = [
            half * (after - before),
            (inward * half) * (inside - outside),
            half * (roll_lanes(here, -1) - roll_lanes(here, 1)),
        ]
        flow_post, order_post = collide(
            comps,
            lambda i: side_ref[side_rows(comps.index(i)), :],
            lambda i: side_ref[side_rows(AT_ORDER + comps.index(i)), :],
            side_ref[side_rows(AT_MOMENTS), :],
            [side_ref[side_rows(AT_MOMENTS + 1 + d), :] for d in range(3)],
            outer[0],
            here,
            force,
        )
        for index, i in enumerate(comps):
            out_ref[index] = flow_post[i]
            out_ref[5 + index] = order_post[i]
        edge_ref[0 if inward == 1 else 1] = here


def plane_potential(phase_ref, low_ref, high_ref, x):
    cells = phase_ref[x]
    around = [
        phase_ref[x - 1],
        phase_ref[x + 1],
        rows_before(cells, side_row(low_ref, AT_PHASE, x)),
        rows_after(cells, side_row(high_ref, AT_PHASE, x)),
        roll_lanes(cells, 1),
        roll_lanes(cells, -1),
    ]
    return potential_of(cells, around)


def collide_plane(x, skip, flow_ref, order_ref, phase_ref, potential_ref, edge_ref, low_side, high_side, flow_out, order_out):
    here = potential_ref[x + 1]
    phase = phase_ref[x]
    half = -0.5 * phase
    along_y = rows_after(here, edge_ref[1, pl.ds(x, 1), :]) - rows_before(here, edge_ref[0, pl.ds(x, 1), :])
    force = [
        half * (potential_ref[x + 2] - potential_ref[x]),
        half * along_y,
        half * (roll_lanes(here, -1) - roll_lanes(here, 1)),
    ]
    density, momentum = moments(lambda i: flow_ref[i, x])
    flow_post, order_post = collide(
        tuple(i for i in range(VELS) if VELOCITY_X[i] == 0 or VELOCITY_X[i] != skip),
        lambda i: flow_ref[i, x],
        lambda i: order_ref[i, x],
        density,
        momentum,
        phase,
        here,
        force,
    )

    def moved(i, cells, first):
        if VELOCITY_Y[i] == 1:
            cells = rows_before(cells, low_side[first + UP_Y.index(i), pl.ds(x, 1), :])
        elif VELOCITY_Y[i] == -1:
            cells = rows_after(cells, high_side[first + DOWN_Y.index(i), pl.ds(x, 1), :])
        if VELOCITY_Z[i] != 0:
            cells = roll_lanes(cells, VELOCITY_Z[i])
        return cells

    for i in flow_post:
        target = x + VELOCITY_X[i]
        flow_out[i, target] = moved(i, flow_post[i], 0)
        order_out[i, target] = moved(i, order_post[i], 5)


def inner_kernel(
    flow_hbm, order_hbm, low_hbm, high_hbm, phase_ref, flow_hbm_out, order_hbm_out,
    flow_ref, order_ref, low_ref, high_ref, flow_out, order_out, potential_ref, low_side, high_side, edge_ref,
    flow_sems, order_sems, side_sems, flow_out_sems, order_out_sems,
):
    whole_order = pltpu.make_async_copy(order_hbm, order_ref, order_sems.at[0])
    sides = [
        pltpu.make_async_copy(low_hbm, low_ref, side_sems.at[0]),
        pltpu.make_async_copy(high_hbm, high_ref, side_sems.at[1]),
    ]
    flow_copies = plane_copies(flow_hbm, flow_ref, flow_sems, INNER_LOADS)
    for copy in [whole_order] + sides + flow_copies:
        copy.start()
    whole_order.wait()

    def phase_step(x, carry):
        add_phase(phase_ref, order_ref, x)
        return carry

    lax.fori_loop(0, PLANES, phase_step, 0)
    for copy in sides:
        copy.wait()
    collide_sides(phase_ref, low_ref, high_ref, None, None, low_side, high_side, edge_ref)

    def potential_step(x, carry):
        potential_ref[x + 1] = plane_potential(phase_ref, low_ref, high_ref, x)
        return carry

    lax.fori_loop(1, PLANES - 1, potential_step, 0)
    flow_writes = plane_copies(flow_out, flow_hbm_out, flow_out_sems, INNER_STORES)
    order_writes = plane_copies(order_out, order_hbm_out, order_out_sems, INNER_STORES)

    def step(x, carry):
        for part, (first, _) in enumerate(INNER_LOADS):

            @pl.when(x == max(first, INNER[0]))
            def _(part=part):
                flow_copies[part].wait()

        collide_plane(
            x, 0, flow_ref, order_ref, phase_ref, potential_ref, edge_ref, low_side, high_side, flow_out, order_out
        )
        for part, (first, count) in enumerate(INNER_LOADS):
            if part > 0:

                @pl.when(x == min(first + count, INNER[1]) - 1)
                def _(part=part):
                    flow_writes[part - 1].start()
                    order_writes[part - 1].start()

        return carry

    lax.fori_loop(INNER[0], INNER[1], step, 0)
    flow_writes[-1].start()
    order_writes[-1].start()
    for copy in flow_writes + order_writes:
        copy.wait()


def outer_kernel(
    offset_ref, flow_hbm, order_hbm, phase_hbm, low_hbm, high_hbm, minus_hbm, same_hbm, plus_hbm, odd_hbm,
    flow_part, order_part, flow_hbm_out, order_hbm_out,
    flow_ref, order_ref, flow_out, order_out, phase_ref, low_ref, high_ref, minus_ref, same_ref, plus_ref, odd_ref,
    below_ref, above_ref, wide_ref, ghost_ref, potential_ref, low_side, high_side, edge_ref,
    small_sems, flow_sems, order_sems, flow_part_sems, order_part_sems, flow_out_sems, order_out_sems,
):
    pairs = (
        (minus_hbm, minus_ref), (same_hbm, same_ref), (plus_hbm, plus_ref), (odd_hbm, odd_ref),
        (phase_hbm, phase_ref), (low_hbm, low_ref), (high_hbm, high_ref),
    )
    small = [pltpu.make_async_copy(a, b, small_sems.at[index]) for index, (a, b) in enumerate(pairs)]
    for copy in small:
        copy.start()
    loads = plane_copies(order_hbm, order_ref, order_sems, OUTER_LOADS)
    loads += plane_copies(flow_hbm, flow_ref, flow_sems, OUTER_LOADS)
    loads += plane_copies(flow_part, flow_out, flow_part_sems, OUTER_PARTS)
    loads += plane_copies(order_part, order_out, order_part_sems, OUTER_PARTS)
    for copy in loads:
        copy.start()

    slab = lax.axis_index("gx")
    is_even = slab % 2 == 0
    inner = lax.rem(offset_ref[even_boundary(slab)] + 5, ROWS)
    for copy in small:
        copy.wait()
    blocks = [
        lambda at: jnp.where(is_even, minus_ref[at], plus_ref[at]),
        lambda at: same_ref[at],
        lambda at: jnp.where(is_even, plus_ref[at], minus_ref[at]),
    ]
    cut_window(blocks, jnp.where(is_even, inner, 9 - inner), above_ref)
    for index in range(PAYLOAD):
        even, odd = above_ref[index], odd_ref[index]
        below_ref[index] = jnp.where(is_even, odd, even)
        above_ref[index] = jnp.where(is_even, even, odd)

    for index, plane in enumerate((0, 1, PLANES - 1, PLANES - 2)):
        wide_ref[index] = jnp.zeros((WINDOW, LANES), jnp.float32)
        for d in range(3):
            wide_ref[index, 3 - d : 4 - d, :] = side_row(low_ref, AT_PHASE + d, plane)
            wide_ref[index, 12 + d : 13 + d, :] = side_row(high_ref, AT_PHASE + d, plane)
        wide_ref[index, 4:12, :] = phase_ref[plane]
    below = ghost_plane(below_ref, UP_X, wide_ref[0], wide_ref[1], 1.0 - SHIFT_FRACTION, WALL_SPEED)
    above = ghost_plane(above_ref, DOWN_X, wide_ref[2], wide_ref[3], SHIFT_FRACTION, -WALL_SPEED)
    for index in range(5):
        ghost_ref[index] = below[3][index]
        ghost_ref[5 + index] = below[4][index]
        ghost_ref[10 + index] = above[3][index]
        ghost_ref[15 + index] = above[4][index]

    def ghost_row(ghost):
        return lambda which, own_row: ghost[2 * which][own_row + WINDOW_PAD : own_row + WINDOW_PAD + 1, :]

    collide_sides(
        phase_ref, low_ref, high_ref, ghost_row(below), ghost_row(above), low_side, high_side, edge_ref
    )
    wide_ref[0] = below[1]
    wide_ref[1] = below[2]
    wide_ref[2] = above[1]
    wide_ref[3] = above[2]
    potential_ref[1] = wide_ref[0, 4:12, :]
    potential_ref[0] = wide_ref[1, 4:12, :]
    potential_ref[PLANES] = wide_ref[2, 4:12, :]
    potential_ref[PLANES + 1] = wide_ref[3, 4:12, :]
    for x in (1, 2, PLANES - 3, PLANES - 2):
        potential_ref[x + 1] = plane_potential(phase_ref, low_ref, high_ref, x)
    for copy in loads:
        copy.wait()
    for comps, first, target in ((UP_X, 0, 0), (DOWN_X, 10, PLANES - 1)):
        for index, i in enumerate(comps):
            start = WINDOW_PAD - VELOCITY_Y[i]
            for out_ref, at in ((flow_out, first + index), (order_out, first + 5 + index)):
                cells = ghost_ref[at, start : start + ROWS, :]
                if VELOCITY_Z[i] != 0:
                    cells = roll_lanes(cells, VELOCITY_Z[i])
                out_ref[i, target] = cells
    flow_writes = plane_copies(flow_out, flow_hbm_out, flow_out_sems, OUTER_STORES)
    order_writes = plane_copies(order_out, order_hbm_out, order_out_sems, OUTER_STORES)
    for end, planes in enumerate((((0, -1), (1, 0)), ((PLANES - 2, 0), (PLANES - 1, 1)))):
        for x, skip in planes:
            collide_plane(
                x, skip, flow_ref, order_ref, phase_ref, potential_ref, edge_ref, low_side, high_side, flow_out, order_out
            )
        flow_writes[end].start()
        order_writes[end].start()
    for copy in flow_writes + order_writes:
        copy.wait()


def vmem(count):
    return [pl.BlockSpec(memory_space=pltpu.VMEM)] * count


def params(limit=VMEM_LIMIT):
    return pltpu.CompilerParams(vmem_limit_bytes=limit)


def f32(*shape):
    return jax.ShapeDtypeStruct(shape, jnp.float32)


def shift_pairs(count, step):
    return [(i, (i + step) % count) for i in range(count)]


def swap_pairs(slabs, strips, first, step):
    pairs = []
    for low in range(first, slabs, 2):
        high = (low + 1) % slabs
        for strip in range(strips):
            other = (strip + step) % strips
            pairs.append((low * strips + strip, high * strips + other))
            pairs.append((high * strips + other, low * strips + strip))
    return pairs


def hbm(count):
    return [pl.BlockSpec(memory_space=pltpu.HBM)] * count


def smem():
    return [pl.BlockSpec(memory_space=pltpu.SMEM)]


def scratch(*shape):
    return pltpu.VMEM(shape, jnp.float32)


def sems(count):
    return pltpu.SemaphoreType.DMA((count,))


def inner_planes(populations, order_pops, from_low, from_high):
    return pl.pallas_call(
        inner_kernel,
        out_shape=(f32(PLANES, ROWS, LANES), f32(*populations.shape), f32(*order_pops.shape)),
        in_specs=hbm(4),
        out_specs=tuple(vmem(1) + hbm(2)),
        scratch_shapes=[
            scratch(*populations.shape),
            scratch(*order_pops.shape),
            scratch(PACKED, LANES),
            scratch(PACKED, LANES),
            scratch(*populations.shape),
            scratch(*order_pops.shape),
            scratch(PLANES + 2, ROWS, LANES),
            scratch(10, PLANES, LANES),
            scratch(10, PLANES, LANES),
            scratch(2, PLANES, LANES),
            sems(len(INNER_LOADS)),
            sems(1),
            sems(2),
            sems(len(INNER_STORES)),
            sems(len(INNER_STORES)),
        ],
        compiler_params=params(),
        name="inner_planes",
    )(populations, order_pops, from_low, from_high)


def odd_window(plane_offsets, from_low, own, from_high):
    return pl.pallas_call(
        window_kernel,
        out_shape=f32(PAYLOAD, WINDOW, LANES),
        in_specs=smem() + vmem(3),
        out_specs=vmem(1)[0],
        compiler_params=params(SMALL_VMEM),
        name="window",
    )(plane_offsets, from_low, own, from_high)


def outer_planes(odd, plane_offsets, populations, order_pops, phase, from_low, from_high, blocks, flow_part, order_part):
    return pl.pallas_call(
        outer_kernel,
        out_shape=(f32(*populations.shape), f32(*order_pops.shape)),
        in_specs=smem() + hbm(11),
        out_specs=tuple(hbm(2)),
        input_output_aliases={10: 0, 11: 1},
        scratch_shapes=[
            scratch(*populations.shape),
            scratch(*order_pops.shape),
            scratch(*populations.shape),
            scratch(*order_pops.shape),
            scratch(PLANES, ROWS, LANES),
            scratch(PACKED, LANES),
            scratch(PACKED, LANES),
            scratch(PAYLOAD, ROWS, LANES),
            scratch(PAYLOAD, ROWS, LANES),
            scratch(PAYLOAD, ROWS, LANES),
            scratch(PAYLOAD, WINDOW, LANES),
            scratch(PAYLOAD, WINDOW, LANES),
            scratch(PAYLOAD, WINDOW, LANES),
            scratch(4, WINDOW, LANES),
            scratch(20, WINDOW, LANES),
            scratch(PLANES + 2, ROWS, LANES),
            scratch(10, PLANES, LANES),
            scratch(10, PLANES, LANES),
            scratch(2, PLANES, LANES),
            sems(7),
            sems(2),
            sems(2),
            sems(2),
            sems(2),
            sems(2),
            sems(2),
        ],
        compiler_params=params(),
        name="outer_planes",
    )(plane_offsets, populations, order_pops, phase, from_low, from_high, *blocks, odd, flow_part, order_part)


def shards(populations, order_pops, plane_offsets):
    slabs, strips = lax.axis_size("gx"), lax.axis_size("gy")
    even_step, odd_step, even, own_odd, to_low, to_high = pl.pallas_call(
        payload_kernel,
        out_shape=(
            jax.ShapeDtypeStruct((1,), jnp.int32),
            jax.ShapeDtypeStruct((1,), jnp.int32),
            f32(PAYLOAD, ROWS, LANES),
            f32(PAYLOAD, ROWS, LANES),
            f32(PACKED, LANES),
            f32(PACKED, LANES),
        ),
        in_specs=smem() + hbm(2),
        out_specs=tuple(smem() * 2 + vmem(4)),
        scratch_shapes=[
            scratch(*populations.shape),
            scratch(*order_pops.shape),
            scratch(PLANES, ROWS, LANES),
            sems(len(FLOW_PIECES)),
            sems(len(ORDER_PIECES)),
        ],
        compiler_params=params(),
        name="payloads",
    )(plane_offsets, populations, order_pops)

    from_low = lax.ppermute(to_high, "gy", shift_pairs(strips, 1))
    from_high = lax.ppermute(to_low, "gy", shift_pairs(strips, -1))
    window = odd_window(plane_offsets, from_low, own_odd, from_high)

    def odd_branch(step):
        return lambda mine: lax.ppermute(mine, ("gx", "gy"), swap_pairs(slabs, strips, 1, step))

    odd = lax.switch(odd_step.reshape(()), [odd_branch(step) for step in range(strips)], window)

    def even_branch(step):
        def run(mine, flow, order, low, high):
            blocks = tuple(
                lax.ppermute(mine, ("gx", "gy"), swap_pairs(slabs, strips, 0, step + d)) for d in (-1, 0, 1)
            )
            return blocks, *inner_planes(flow, order, low, high)

        return run

    even, odd = lax.optimization_barrier((even, odd))
    blocks, phase, flow_part, order_part = lax.switch(
        even_step.reshape(()),
        [even_branch(step) for step in range(strips)],
        even, populations, order_pops, from_low, from_high,
    )
    return outer_planes(
        odd, plane_offsets, populations, order_pops, phase, from_low, from_high, blocks, flow_part, order_part
    )


def solution(mesh):
    return jax.shard_map(
        shards,
        mesh=mesh,
        in_specs=(P(None, "gx", "gy", None), P(None, "gx", "gy", None), P()),
        out_specs=(P(None, "gx", "gy", None), P(None, "gx", "gy", None)),
        check_vma=False,
    )
```

```python
import jax
import jax.numpy as jnp
from jax import lax
from jax.experimental import pallas as pl
from jax.experimental.pallas import tpu as pltpu
from jax.sharding import PartitionSpec as P

SHIFT_FRACTION = 0.375
WALL_SPEED = 0.05
RELAX_FLOW = 0.8
RELAX_ORDER = 0.9
BULK_COEFF = 0.05
SURFACE_COEFF = 0.04
MOBILITY = 1.0
VELOCITY_X = (0, 1, -1, 0, 0, 0, 0, 1, -1, 1, -1, 1, -1, 1, -1, 0, 0, 0, 0)
VELOCITY_Y = (0, 0, 0, 1, -1, 0, 0, 1, -1, -1, 1, 0, 0, 0, 0, 1, -1, 1, -1)
VELOCITY_Z = (0, 0, 0, 0, 0, 1, -1, 0, 0, 0, 0, 1, -1, -1, 1, 1, -1, -1, 1)
WEIGHT_TABLE = (1.0 / 3.0,) + (1.0 / 18.0,) * 6 + (1.0 / 36.0,) * 12

VELS = 19
PLANES = 16
ROWS = 8
LANES = 128
UP_X = tuple(i for i in range(VELS) if VELOCITY_X[i] == 1)
DOWN_X = tuple(i for i in range(VELS) if VELOCITY_X[i] == -1)
UP_Y = tuple(i for i in range(VELS) if VELOCITY_Y[i] == 1)
DOWN_Y = tuple(i for i in range(VELS) if VELOCITY_Y[i] == -1)
PAYLOAD = 17
AT_MOMENTS = 5
AT_ORDER = 9
AT_PHASE = 14
WINDOW = 16
WINDOW_PAD = 4

SMALL_VMEM = 16 * 1024 * 1024
MAIN_VMEM = 24 * 1024 * 1024


def roll_rows(cells, step):
    return pltpu.roll(cells, step % cells.shape[0], 0)


def roll_lanes(cells, step):
    return pltpu.roll(cells, step % LANES, cells.ndim - 1)


def moments(flow):
    parts = [flow(i) for i in range(VELS)]
    density = parts[0]
    for part in parts[1:]:
        density = density + part
    speeds = []
    for table in (VELOCITY_X, VELOCITY_Y, VELOCITY_Z):
        plus = [parts[i] for i in range(VELS) if table[i] == 1]
        minus = [parts[i] for i in range(VELS) if table[i] == -1]
        total = plus[0] - minus[0]
        for a, b in zip(plus[1:], minus[1:]):
            total = total + (a - b)
        speeds.append(total)
    return density, speeds


def potential_of(phase, neighbours):
    around = neighbours[0]
    for cells in neighbours[1:]:
        around = around + cells
    bulk = BULK_COEFF * (phase * phase * phase - phase)
    return bulk - SURFACE_COEFF * (around - 6.0 * phase)


def dot_velocity(i, vector):
    total = None
    for sign, part in zip((VELOCITY_X[i], VELOCITY_Y[i], VELOCITY_Z[i]), vector):
        if sign == 0:
            continue
        if total is None:
            total = part if sign == 1 else -part
        else:
            total = total + part if sign == 1 else total - part
    return total


def collide(wanted, flow, order, density, momentum, phase, potential, force):
    inverse = 1.0 / density
    speed = [(momentum[d] + 0.5 * force[d]) * inverse for d in range(3)]
    source = 1.0 - 0.5 / RELAX_FLOW
    relaxed = density * (1.0 / RELAX_FLOW)
    speed_sq = speed[0] * speed[0] + speed[1] * speed[1] + speed[2] * speed[2]
    work = speed[0] * force[0] + speed[1] * force[1] + speed[2] * force[2]
    even = relaxed * (1.0 - 1.5 * speed_sq) - (3.0 * source) * work
    odd = [3.0 * (relaxed * speed[d] + source * force[d]) for d in range(3)]
    quad = [4.5 * relaxed * speed[d] + (9.0 * source) * force[d] for d in range(3)]
    order_even = (3.0 * MOBILITY / RELAX_ORDER) * potential
    carried = (3.0 / RELAX_ORDER) * phase
    order_odd = [carried * speed[d] for d in range(3)]
    flow_out, order_out = {}, {}
    keep_flow = 1.0 - 1.0 / RELAX_FLOW
    keep_order = 1.0 - 1.0 / RELAX_ORDER
    done = set()
    for i in wanted:
        if i in done:
            continue
        weight = WEIGHT_TABLE[i]
        if i == 0:
            flow_out[0] = keep_flow * flow(0) + weight * even
            rest = phase - (2.0 * MOBILITY) * potential
            order_out[0] = keep_order * order(0) + (1.0 / RELAX_ORDER) * rest
            continue
        first = i if i % 2 == 1 else i - 1
        pair_even = weight * (even + dot_velocity(first, speed) * dot_velocity(first, quad))
        pair_odd = weight * dot_velocity(first, odd)
        pair_order = weight * dot_velocity(first, order_odd)
        for member, sign in ((first, 1), (first + 1, -1)):
            if member not in wanted:
                continue
            done.add(member)
            both = pair_even + pair_odd if sign == 1 else pair_even - pair_odd
            flow_out[member] = keep_flow * flow(member) + both
            both = weight * order_even
            both = both + pair_order if sign == 1 else both - pair_order
            order_out[member] = keep_order * order(member) + both
    return flow_out, order_out


def add_phase(phase_ref, order_ref, x):
    total = order_ref[0, x]
    for i in range(1, VELS):
        total = total + order_ref[i, x]
    phase_ref[x] = total


def plane_copies(source, target, sems, pieces):
    return [
        pltpu.make_async_copy(source.at[:, pl.ds(first, count)], target.at[:, pl.ds(first, count)], sems.at[index])
        for index, (first, count) in enumerate(pieces)
    ]


QUARTERS = ((0, 4), (4, 4), (8, 4), (12, 4))


def even_boundary(slab):
    return slab + 1 - slab % 2


def odd_boundary(slab, slabs):
    return lax.rem(slab + slab % 2, slabs)


def side_rows(index):
    return pl.ds(index * PLANES, PLANES)


def side_row(ref, index, x):
    return ref[pl.ds(index * PLANES + x, 1), :]


def payload_kernel(
    offset_ref, flow_ref, order_ref, even_step, odd_step, even_ref, odd_ref, low_ref, high_ref, phase_ref
):
    slab = lax.axis_index("gx")
    is_even = slab % 2 == 0
    strips = lax.axis_size("gy")
    even_step[0] = lax.rem((offset_ref[even_boundary(slab)] + 5) // ROWS, strips)
    odd_step[0] = lax.rem((offset_ref[odd_boundary(slab, offset_ref.shape[0])] + 5) // ROWS, strips)
    for x in range(PLANES):
        add_phase(phase_ref, order_ref, x)
    sides = []
    for plane, inward, comps in ((PLANES - 1, -1, UP_X), (0, 1, DOWN_X)):
        density, momentum = moments(lambda i: flow_ref[i, plane])
        parts = [flow_ref[i, plane] for i in comps] + [density] + momentum
        parts += [order_ref[i, plane] for i in comps]
        parts += [phase_ref[plane + inward * d] for d in range(3)]
        sides.append(parts)
    for index, (last, first) in enumerate(zip(*sides)):
        even_ref[index] = jnp.where(is_even, last, first)
        odd_ref[index] = jnp.where(is_even, first, last)
    for out_ref, row, inward, comps in ((high_ref, ROWS - 1, -1, UP_Y), (low_ref, 0, 1, DOWN_Y)):
        density, momentum = moments(lambda i: flow_ref[i, :, row, :])
        parts = [flow_ref[i, :, row, :] for i in comps] + [density] + momentum
        parts += [order_ref[i, :, row, :] for i in comps]
        parts += [phase_ref[:, row + inward * d, :] for d in range(3)]
        for index, part in enumerate(parts):
            out_ref[side_rows(index), :] = part


def window_kernel(offset_ref, before_ref, own_ref, after_ref, out_ref):
    slab = lax.axis_index("gx")
    inner = lax.rem(offset_ref[odd_boundary(slab, offset_ref.shape[0])] + 5, ROWS)

    blocks = [lambda index, ref=ref: ref[index] for ref in (before_ref, own_ref, after_ref)]
    cut_window(blocks, jnp.where(slab % 2 == 0, inner, 9 - inner), out_ref)


def cut_window(blocks, start, window_ref):
    row = lax.broadcasted_iota(jnp.int32, (ROWS, LANES), 0)
    inner = lax.rem(start, ROWS)
    back = lax.rem(ROWS - inner, ROWS)
    early = row < ROWS - inner
    near = start < ROWS
    for index in range(PAYLOAD):
        rolled = [pltpu.roll(block(index), back, 0) for block in blocks]
        first = jnp.where(near, rolled[0], rolled[1])
        second = jnp.where(near, rolled[1], rolled[2])
        window_ref[index, 0:ROWS] = jnp.where(early, first, second)
        window_ref[index, ROWS : 2 * ROWS] = jnp.where(early, second, rolled[2])


def ghost_plane(window_ref, comps, own, own_next, weight, kick_speed):
    other = 1.0 - weight

    def sheared(cells):
        return weight * cells + other * roll_rows(cells, 1)

    def seen(cells):
        return other * roll_rows(cells, -1) + weight * cells

    def sides(cells):
        return [roll_rows(cells, 1), roll_rows(cells, -1), roll_lanes(cells, 1), roll_lanes(cells, -1)]

    near, second, third = [window_ref[AT_PHASE + d] for d in range(3)]
    ghost_phase = sheared(near)
    own_potential = potential_of(own, [own_next, ghost_phase] + sides(own))
    near_potential = potential_of(near, [second, seen(own)] + sides(near))
    second_potential = potential_of(second, [third, near] + sides(second))
    beyond = seen(own_potential)
    outward = 1.0 if VELOCITY_X[comps[0]] == 1 else -1.0
    half = -0.5 * near
    force = [
        outward * half * (beyond - second_potential),
        half * (roll_rows(near_potential, -1) - roll_rows(near_potential, 1)),
        half * (roll_lanes(near_potential, -1) - roll_lanes(near_potential, 1)),
    ]
    density = window_ref[AT_MOMENTS]
    momentum = [window_ref[AT_MOMENTS + 1 + d] for d in range(3)]
    flow_out, order_out = collide(
        comps,
        lambda i: window_ref[comps.index(i)],
        lambda i: window_ref[AT_ORDER + comps.index(i)],
        density,
        momentum,
        near,
        near_potential,
        force,
    )
    flow_ghost = []
    for i in comps:
        cells = flow_out[i]
        if VELOCITY_Y[i] != 0:
            cells = cells + (WEIGHT_TABLE[i] * 3.0 * VELOCITY_Y[i] * kick_speed) * density
        flow_ghost.append(sheared(cells))
    order_ghost = [sheared(order_out[i]) for i in comps]
    return ghost_phase, own_potential, sheared(near_potential), flow_ghost, order_ghost


def rows_before(cells, line):
    row = lax.broadcasted_iota(jnp.int32, (ROWS, LANES), 0)
    return jnp.where(row == 0, line, roll_rows(cells, 1))


def rows_after(cells, line):
    row = lax.broadcasted_iota(jnp.int32, (ROWS, LANES), 0)
    return jnp.where(row == ROWS - 1, line, roll_rows(cells, -1))


def collide_sides(phase_ref, low_ref, high_ref, below, above, low_side, high_side, edge_ref):
    plane_at = lax.broadcasted_iota(jnp.int32, (PLANES, LANES), 0)

    def across(cells, which, own_row):
        before, after = roll_rows(cells, 1), roll_rows(cells, -1)
        if below is not None:
            before = jnp.where(plane_at == 0, below(which, own_row), before)
            after = jnp.where(plane_at == PLANES - 1, above(which, own_row), after)
        return before, after

    for side_ref, out_ref, edge, beside, inward, comps in (
        (low_ref, low_side, 0, -1, 1, UP_Y),
        (high_ref, high_side, ROWS - 1, ROWS, -1, DOWN_Y),
    ):
        own = [phase_ref[:, edge + inward * d, :] for d in range(2)]
        outer = [side_ref[side_rows(AT_PHASE + d), :] for d in range(3)]
        lines = [own[1], own[0]] + outer
        potentials = []
        for index in range(1, 4):
            cells = lines[index]
            around = list(across(cells, 0, edge + inward * (1 - index)))
            around += [lines[index - 1], lines[index + 1], roll_lanes(cells, 1), roll_lanes(cells, -1)]
            potentials.append(potential_of(cells, around))
        inside, here, outside = potentials
        before, after = across(here, 1, beside)
        half = -0.5 * outer[0]
        force = [
            half * (after - before),
            (inward * half) * (inside - outside),
            half * (roll_lanes(here, -1) - roll_lanes(here, 1)),
        ]
        flow_post, order_post = collide(
            comps,
            lambda i: side_ref[side_rows(comps.index(i)), :],
            lambda i: side_ref[side_rows(AT_ORDER + comps.index(i)), :],
            side_ref[side_rows(AT_MOMENTS), :],
            [side_ref[side_rows(AT_MOMENTS + 1 + d), :] for d in range(3)],
            outer[0],
            here,
            force,
        )
        for index, i in enumerate(comps):
            out_ref[index] = flow_post[i]
            out_ref[5 + index] = order_post[i]
        edge_ref[0 if inward == 1 else 1] = here


def plane_potential(phase_ref, low_ref, high_ref, x):
    cells = phase_ref[x]
    around = [
        phase_ref[x - 1],
        phase_ref[x + 1],
        rows_before(cells, side_row(low_ref, AT_PHASE, x)),
        rows_after(cells, side_row(high_ref, AT_PHASE, x)),
        roll_lanes(cells, 1),
        roll_lanes(cells, -1),
    ]
    return potential_of(cells, around)


def collide_plane(x, skip, flow_ref, order_ref, phase_ref, potential_ref, edge_ref, low_side, high_side, flow_out, order_out):
    here = potential_ref[x + 1]
    phase = phase_ref[x]
    half = -0.5 * phase
    along_y = rows_after(here, edge_ref[1, pl.ds(x, 1), :]) - rows_before(here, edge_ref[0, pl.ds(x, 1), :])
    force = [
        half * (potential_ref[x + 2] - potential_ref[x]),
        half * along_y,
        half * (roll_lanes(here, -1) - roll_lanes(here, 1)),
    ]
    density, momentum = moments(lambda i: flow_ref[i, x])
    flow_post, order_post = collide(
        tuple(i for i in range(VELS) if VELOCITY_X[i] == 0 or VELOCITY_X[i] != skip),
        lambda i: flow_ref[i, x],
        lambda i: order_ref[i, x],
        density,
        momentum,
        phase,
        here,
        force,
    )

    def moved(i, cells, first):
        if VELOCITY_Y[i] == 1:
            cells = rows_before(cells, low_side[first + UP_Y.index(i), pl.ds(x, 1), :])
        elif VELOCITY_Y[i] == -1:
            cells = rows_after(cells, high_side[first + DOWN_Y.index(i), pl.ds(x, 1), :])
        if VELOCITY_Z[i] != 0:
            cells = roll_lanes(cells, VELOCITY_Z[i])
        return cells

    for i in flow_post:
        target = x + VELOCITY_X[i]
        flow_out[i, target] = moved(i, flow_post[i], 0)
        order_out[i, target] = moved(i, order_post[i], 5)


def main_kernel(
    offset_ref, flow_ref, order_ref, low_ref, high_ref, minus_ref, same_ref, plus_ref, odd_ref, flow_hbm_out, order_hbm_out,
    flow_out, order_out, phase_ref, below_ref, above_ref, wide_ref, ghost_ref, potential_ref, low_side, high_side, edge_ref,
    flow_out_sems, order_out_sems,
):
    for x in range(PLANES):
        add_phase(phase_ref, order_ref, x)
    slab = lax.axis_index("gx")
    is_even = slab % 2 == 0
    inner = lax.rem(offset_ref[even_boundary(slab)] + 5, ROWS)
    blocks = [
        lambda at: jnp.where(is_even, minus_ref[at], plus_ref[at]),
        lambda at: same_ref[at],
        lambda at: jnp.where(is_even, plus_ref[at], minus_ref[at]),
    ]
    cut_window(blocks, jnp.where(is_even, inner, 9 - inner), above_ref)
    for index in range(PAYLOAD):
        even, odd = above_ref[index], odd_ref[index]
        below_ref[index] = jnp.where(is_even, odd, even)
        above_ref[index] = jnp.where(is_even, even, odd)

    for index, plane in enumerate((0, 1, PLANES - 1, PLANES - 2)):
        wide_ref[index] = jnp.zeros((WINDOW, LANES), jnp.float32)
        for d in range(3):
            wide_ref[index, 3 - d : 4 - d, :] = side_row(low_ref, AT_PHASE + d, plane)
            wide_ref[index, 12 + d : 13 + d, :] = side_row(high_ref, AT_PHASE + d, plane)
        wide_ref[index, 4:12, :] = phase_ref[plane]
    below = ghost_plane(below_ref, UP_X, wide_ref[0], wide_ref[1], 1.0 - SHIFT_FRACTION, WALL_SPEED)
    above = ghost_plane(above_ref, DOWN_X, wide_ref[2], wide_ref[3], SHIFT_FRACTION, -WALL_SPEED)
    for index in range(5):
        ghost_ref[index] = below[3][index]
        ghost_ref[5 + index] = below[4][index]
        ghost_ref[10 + index] = above[3][index]
        ghost_ref[15 + index] = above[4][index]

    def ghost_row(ghost):
        return lambda which, own_row: ghost[2 * which][own_row + WINDOW_PAD : own_row + WINDOW_PAD + 1, :]

    collide_sides(
        phase_ref, low_ref, high_ref, ghost_row(below), ghost_row(above), low_side, high_side, edge_ref
    )
    wide_ref[0] = below[1]
    wide_ref[1] = below[2]
    wide_ref[2] = above[1]
    wide_ref[3] = above[2]
    potential_ref[1] = wide_ref[0, 4:12, :]
    potential_ref[0] = wide_ref[1, 4:12, :]
    potential_ref[PLANES] = wide_ref[2, 4:12, :]
    potential_ref[PLANES + 1] = wide_ref[3, 4:12, :]
    for x in range(1, PLANES - 1):
        potential_ref[x + 1] = plane_potential(phase_ref, low_ref, high_ref, x)
    for comps, first, target in ((UP_X, 0, 0), (DOWN_X, 10, PLANES - 1)):
        for index, i in enumerate(comps):
            start = WINDOW_PAD - VELOCITY_Y[i]
            for out_ref, at in ((flow_out, first + index), (order_out, first + 5 + index)):
                cells = ghost_ref[at, start : start + ROWS, :]
                if VELOCITY_Z[i] != 0:
                    cells = roll_lanes(cells, VELOCITY_Z[i])
                out_ref[i, target] = cells
    flow_writes = plane_copies(flow_out, flow_hbm_out, flow_out_sems, QUARTERS)
    order_writes = plane_copies(order_out, order_hbm_out, order_out_sems, QUARTERS)

    def one_plane(x, skip):
        collide_plane(
            x, skip, flow_ref, order_ref, phase_ref, potential_ref, edge_ref, low_side, high_side, flow_out, order_out
        )

    def step(x, carry):
        one_plane(x, 0)
        for quarter, (first, count) in enumerate(QUARTERS[:-1]):

            @pl.when(x == first + count)
            def _(quarter=quarter):
                flow_writes[quarter].start()
                order_writes[quarter].start()

        return carry

    one_plane(0, -1)
    lax.fori_loop(1, PLANES - 1, step, 0)
    one_plane(PLANES - 1, 1)
    flow_writes[-1].start()
    order_writes[-1].start()
    for copy in flow_writes + order_writes:
        copy.wait()


def vmem(count):
    return [pl.BlockSpec(memory_space=pltpu.VMEM)] * count


def params(limit):
    return pltpu.CompilerParams(vmem_limit_bytes=limit)


def f32(*shape):
    return jax.ShapeDtypeStruct(shape, jnp.float32)


def shift_pairs(count, step):
    return [(i, (i + step) % count) for i in range(count)]


def swap_pairs(slabs, strips, first, step):
    pairs = []
    for low in range(first, slabs, 2):
        high = (low + 1) % slabs
        for strip in range(strips):
            other = (strip + step) % strips
            pairs.append((low * strips + strip, high * strips + other))
            pairs.append((high * strips + other, low * strips + strip))
    return pairs


def hbm(count):
    return [pl.BlockSpec(memory_space=pltpu.HBM)] * count


def smem():
    return [pl.BlockSpec(memory_space=pltpu.SMEM)]


def scratch(*shape):
    return pltpu.VMEM(shape, jnp.float32)


def sems(count):
    return pltpu.SemaphoreType.DMA((count,))


def main_planes(plane_offsets, flow, order, from_low, from_high, blocks, odd):
    return pl.pallas_call(
        main_kernel,
        out_shape=(f32(*flow.shape), f32(*order.shape)),
        in_specs=smem() + vmem(8),
        out_specs=tuple(hbm(2)),
        scratch_shapes=[
            scratch(*flow.shape),
            scratch(*order.shape),
            scratch(PLANES, ROWS, LANES),
            scratch(PAYLOAD, WINDOW, LANES),
            scratch(PAYLOAD, WINDOW, LANES),
            scratch(4, WINDOW, LANES),
            scratch(20, WINDOW, LANES),
            scratch(PLANES + 2, ROWS, LANES),
            scratch(10, PLANES, LANES),
            scratch(10, PLANES, LANES),
            scratch(2, PLANES, LANES),
            sems(len(QUARTERS)),
            sems(len(QUARTERS)),
        ],
        compiler_params=params(MAIN_VMEM),
        name="collide_stream",
    )(plane_offsets, flow, order, from_low, from_high, *blocks, odd)


def shards(populations, order_pops, plane_offsets):
    slabs, strips = lax.axis_size("gx"), lax.axis_size("gy")
    even_step, odd_step, even, own, to_low, to_high = pl.pallas_call(
        payload_kernel,
        out_shape=(
            jax.ShapeDtypeStruct((1,), jnp.int32),
            jax.ShapeDtypeStruct((1,), jnp.int32),
            f32(PAYLOAD, ROWS, LANES),
            f32(PAYLOAD, ROWS, LANES),
            f32(PAYLOAD * PLANES, LANES),
            f32(PAYLOAD * PLANES, LANES),
        ),
        in_specs=smem() + vmem(2),
        out_specs=tuple(smem() * 2 + vmem(4)),
        scratch_shapes=[scratch(PLANES, ROWS, LANES)],
        compiler_params=params(SMALL_VMEM),
        name="payloads",
    )(plane_offsets, populations, order_pops)

    up, down = shift_pairs(strips, 1), shift_pairs(strips, -1)
    before = lax.ppermute(own, "gy", up)
    after = lax.ppermute(own, "gy", down)

    def even_branch(step):
        def run(mine):
            return tuple(
                lax.ppermute(mine, ("gx", "gy"), swap_pairs(slabs, strips, 0, step + d)) for d in (-1, 0, 1)
            )

        return run

    blocks = lax.switch(even_step.reshape(()), [even_branch(step) for step in range(strips)], even)
    before, after, blocks = lax.optimization_barrier((before, after, blocks))
    window = pl.pallas_call(
        window_kernel,
        out_shape=f32(PAYLOAD, WINDOW, LANES),
        in_specs=smem() + vmem(3),
        out_specs=vmem(1)[0],
        compiler_params=params(SMALL_VMEM),
        name="window",
    )(plane_offsets, before, own, after)

    to_low, to_high, window = lax.optimization_barrier((to_low, to_high, window))
    from_low = lax.ppermute(to_high, "gy", up)
    from_high = lax.ppermute(to_low, "gy", down)

    def odd_branch(step):
        return lambda mine: lax.ppermute(mine, ("gx", "gy"), swap_pairs(slabs, strips, 1, step))

    odd = lax.switch(odd_step.reshape(()), [odd_branch(step) for step in range(strips)], window)
    return main_planes(plane_offsets, populations, order_pops, from_low, from_high, blocks, odd)


def solution(mesh):
    return jax.shard_map(
        shards,
        mesh=mesh,
        in_specs=(P(None, "gx", "gy", None), P(None, "gx", "gy", None), P()),
        out_specs=(P(None, "gx", "gy", None), P(None, "gx", "gy", None)),
        check_vma=False,
    )
```

```python
import jax
import jax.numpy as jnp
from jax import lax
from jax.experimental import pallas as pl
from jax.experimental.pallas import tpu as pltpu
from jax.sharding import PartitionSpec as P

SHIFT_FRACTION = 0.375
WALL_SPEED = 0.05
RELAX_FLOW = 0.8
RELAX_ORDER = 0.9
BULK_COEFF = 0.05
SURFACE_COEFF = 0.04
MOBILITY = 1.0
VELOCITY_X = (0, 1, -1, 0, 0, 0, 0, 1, -1, 1, -1, 1, -1, 1, -1, 0, 0, 0, 0)
VELOCITY_Y = (0, 0, 0, 1, -1, 0, 0, 1, -1, -1, 1, 0, 0, 0, 0, 1, -1, 1, -1)
VELOCITY_Z = (0, 0, 0, 0, 0, 1, -1, 0, 0, 0, 0, 1, -1, -1, 1, 1, -1, -1, 1)
WEIGHT_TABLE = (1.0 / 3.0,) + (1.0 / 18.0,) * 6 + (1.0 / 36.0,) * 12

VELS = 19
PLANES = 16
ROWS = 8
LANES = 128
UP_X = tuple(i for i in range(VELS) if VELOCITY_X[i] == 1)
DOWN_X = tuple(i for i in range(VELS) if VELOCITY_X[i] == -1)
UP_Y = tuple(i for i in range(VELS) if VELOCITY_Y[i] == 1)
DOWN_Y = tuple(i for i in range(VELS) if VELOCITY_Y[i] == -1)
PAYLOAD = 17
AT_MOMENTS = 5
AT_ORDER = 9
AT_PHASE = 14
WINDOW = 16
WINDOW_PAD = 4

SMALL_VMEM = 16 * 1024 * 1024
MAIN_VMEM = 24 * 1024 * 1024


def roll_rows(cells, step):
    return pltpu.roll(cells, step % cells.shape[0], 0)


def roll_lanes(cells, step):
    return pltpu.roll(cells, step % LANES, cells.ndim - 1)


def moments(flow):
    parts = [flow(i) for i in range(VELS)]
    density = parts[0]
    for part in parts[1:]:
        density = density + part
    speeds = []
    for table in (VELOCITY_X, VELOCITY_Y, VELOCITY_Z):
        plus = [parts[i] for i in range(VELS) if table[i] == 1]
        minus = [parts[i] for i in range(VELS) if table[i] == -1]
        total = plus[0] - minus[0]
        for a, b in zip(plus[1:], minus[1:]):
            total = total + (a - b)
        speeds.append(total)
    return density, speeds


def potential_of(phase, neighbours):
    around = neighbours[0]
    for cells in neighbours[1:]:
        around = around + cells
    bulk = BULK_COEFF * (phase * phase * phase - phase)
    return bulk - SURFACE_COEFF * (around - 6.0 * phase)


def dot_velocity(i, vector):
    total = None
    for sign, part in zip((VELOCITY_X[i], VELOCITY_Y[i], VELOCITY_Z[i]), vector):
        if sign == 0:
            continue
        if total is None:
            total = part if sign == 1 else -part
        else:
            total = total + part if sign == 1 else total - part
    return total


def collide(wanted, flow, order, density, momentum, phase, potential, force):
    inverse = 1.0 / density
    speed = [(momentum[d] + 0.5 * force[d]) * inverse for d in range(3)]
    source = 1.0 - 0.5 / RELAX_FLOW
    relaxed = density * (1.0 / RELAX_FLOW)
    speed_sq = speed[0] * speed[0] + speed[1] * speed[1] + speed[2] * speed[2]
    work = speed[0] * force[0] + speed[1] * force[1] + speed[2] * force[2]
    even = relaxed * (1.0 - 1.5 * speed_sq) - (3.0 * source) * work
    odd = [3.0 * (relaxed * speed[d] + source * force[d]) for d in range(3)]
    quad = [4.5 * relaxed * speed[d] + (9.0 * source) * force[d] for d in range(3)]
    order_even = (3.0 * MOBILITY / RELAX_ORDER) * potential
    carried = (3.0 / RELAX_ORDER) * phase
    order_odd = [carried * speed[d] for d in range(3)]
    flow_out, order_out = {}, {}
    keep_flow = 1.0 - 1.0 / RELAX_FLOW
    keep_order = 1.0 - 1.0 / RELAX_ORDER
    done = set()
    for i in wanted:
        if i in done:
            continue
        weight = WEIGHT_TABLE[i]
        if i == 0:
            flow_out[0] = keep_flow * flow(0) + weight * even
            rest = phase - (2.0 * MOBILITY) * potential
            order_out[0] = keep_order * order(0) + (1.0 / RELAX_ORDER) * rest
            continue
        first = i if i % 2 == 1 else i - 1
        pair_even = weight * (even + dot_velocity(first, speed) * dot_velocity(first, quad))
        pair_odd = weight * dot_velocity(first, odd)
        pair_order = weight * dot_velocity(first, order_odd)
        for member, sign in ((first, 1), (first + 1, -1)):
            if member not in wanted:
                continue
            done.add(member)
            both = pair_even + pair_odd if sign == 1 else pair_even - pair_odd
            flow_out[member] = keep_flow * flow(member) + both
            both = weight * order_even
            both = both + pair_order if sign == 1 else both - pair_order
            order_out[member] = keep_order * order(member) + both
    return flow_out, order_out


def add_phase(phase_ref, order_ref, x):
    total = order_ref[0, x]
    for i in range(1, VELS):
        total = total + order_ref[i, x]
    phase_ref[x] = total


def plane_copies(source, target, sems, pieces):
    return [
        pltpu.make_async_copy(source.at[:, pl.ds(first, count)], target.at[:, pl.ds(first, count)], sems.at[index])
        for index, (first, count) in enumerate(pieces)
    ]


QUARTERS = ((0, 4), (4, 4), (8, 4), (12, 4))


def even_boundary(slab):
    return slab + 1 - slab % 2


def odd_boundary(slab, slabs):
    return lax.rem(slab + slab % 2, slabs)


PACKED = PAYLOAD * (ROWS + PLANES)


def block_rows(index):
    return pl.ds(index * ROWS, ROWS)


def side_rows(index):
    return pl.ds(PAYLOAD * ROWS + index * PLANES, PLANES)


def side_row(ref, index, x):
    return ref[pl.ds(PAYLOAD * ROWS + index * PLANES + x, 1), :]


def payload_kernel(flow_ref, order_ref, even_ref, odd_ref, low_ref, high_ref, phase_ref):
    is_even = lax.axis_index("gx") % 2 == 0
    for x in range(PLANES):
        add_phase(phase_ref, order_ref, x)
    sides = []
    for plane, inward, comps in ((PLANES - 1, -1, UP_X), (0, 1, DOWN_X)):
        density, momentum = moments(lambda i: flow_ref[i, plane])
        parts = [flow_ref[i, plane] for i in comps] + [density] + momentum
        parts += [order_ref[i, plane] for i in comps]
        parts += [phase_ref[plane + inward * d] for d in range(3)]
        sides.append(parts)
    for index, (last, first) in enumerate(zip(*sides)):
        even_ref[index] = jnp.where(is_even, last, first)
        odd = jnp.where(is_even, first, last)
        odd_ref[index] = odd
        low_ref[block_rows(index), :] = odd
        high_ref[block_rows(index), :] = odd
    for out_ref, row, inward, comps in ((high_ref, ROWS - 1, -1, UP_Y), (low_ref, 0, 1, DOWN_Y)):
        density, momentum = moments(lambda i: flow_ref[i, :, row, :])
        parts = [flow_ref[i, :, row, :] for i in comps] + [density] + momentum
        parts += [order_ref[i, :, row, :] for i in comps]
        parts += [phase_ref[:, row + inward * d, :] for d in range(3)]
        for index, part in enumerate(parts):
            out_ref[side_rows(index), :] = part


def window_kernel(offset_ref, before_ref, own_ref, after_ref, out_ref):
    slab = lax.axis_index("gx")
    inner = lax.rem(offset_ref[odd_boundary(slab, offset_ref.shape[0])] + 5, ROWS)

    blocks = [
        lambda index: before_ref[block_rows(index), :],
        lambda index: own_ref[index],
        lambda index: after_ref[block_rows(index), :],
    ]
    cut_window(blocks, jnp.where(slab % 2 == 0, inner, 9 - inner), out_ref)


def cut_window(blocks, start, window_ref):
    row = lax.broadcasted_iota(jnp.int32, (ROWS, LANES), 0)
    inner = lax.rem(start, ROWS)
    back = lax.rem(ROWS - inner, ROWS)
    early = row < ROWS - inner
    near = start < ROWS
    for index in range(PAYLOAD):
        rolled = [pltpu.roll(block(index), back, 0) for block in blocks]
        first = jnp.where(near, rolled[0], rolled[1])
        second = jnp.where(near, rolled[1], rolled[2])
        window_ref[index, 0:ROWS] = jnp.where(early, first, second)
        window_ref[index, ROWS : 2 * ROWS] = jnp.where(early, second, rolled[2])


def ghost_plane(window_ref, comps, own, own_next, weight, kick_speed):
    other = 1.0 - weight

    def sheared(cells):
        return weight * cells + other * roll_rows(cells, 1)

    def seen(cells):
        return other * roll_rows(cells, -1) + weight * cells

    def sides(cells):
        return [roll_rows(cells, 1), roll_rows(cells, -1), roll_lanes(cells, 1), roll_lanes(cells, -1)]

    near, second, third = [window_ref[AT_PHASE + d] for d in range(3)]
    ghost_phase = sheared(near)
    own_potential = potential_of(own, [own_next, ghost_phase] + sides(own))
    near_potential = potential_of(near, [second, seen(own)] + sides(near))
    second_potential = potential_of(second, [third, near] + sides(second))
    beyond = seen(own_potential)
    outward = 1.0 if VELOCITY_X[comps[0]] == 1 else -1.0
    half = -0.5 * near
    force = [
        outward * half * (beyond - second_potential),
        half * (roll_rows(near_potential, -1) - roll_rows(near_potential, 1)),
        half * (roll_lanes(near_potential, -1) - roll_lanes(near_potential, 1)),
    ]
    density = window_ref[AT_MOMENTS]
    momentum = [window_ref[AT_MOMENTS + 1 + d] for d in range(3)]
    flow_out, order_out = collide(
        comps,
        lambda i: window_ref[comps.index(i)],
        lambda i: window_ref[AT_ORDER + comps.index(i)],
        density,
        momentum,
        near,
        near_potential,
        force,
    )
    flow_ghost = []
    for i in comps:
        cells = flow_out[i]
        if VELOCITY_Y[i] != 0:
            cells = cells + (WEIGHT_TABLE[i] * 3.0 * VELOCITY_Y[i] * kick_speed) * density
        flow_ghost.append(sheared(cells))
    order_ghost = [sheared(order_out[i]) for i in comps]
    return ghost_phase, own_potential, sheared(near_potential), flow_ghost, order_ghost


def rows_before(cells, line):
    row = lax.broadcasted_iota(jnp.int32, (ROWS, LANES), 0)
    return jnp.where(row == 0, line, roll_rows(cells, 1))


def rows_after(cells, line):
    row = lax.broadcasted_iota(jnp.int32, (ROWS, LANES), 0)
    return jnp.where(row == ROWS - 1, line, roll_rows(cells, -1))


def collide_sides(phase_ref, low_ref, high_ref, below, above, low_side, high_side, edge_ref):
    plane_at = lax.broadcasted_iota(jnp.int32, (PLANES, LANES), 0)

    def across(cells, which, own_row):
        before, after = roll_rows(cells, 1), roll_rows(cells, -1)
        if below is not None:
            before = jnp.where(plane_at == 0, below(which, own_row), before)
            after = jnp.where(plane_at == PLANES - 1, above(which, own_row), after)
        return before, after

    for side_ref, out_ref, edge, beside, inward, comps in (
        (low_ref, low_side, 0, -1, 1, UP_Y),
        (high_ref, high_side, ROWS - 1, ROWS, -1, DOWN_Y),
    ):
        own = [phase_ref[:, edge + inward * d, :] for d in range(2)]
        outer = [side_ref[side_rows(AT_PHASE + d), :] for d in range(3)]
        lines = [own[1], own[0]] + outer
        potentials = []
        for index in range(1, 4):
            cells = lines[index]
            around = list(across(cells, 0, edge + inward * (1 - index)))
            around += [lines[index - 1], lines[index + 1], roll_lanes(cells, 1), roll_lanes(cells, -1)]
            potentials.append(potential_of(cells, around))
        inside, here, outside = potentials
        before, after = across(here, 1, beside)
        half = -0.5 * outer[0]
        force = [
            half * (after - before),
            (inward * half) * (inside - outside),
            half * (roll_lanes(here, -1) - roll_lanes(here, 1)),
        ]
        flow_post, order_post = collide(
            comps,
            lambda i: side_ref[side_rows(comps.index(i)), :],
            lambda i: side_ref[side_rows(AT_ORDER + comps.index(i)), :],
            side_ref[side_rows(AT_MOMENTS), :],
            [side_ref[side_rows(AT_MOMENTS + 1 + d), :] for d in range(3)],
            outer[0],
            here,
            force,
        )
        for index, i in enumerate(comps):
            out_ref[index] = flow_post[i]
            out_ref[5 + index] = order_post[i]
        edge_ref[0 if inward == 1 else 1] = here


def plane_potential(phase_ref, low_ref, high_ref, x):
    cells = phase_ref[x]
    around = [
        phase_ref[x - 1],
        phase_ref[x + 1],
        rows_before(cells, side_row(low_ref, AT_PHASE, x)),
        rows_after(cells, side_row(high_ref, AT_PHASE, x)),
        roll_lanes(cells, 1),
        roll_lanes(cells, -1),
    ]
    return potential_of(cells, around)


def collide_plane(x, skip, flow_ref, order_ref, phase_ref, potential_ref, edge_ref, low_side, high_side, flow_out, order_out):
    here = potential_ref[x + 1]
    phase = phase_ref[x]
    half = -0.5 * phase
    along_y = rows_after(here, edge_ref[1, pl.ds(x, 1), :]) - rows_before(here, edge_ref[0, pl.ds(x, 1), :])
    force = [
        half * (potential_ref[x + 2] - potential_ref[x]),
        half * along_y,
        half * (roll_lanes(here, -1) - roll_lanes(here, 1)),
    ]
    density, momentum = moments(lambda i: flow_ref[i, x])
    flow_post, order_post = collide(
        tuple(i for i in range(VELS) if VELOCITY_X[i] == 0 or VELOCITY_X[i] != skip),
        lambda i: flow_ref[i, x],
        lambda i: order_ref[i, x],
        density,
        momentum,
        phase,
        here,
        force,
    )

    def moved(i, cells, first):
        if VELOCITY_Y[i] == 1:
            cells = rows_before(cells, low_side[first + UP_Y.index(i), pl.ds(x, 1), :])
        elif VELOCITY_Y[i] == -1:
            cells = rows_after(cells, high_side[first + DOWN_Y.index(i), pl.ds(x, 1), :])
        if VELOCITY_Z[i] != 0:
            cells = roll_lanes(cells, VELOCITY_Z[i])
        return cells

    for i in flow_post:
        target = x + VELOCITY_X[i]
        flow_out[i, target] = moved(i, flow_post[i], 0)
        order_out[i, target] = moved(i, order_post[i], 5)


def main_kernel(
    offset_ref, flow_ref, order_ref, low_ref, high_ref, minus_ref, same_ref, plus_ref, odd_ref, flow_hbm_out, order_hbm_out,
    flow_out, order_out, phase_ref, below_ref, above_ref, wide_ref, ghost_ref, potential_ref, low_side, high_side, edge_ref,
    flow_out_sems, order_out_sems,
):
    for x in range(PLANES):
        add_phase(phase_ref, order_ref, x)
    slab = lax.axis_index("gx")
    is_even = slab % 2 == 0
    inner = lax.rem(offset_ref[even_boundary(slab)] + 5, ROWS)
    blocks = [
        lambda at: jnp.where(is_even, minus_ref[at], plus_ref[at]),
        lambda at: same_ref[at],
        lambda at: jnp.where(is_even, plus_ref[at], minus_ref[at]),
    ]
    cut_window(blocks, jnp.where(is_even, inner, 9 - inner), above_ref)
    for index in range(PAYLOAD):
        even, odd = above_ref[index], odd_ref[index]
        below_ref[index] = jnp.where(is_even, odd, even)
        above_ref[index] = jnp.where(is_even, even, odd)

    for index, plane in enumerate((0, 1, PLANES - 1, PLANES - 2)):
        wide_ref[index] = jnp.zeros((WINDOW, LANES), jnp.float32)
        for d in range(3):
            wide_ref[index, 3 - d : 4 - d, :] = side_row(low_ref, AT_PHASE + d, plane)
            wide_ref[index, 12 + d : 13 + d, :] = side_row(high_ref, AT_PHASE + d, plane)
        wide_ref[index, 4:12, :] = phase_ref[plane]
    below = ghost_plane(below_ref, UP_X, wide_ref[0], wide_ref[1], 1.0 - SHIFT_FRACTION, WALL_SPEED)
    above = ghost_plane(above_ref, DOWN_X, wide_ref[2], wide_ref[3], SHIFT_FRACTION, -WALL_SPEED)
    for index in range(5):
        ghost_ref[index] = below[3][index]
        ghost_ref[5 + index] = below[4][index]
        ghost_ref[10 + index] = above[3][index]
        ghost_ref[15 + index] = above[4][index]

    def ghost_row(ghost):
        return lambda which, own_row: ghost[2 * which][own_row + WINDOW_PAD : own_row + WINDOW_PAD + 1, :]

    collide_sides(
        phase_ref, low_ref, high_ref, ghost_row(below), ghost_row(above), low_side, high_side, edge_ref
    )
    wide_ref[0] = below[1]
    wide_ref[1] = below[2]
    wide_ref[2] = above[1]
    wide_ref[3] = above[2]
    potential_ref[1] = wide_ref[0, 4:12, :]
    potential_ref[0] = wide_ref[1, 4:12, :]
    potential_ref[PLANES] = wide_ref[2, 4:12, :]
    potential_ref[PLANES + 1] = wide_ref[3, 4:12, :]
    for x in range(1, PLANES - 1):
        potential_ref[x + 1] = plane_potential(phase_ref, low_ref, high_ref, x)
    for comps, first, target in ((UP_X, 0, 0), (DOWN_X, 10, PLANES - 1)):
        for index, i in enumerate(comps):
            start = WINDOW_PAD - VELOCITY_Y[i]
            for out_ref, at in ((flow_out, first + index), (order_out, first + 5 + index)):
                cells = ghost_ref[at, start : start + ROWS, :]
                if VELOCITY_Z[i] != 0:
                    cells = roll_lanes(cells, VELOCITY_Z[i])
                out_ref[i, target] = cells
    flow_writes = plane_copies(flow_out, flow_hbm_out, flow_out_sems, QUARTERS)
    order_writes = plane_copies(order_out, order_hbm_out, order_out_sems, QUARTERS)

    def one_plane(x, skip):
        collide_plane(
            x, skip, flow_ref, order_ref, phase_ref, potential_ref, edge_ref, low_side, high_side, flow_out, order_out
        )

    def step(x, carry):
        one_plane(x, 0)
        for quarter, (first, count) in enumerate(QUARTERS[:-1]):

            @pl.when(x == first + count)
            def _(quarter=quarter):
                flow_writes[quarter].start()
                order_writes[quarter].start()

        return carry

    one_plane(0, -1)
    lax.fori_loop(1, PLANES - 1, step, 0)
    one_plane(PLANES - 1, 1)
    flow_writes[-1].start()
    order_writes[-1].start()
    for copy in flow_writes + order_writes:
        copy.wait()


def vmem(count):
    return [pl.BlockSpec(memory_space=pltpu.VMEM)] * count


def params(limit):
    return pltpu.CompilerParams(vmem_limit_bytes=limit)


def f32(*shape):
    return jax.ShapeDtypeStruct(shape, jnp.float32)


def shift_pairs(count, step):
    return [(i, (i + step) % count) for i in range(count)]


def swap_pairs(slabs, strips, first, step):
    pairs = []
    for low in range(first, slabs, 2):
        high = (low + 1) % slabs
        for strip in range(strips):
            other = (strip + step) % strips
            pairs.append((low * strips + strip, high * strips + other))
            pairs.append((high * strips + other, low * strips + strip))
    return pairs


def hbm(count):
    return [pl.BlockSpec(memory_space=pltpu.HBM)] * count


def smem():
    return [pl.BlockSpec(memory_space=pltpu.SMEM)]


def scratch(*shape):
    return pltpu.VMEM(shape, jnp.float32)


def sems(count):
    return pltpu.SemaphoreType.DMA((count,))


def main_planes(plane_offsets, flow, order, from_low, from_high, blocks, odd):
    return pl.pallas_call(
        main_kernel,
        out_shape=(f32(*flow.shape), f32(*order.shape)),
        in_specs=smem() + vmem(8),
        out_specs=tuple(hbm(2)),
        scratch_shapes=[
            scratch(*flow.shape),
            scratch(*order.shape),
            scratch(PLANES, ROWS, LANES),
            scratch(PAYLOAD, WINDOW, LANES),
            scratch(PAYLOAD, WINDOW, LANES),
            scratch(4, WINDOW, LANES),
            scratch(20, WINDOW, LANES),
            scratch(PLANES + 2, ROWS, LANES),
            scratch(10, PLANES, LANES),
            scratch(10, PLANES, LANES),
            scratch(2, PLANES, LANES),
            sems(len(QUARTERS)),
            sems(len(QUARTERS)),
        ],
        compiler_params=params(MAIN_VMEM),
        name="collide_stream",
    )(plane_offsets, flow, order, from_low, from_high, *blocks, odd)


def shards(populations, order_pops, plane_offsets):
    slabs, strips = lax.axis_size("gx"), lax.axis_size("gy")
    slab = lax.axis_index("gx").astype(jnp.uint32)

    def step_at(boundary):
        offset = lax.dynamic_index_in_dim(plane_offsets, boundary, keepdims=False).astype(jnp.uint32)
        return lax.rem((offset + jnp.uint32(5)) // jnp.uint32(ROWS), jnp.uint32(strips)).astype(jnp.int32)

    even_step = step_at(slab | jnp.uint32(1))
    odd_step = step_at(lax.rem(slab + (slab & jnp.uint32(1)), jnp.uint32(slabs)))

    even, own, to_low, to_high = pl.pallas_call(
        payload_kernel,
        out_shape=(
            f32(PAYLOAD, ROWS, LANES),
            f32(PAYLOAD, ROWS, LANES),
            f32(PACKED, LANES),
            f32(PACKED, LANES),
        ),
        in_specs=vmem(2),
        out_specs=tuple(vmem(4)),
        scratch_shapes=[scratch(PLANES, ROWS, LANES)],
        compiler_params=params(SMALL_VMEM),
        name="payloads",
    )(populations, order_pops)

    from_low = lax.ppermute(to_high, "gy", shift_pairs(strips, 1))
    from_high = lax.ppermute(to_low, "gy", shift_pairs(strips, -1))

    def even_branch(step):
        def run(mine):
            return tuple(
                lax.ppermute(mine, ("gx", "gy"), swap_pairs(slabs, strips, 0, step + d)) for d in (-1, 0, 1)
            )

        return run

    blocks = lax.switch(even_step, [even_branch(step) for step in range(strips)], even)
    from_low, from_high, blocks = lax.optimization_barrier((from_low, from_high, blocks))
    window = pl.pallas_call(
        window_kernel,
        out_shape=f32(PAYLOAD, WINDOW, LANES),
        in_specs=smem() + vmem(3),
        out_specs=vmem(1)[0],
        compiler_params=params(SMALL_VMEM),
        name="window",
    )(plane_offsets, from_low, own, from_high)

    def odd_branch(step):
        return lambda mine: lax.ppermute(mine, ("gx", "gy"), swap_pairs(slabs, strips, 1, step))

    odd = lax.switch(odd_step, [odd_branch(step) for step in range(strips)], window)
    return main_planes(plane_offsets, populations, order_pops, from_low, from_high, blocks, odd)


def solution(mesh):
    return jax.shard_map(
        shards,
        mesh=mesh,
        in_specs=(P(None, "gx", "gy", None), P(None, "gx", "gy", None), P()),
        out_specs=(P(None, "gx", "gy", None), P(None, "gx", "gy", None)),
        check_vma=False,
    )
```

```python
import jax
import jax.numpy as jnp
from jax import lax
from jax.experimental import pallas as pl
from jax.experimental.pallas import tpu as pltpu
from jax.sharding import PartitionSpec as P

SHIFT_FRACTION = 0.375
WALL_SPEED = 0.05
RELAX_FLOW = 0.8
RELAX_ORDER = 0.9
BULK_COEFF = 0.05
SURFACE_COEFF = 0.04
MOBILITY = 1.0
VELOCITY_X = (0, 1, -1, 0, 0, 0, 0, 1, -1, 1, -1, 1, -1, 1, -1, 0, 0, 0, 0)
VELOCITY_Y = (0, 0, 0, 1, -1, 0, 0, 1, -1, -1, 1, 0, 0, 0, 0, 1, -1, 1, -1)
VELOCITY_Z = (0, 0, 0, 0, 0, 1, -1, 0, 0, 0, 0, 1, -1, -1, 1, 1, -1, -1, 1)
WEIGHT_TABLE = (1.0 / 3.0,) + (1.0 / 18.0,) * 6 + (1.0 / 36.0,) * 12

VELS = 19
PLANES = 16
ROWS = 8
LANES = 128
UP_X = tuple(i for i in range(VELS) if VELOCITY_X[i] == 1)
DOWN_X = tuple(i for i in range(VELS) if VELOCITY_X[i] == -1)
UP_Y = tuple(i for i in range(VELS) if VELOCITY_Y[i] == 1)
DOWN_Y = tuple(i for i in range(VELS) if VELOCITY_Y[i] == -1)
PAYLOAD = 17
AT_MOMENTS = 5
AT_ORDER = 9
AT_PHASE = 14
WINDOW = 16
WINDOW_PAD = 4

SMALL_VMEM = 16 * 1024 * 1024
MAIN_VMEM = 24 * 1024 * 1024


def roll_rows(cells, step):
    return pltpu.roll(cells, step % cells.shape[0], 0)


def roll_lanes(cells, step):
    return pltpu.roll(cells, step % LANES, cells.ndim - 1)


def moments(flow):
    parts = [flow(i) for i in range(VELS)]
    density = parts[0]
    for part in parts[1:]:
        density = density + part
    speeds = []
    for table in (VELOCITY_X, VELOCITY_Y, VELOCITY_Z):
        plus = [parts[i] for i in range(VELS) if table[i] == 1]
        minus = [parts[i] for i in range(VELS) if table[i] == -1]
        total = plus[0] - minus[0]
        for a, b in zip(plus[1:], minus[1:]):
            total = total + (a - b)
        speeds.append(total)
    return density, speeds


def potential_of(phase, neighbours):
    around = neighbours[0]
    for cells in neighbours[1:]:
        around = around + cells
    bulk = BULK_COEFF * (phase * phase * phase - phase)
    return bulk - SURFACE_COEFF * (around - 6.0 * phase)


def dot_velocity(i, vector):
    total = None
    for sign, part in zip((VELOCITY_X[i], VELOCITY_Y[i], VELOCITY_Z[i]), vector):
        if sign == 0:
            continue
        if total is None:
            total = part if sign == 1 else -part
        else:
            total = total + part if sign == 1 else total - part
    return total


def collide(wanted, flow, order, density, momentum, phase, potential, force):
    inverse = 1.0 / density
    speed = [(momentum[d] + 0.5 * force[d]) * inverse for d in range(3)]
    source = 1.0 - 0.5 / RELAX_FLOW
    relaxed = density * (1.0 / RELAX_FLOW)
    speed_sq = speed[0] * speed[0] + speed[1] * speed[1] + speed[2] * speed[2]
    work = speed[0] * force[0] + speed[1] * force[1] + speed[2] * force[2]
    even = relaxed * (1.0 - 1.5 * speed_sq) - (3.0 * source) * work
    odd = [3.0 * (relaxed * speed[d] + source * force[d]) for d in range(3)]
    quad = [4.5 * relaxed * speed[d] + (9.0 * source) * force[d] for d in range(3)]
    order_even = (3.0 * MOBILITY / RELAX_ORDER) * potential
    carried = (3.0 / RELAX_ORDER) * phase
    order_odd = [carried * speed[d] for d in range(3)]
    flow_out, order_out = {}, {}
    keep_flow = 1.0 - 1.0 / RELAX_FLOW
    keep_order = 1.0 - 1.0 / RELAX_ORDER
    done = set()
    for i in wanted:
        if i in done:
            continue
        weight = WEIGHT_TABLE[i]
        if i == 0:
            flow_out[0] = keep_flow * flow(0) + weight * even
            rest = phase - (2.0 * MOBILITY) * potential
            order_out[0] = keep_order * order(0) + (1.0 / RELAX_ORDER) * rest
            continue
        first = i if i % 2 == 1 else i - 1
        pair_even = weight * (even + dot_velocity(first, speed) * dot_velocity(first, quad))
        pair_odd = weight * dot_velocity(first, odd)
        pair_order = weight * dot_velocity(first, order_odd)
        for member, sign in ((first, 1), (first + 1, -1)):
            if member not in wanted:
                continue
            done.add(member)
            both = pair_even + pair_odd if sign == 1 else pair_even - pair_odd
            flow_out[member] = keep_flow * flow(member) + both
            both = weight * order_even
            both = both + pair_order if sign == 1 else both - pair_order
            order_out[member] = keep_order * order(member) + both
    return flow_out, order_out


def add_phase(phase_ref, order_ref, x):
    total = order_ref[0, x]
    for i in range(1, VELS):
        total = total + order_ref[i, x]
    phase_ref[x] = total


def plane_copies(source, target, sems, pieces):
    return [
        pltpu.make_async_copy(source.at[:, pl.ds(first, count)], target.at[:, pl.ds(first, count)], sems.at[index])
        for index, (first, count) in enumerate(pieces)
    ]


STORES = ((3, 5), (8, 5), (0, 3), (PLANES - 3, 3))


def even_boundary(slab):
    return slab + 1 - slab % 2


def odd_boundary(slab, slabs):
    return lax.rem(slab + slab % 2, slabs)


PACKED = PAYLOAD * (ROWS + PLANES)


def block_rows(index):
    return pl.ds(index * ROWS, ROWS)


def side_rows(index):
    return pl.ds(PAYLOAD * ROWS + index * PLANES, PLANES)


def side_row(ref, index, x):
    return ref[pl.ds(PAYLOAD * ROWS + index * PLANES + x, 1), :]


def payload_kernel(flow_ref, order_ref, even_ref, odd_ref, low_ref, high_ref, phase_ref):
    is_even = lax.axis_index("gx") % 2 == 0
    for x in range(PLANES):
        add_phase(phase_ref, order_ref, x)
    sides = []
    for plane, inward, comps in ((PLANES - 1, -1, UP_X), (0, 1, DOWN_X)):
        density, momentum = moments(lambda i: flow_ref[i, plane])
        parts = [flow_ref[i, plane] for i in comps] + [density] + momentum
        parts += [order_ref[i, plane] for i in comps]
        parts += [phase_ref[plane + inward * d] for d in range(3)]
        sides.append(parts)
    for index, (last, first) in enumerate(zip(*sides)):
        even_ref[index] = jnp.where(is_even, last, first)
        odd = jnp.where(is_even, first, last)
        odd_ref[index] = odd
        low_ref[block_rows(index), :] = odd
        high_ref[block_rows(index), :] = odd
    for out_ref, row, inward, comps in ((high_ref, ROWS - 1, -1, UP_Y), (low_ref, 0, 1, DOWN_Y)):
        density, momentum = moments(lambda i: flow_ref[i, :, row, :])
        parts = [flow_ref[i, :, row, :] for i in comps] + [density] + momentum
        parts += [order_ref[i, :, row, :] for i in comps]
        parts += [phase_ref[:, row + inward * d, :] for d in range(3)]
        for index, part in enumerate(parts):
            out_ref[side_rows(index), :] = part


def window_kernel(offset_ref, before_ref, own_ref, after_ref, out_ref):
    slab = lax.axis_index("gx")
    inner = lax.rem(offset_ref[odd_boundary(slab, offset_ref.shape[0])] + 5, ROWS)

    blocks = [
        lambda index: before_ref[block_rows(index), :],
        lambda index: own_ref[index],
        lambda index: after_ref[block_rows(index), :],
    ]
    cut_window(blocks, jnp.where(slab % 2 == 0, inner, 9 - inner), out_ref)


def cut_window(blocks, start, window_ref):
    row = lax.broadcasted_iota(jnp.int32, (ROWS, LANES), 0)
    inner = lax.rem(start, ROWS)
    back = lax.rem(ROWS - inner, ROWS)
    early = row < ROWS - inner
    near = start < ROWS
    for index in range(PAYLOAD):
        rolled = [pltpu.roll(block(index), back, 0) for block in blocks]
        first = jnp.where(near, rolled[0], rolled[1])
        second = jnp.where(near, rolled[1], rolled[2])
        window_ref[index, 0:ROWS] = jnp.where(early, first, second)
        window_ref[index, ROWS : 2 * ROWS] = jnp.where(early, second, rolled[2])


def ghost_plane(window_ref, comps, own, own_next, weight, kick_speed):
    other = 1.0 - weight

    def sheared(cells):
        return weight * cells + other * roll_rows(cells, 1)

    def seen(cells):
        return other * roll_rows(cells, -1) + weight * cells

    def sides(cells):
        return [roll_rows(cells, 1), roll_rows(cells, -1), roll_lanes(cells, 1), roll_lanes(cells, -1)]

    near, second, third = [window_ref[AT_PHASE + d] for d in range(3)]
    ghost_phase = sheared(near)
    own_potential = potential_of(own, [own_next, ghost_phase] + sides(own))
    near_potential = potential_of(near, [second, seen(own)] + sides(near))
    second_potential = potential_of(second, [third, near] + sides(second))
    beyond = seen(own_potential)
    outward = 1.0 if VELOCITY_X[comps[0]] == 1 else -1.0
    half = -0.5 * near
    force = [
        outward * half * (beyond - second_potential),
        half * (roll_rows(near_potential, -1) - roll_rows(near_potential, 1)),
        half * (roll_lanes(near_potential, -1) - roll_lanes(near_potential, 1)),
    ]
    density = window_ref[AT_MOMENTS]
    momentum = [window_ref[AT_MOMENTS + 1 + d] for d in range(3)]
    flow_out, order_out = collide(
        comps,
        lambda i: window_ref[comps.index(i)],
        lambda i: window_ref[AT_ORDER + comps.index(i)],
        density,
        momentum,
        near,
        near_potential,
        force,
    )
    flow_ghost = []
    for i in comps:
        cells = flow_out[i]
        if VELOCITY_Y[i] != 0:
            cells = cells + (WEIGHT_TABLE[i] * 3.0 * VELOCITY_Y[i] * kick_speed) * density
        flow_ghost.append(sheared(cells))
    order_ghost = [sheared(order_out[i]) for i in comps]
    return ghost_phase, own_potential, sheared(near_potential), flow_ghost, order_ghost


def rows_before(cells, line):
    row = lax.broadcasted_iota(jnp.int32, (ROWS, LANES), 0)
    return jnp.where(row == 0, line, roll_rows(cells, 1))


def rows_after(cells, line):
    row = lax.broadcasted_iota(jnp.int32, (ROWS, LANES), 0)
    return jnp.where(row == ROWS - 1, line, roll_rows(cells, -1))


def collide_sides(phase_ref, low_ref, high_ref, below, above, low_side, high_side, edge_ref):
    plane_at = lax.broadcasted_iota(jnp.int32, (PLANES, LANES), 0)

    def across(cells, which, own_row):
        before, after = roll_rows(cells, 1), roll_rows(cells, -1)
        if below is not None:
            before = jnp.where(plane_at == 0, below(which, own_row), before)
            after = jnp.where(plane_at == PLANES - 1, above(which, own_row), after)
        return before, after

    for side_ref, out_ref, edge, beside, inward, comps in (
        (low_ref, low_side, 0, -1, 1, UP_Y),
        (high_ref, high_side, ROWS - 1, ROWS, -1, DOWN_Y),
    ):
        own = [phase_ref[:, edge + inward * d, :] for d in range(2)]
        outer = [side_ref[side_rows(AT_PHASE + d), :] for d in range(3)]
        lines = [own[1], own[0]] + outer
        potentials = []
        for index in range(1, 4):
            cells = lines[index]
            around = list(across(cells, 0, edge + inward * (1 - index)))
            around += [lines[index - 1], lines[index + 1], roll_lanes(cells, 1), roll_lanes(cells, -1)]
            potentials.append(potential_of(cells, around))
        inside, here, outside = potentials
        before, after = across(here, 1, beside)
        half = -0.5 * outer[0]
        force = [
            half * (after - before),
            (inward * half) * (inside - outside),
            half * (roll_lanes(here, -1) - roll_lanes(here, 1)),
        ]
        flow_post, order_post = collide(
            comps,
            lambda i: side_ref[side_rows(comps.index(i)), :],
            lambda i: side_ref[side_rows(AT_ORDER + comps.index(i)), :],
            side_ref[side_rows(AT_MOMENTS), :],
            [side_ref[side_rows(AT_MOMENTS + 1 + d), :] for d in range(3)],
            outer[0],
            here,
            force,
        )
        for index, i in enumerate(comps):
            out_ref[index] = flow_post[i]
            out_ref[5 + index] = order_post[i]
        edge_ref[0 if inward == 1 else 1] = here


def plane_potential(phase_ref, low_ref, high_ref, x):
    cells = phase_ref[x]
    around = [
        phase_ref[x - 1],
        phase_ref[x + 1],
        rows_before(cells, side_row(low_ref, AT_PHASE, x)),
        rows_after(cells, side_row(high_ref, AT_PHASE, x)),
        roll_lanes(cells, 1),
        roll_lanes(cells, -1),
    ]
    return potential_of(cells, around)


def collide_plane(x, skip, flow_ref, order_ref, phase_ref, potential_ref, edge_ref, low_side, high_side, flow_out, order_out):
    here = potential_ref[x + 1]
    phase = phase_ref[x]
    half = -0.5 * phase
    along_y = rows_after(here, edge_ref[1, pl.ds(x, 1), :]) - rows_before(here, edge_ref[0, pl.ds(x, 1), :])
    force = [
        half * (potential_ref[x + 2] - potential_ref[x]),
        half * along_y,
        half * (roll_lanes(here, -1) - roll_lanes(here, 1)),
    ]
    density, momentum = moments(lambda i: flow_ref[i, x])
    flow_post, order_post = collide(
        tuple(i for i in range(VELS) if VELOCITY_X[i] == 0 or VELOCITY_X[i] != skip),
        lambda i: flow_ref[i, x],
        lambda i: order_ref[i, x],
        density,
        momentum,
        phase,
        here,
        force,
    )

    def moved(i, cells, first):
        if VELOCITY_Y[i] == 1:
            cells = rows_before(cells, low_side[first + UP_Y.index(i), pl.ds(x, 1), :])
        elif VELOCITY_Y[i] == -1:
            cells = rows_after(cells, high_side[first + DOWN_Y.index(i), pl.ds(x, 1), :])
        if VELOCITY_Z[i] != 0:
            cells = roll_lanes(cells, VELOCITY_Z[i])
        return cells

    for i in flow_post:
        target = x + VELOCITY_X[i]
        flow_out[i, target] = moved(i, flow_post[i], 0)
        order_out[i, target] = moved(i, order_post[i], 5)


def main_kernel(
    offset_ref, flow_ref, order_ref, low_ref, high_ref, minus_hbm, same_hbm, plus_hbm, odd_hbm, flow_hbm_out, order_hbm_out,
    minus_ref, same_ref, plus_ref, odd_ref, flow_out, order_out, phase_ref, below_ref, above_ref, wide_ref, ghost_ref, potential_ref, low_side, high_side, edge_ref,
    arrival_sems, flow_out_sems, order_out_sems,
):
    pairs = ((minus_hbm, minus_ref), (same_hbm, same_ref), (plus_hbm, plus_ref), (odd_hbm, odd_ref))
    arrivals = [pltpu.make_async_copy(a, b, arrival_sems.at[index]) for index, (a, b) in enumerate(pairs)]
    for copy in arrivals:
        copy.start()
    flow_writes = plane_copies(flow_out, flow_hbm_out, flow_out_sems, STORES)
    order_writes = plane_copies(order_out, order_hbm_out, order_out_sems, STORES)

    def one_plane(x, skip):
        collide_plane(
            x, skip, flow_ref, order_ref, phase_ref, potential_ref, edge_ref, low_side, high_side, flow_out, order_out
        )

    for x in range(PLANES):
        add_phase(phase_ref, order_ref, x)
    collide_sides(phase_ref, low_ref, high_ref, None, None, low_side, high_side, edge_ref)
    for x in range(1, PLANES - 1):
        potential_ref[x + 1] = plane_potential(phase_ref, low_ref, high_ref, x)

    def step(x, carry):
        one_plane(x, 0)
        for part, (first, count) in enumerate(STORES[:-2]):

            @pl.when(x == first + count)
            def _(part=part):
                flow_writes[part].start()
                order_writes[part].start()

        return carry

    lax.fori_loop(2, PLANES - 2, step, 0)
    for copy in arrivals:
        copy.wait()
    slab = lax.axis_index("gx")
    is_even = slab % 2 == 0
    inner = lax.rem(offset_ref[even_boundary(slab)] + 5, ROWS)
    blocks = [
        lambda at: jnp.where(is_even, minus_ref[at], plus_ref[at]),
        lambda at: same_ref[at],
        lambda at: jnp.where(is_even, plus_ref[at], minus_ref[at]),
    ]
    cut_window(blocks, jnp.where(is_even, inner, 9 - inner), above_ref)
    for index in range(PAYLOAD):
        even, odd = above_ref[index], odd_ref[index]
        below_ref[index] = jnp.where(is_even, odd, even)
        above_ref[index] = jnp.where(is_even, even, odd)

    for index, plane in enumerate((0, 1, PLANES - 1, PLANES - 2)):
        wide_ref[index] = jnp.zeros((WINDOW, LANES), jnp.float32)
        for d in range(3):
            wide_ref[index, 3 - d : 4 - d, :] = side_row(low_ref, AT_PHASE + d, plane)
            wide_ref[index, 12 + d : 13 + d, :] = side_row(high_ref, AT_PHASE + d, plane)
        wide_ref[index, 4:12, :] = phase_ref[plane]
    below = ghost_plane(below_ref, UP_X, wide_ref[0], wide_ref[1], 1.0 - SHIFT_FRACTION, WALL_SPEED)
    above = ghost_plane(above_ref, DOWN_X, wide_ref[2], wide_ref[3], SHIFT_FRACTION, -WALL_SPEED)
    for index in range(5):
        ghost_ref[index] = below[3][index]
        ghost_ref[5 + index] = below[4][index]
        ghost_ref[10 + index] = above[3][index]
        ghost_ref[15 + index] = above[4][index]

    def ghost_row(ghost):
        return lambda which, own_row: ghost[2 * which][own_row + WINDOW_PAD : own_row + WINDOW_PAD + 1, :]

    collide_sides(
        phase_ref, low_ref, high_ref, ghost_row(below), ghost_row(above), low_side, high_side, edge_ref
    )
    wide_ref[0] = below[1]
    wide_ref[1] = below[2]
    wide_ref[2] = above[1]
    wide_ref[3] = above[2]
    potential_ref[1] = wide_ref[0, 4:12, :]
    potential_ref[0] = wide_ref[1, 4:12, :]
    potential_ref[PLANES] = wide_ref[2, 4:12, :]
    potential_ref[PLANES + 1] = wide_ref[3, 4:12, :]
    for comps, first, target in ((UP_X, 0, 0), (DOWN_X, 10, PLANES - 1)):
        for index, i in enumerate(comps):
            start = WINDOW_PAD - VELOCITY_Y[i]
            for out_ref, at in ((flow_out, first + index), (order_out, first + 5 + index)):
                cells = ghost_ref[at, start : start + ROWS, :]
                if VELOCITY_Z[i] != 0:
                    cells = roll_lanes(cells, VELOCITY_Z[i])
                out_ref[i, target] = cells
    one_plane(0, -1)
    one_plane(1, 0)
    flow_writes[-2].start()
    order_writes[-2].start()
    one_plane(PLANES - 2, 0)
    one_plane(PLANES - 1, 1)
    flow_writes[-1].start()
    order_writes[-1].start()
    for copy in flow_writes + order_writes:
        copy.wait()


def vmem(count):
    return [pl.BlockSpec(memory_space=pltpu.VMEM)] * count


def params(limit):
    return pltpu.CompilerParams(vmem_limit_bytes=limit)


def f32(*shape):
    return jax.ShapeDtypeStruct(shape, jnp.float32)


def shift_pairs(count, step):
    return [(i, (i + step) % count) for i in range(count)]


def swap_pairs(slabs, strips, first, step):
    pairs = []
    for low in range(first, slabs, 2):
        high = (low + 1) % slabs
        for strip in range(strips):
            other = (strip + step) % strips
            pairs.append((low * strips + strip, high * strips + other))
            pairs.append((high * strips + other, low * strips + strip))
    return pairs


def hbm(count):
    return [pl.BlockSpec(memory_space=pltpu.HBM)] * count


def smem():
    return [pl.BlockSpec(memory_space=pltpu.SMEM)]


def scratch(*shape):
    return pltpu.VMEM(shape, jnp.float32)


def sems(count):
    return pltpu.SemaphoreType.DMA((count,))


def main_planes(plane_offsets, flow, order, from_low, from_high, blocks, odd):
    return pl.pallas_call(
        main_kernel,
        out_shape=(f32(*flow.shape), f32(*order.shape)),
        in_specs=smem() + vmem(4) + hbm(4),
        out_specs=tuple(hbm(2)),
        scratch_shapes=[
            scratch(PAYLOAD, ROWS, LANES),
            scratch(PAYLOAD, ROWS, LANES),
            scratch(PAYLOAD, ROWS, LANES),
            scratch(PAYLOAD, WINDOW, LANES),
            scratch(*flow.shape),
            scratch(*order.shape),
            scratch(PLANES, ROWS, LANES),
            scratch(PAYLOAD, WINDOW, LANES),
            scratch(PAYLOAD, WINDOW, LANES),
            scratch(4, WINDOW, LANES),
            scratch(20, WINDOW, LANES),
            scratch(PLANES + 2, ROWS, LANES),
            scratch(10, PLANES, LANES),
            scratch(10, PLANES, LANES),
            scratch(2, PLANES, LANES),
            sems(4),
            sems(len(STORES)),
            sems(len(STORES)),
        ],
        compiler_params=params(MAIN_VMEM),
        name="collide_stream",
    )(plane_offsets, flow, order, from_low, from_high, *blocks, odd)


def shards(populations, order_pops, plane_offsets):
    slabs, strips = lax.axis_size("gx"), lax.axis_size("gy")
    slab = lax.axis_index("gx").astype(jnp.uint32)

    shifts = ((plane_offsets + 5) // ROWS) % strips

    def step_at(boundary):
        return lax.dynamic_index_in_dim(shifts, boundary, keepdims=False)

    even_step = step_at(slab | jnp.uint32(1))
    odd_step = step_at(lax.rem(slab + (slab & jnp.uint32(1)), jnp.uint32(slabs)))

    even, own, to_low, to_high = pl.pallas_call(
        payload_kernel,
        out_shape=(
            f32(PAYLOAD, ROWS, LANES),
            f32(PAYLOAD, ROWS, LANES),
            f32(PACKED, LANES),
            f32(PACKED, LANES),
        ),
        in_specs=vmem(2),
        out_specs=tuple(vmem(4)),
        scratch_shapes=[scratch(PLANES, ROWS, LANES)],
        compiler_params=params(SMALL_VMEM),
        name="payloads",
    )(populations, order_pops)

    from_low = lax.ppermute(to_high, "gy", shift_pairs(strips, 1))
    from_high = lax.ppermute(to_low, "gy", shift_pairs(strips, -1))

    def even_branch(step):
        def run(mine):
            return tuple(
                lax.ppermute(mine, ("gx", "gy"), swap_pairs(slabs, strips, 0, step + d)) for d in (-1, 0, 1)
            )

        return run

    blocks = lax.switch(even_step, [even_branch(step) for step in range(strips)], even)
    from_low, from_high, blocks = lax.optimization_barrier((from_low, from_high, blocks))
    window = pl.pallas_call(
        window_kernel,
        out_shape=f32(PAYLOAD, WINDOW, LANES),
        in_specs=smem() + vmem(3),
        out_specs=vmem(1)[0],
        compiler_params=params(SMALL_VMEM),
        name="window",
    )(plane_offsets, from_low, own, from_high)

    def odd_branch(step):
        return lambda mine: lax.ppermute(mine, ("gx", "gy"), swap_pairs(slabs, strips, 1, step))

    odd = lax.switch(odd_step, [odd_branch(step) for step in range(strips)], window)
    return main_planes(plane_offsets, populations, order_pops, from_low, from_high, blocks, odd)


def solution(mesh):
    return jax.shard_map(
        shards,
        mesh=mesh,
        in_specs=(P(None, "gx", "gy", None), P(None, "gx", "gy", None), P()),
        out_specs=(P(None, "gx", "gy", None), P(None, "gx", "gy", None)),
        check_vma=False,
    )
```

```python
import jax
import jax.numpy as jnp
from jax import lax
from jax.experimental import pallas as pl
from jax.experimental.pallas import tpu as pltpu
from jax.sharding import PartitionSpec as P

SHIFT_FRACTION = 0.375
WALL_SPEED = 0.05
RELAX_FLOW = 0.8
RELAX_ORDER = 0.9
BULK_COEFF = 0.05
SURFACE_COEFF = 0.04
MOBILITY = 1.0
VELOCITY_X = (0, 1, -1, 0, 0, 0, 0, 1, -1, 1, -1, 1, -1, 1, -1, 0, 0, 0, 0)
VELOCITY_Y = (0, 0, 0, 1, -1, 0, 0, 1, -1, -1, 1, 0, 0, 0, 0, 1, -1, 1, -1)
VELOCITY_Z = (0, 0, 0, 0, 0, 1, -1, 0, 0, 0, 0, 1, -1, -1, 1, 1, -1, -1, 1)
WEIGHT_TABLE = (1.0 / 3.0,) + (1.0 / 18.0,) * 6 + (1.0 / 36.0,) * 12

VELS = 19
PLANES = 16
ROWS = 8
LANES = 128
UP_X = tuple(i for i in range(VELS) if VELOCITY_X[i] == 1)
DOWN_X = tuple(i for i in range(VELS) if VELOCITY_X[i] == -1)
UP_Y = tuple(i for i in range(VELS) if VELOCITY_Y[i] == 1)
DOWN_Y = tuple(i for i in range(VELS) if VELOCITY_Y[i] == -1)
PAYLOAD = 17
AT_MOMENTS = 5
AT_ORDER = 9
AT_PHASE = 14
WINDOW = 16
WINDOW_PAD = 4

SMALL_VMEM = 16 * 1024 * 1024
MAIN_VMEM = 24 * 1024 * 1024


def roll_rows(cells, step):
    return pltpu.roll(cells, step % cells.shape[0], 0)


def roll_lanes(cells, step):
    return pltpu.roll(cells, step % LANES, cells.ndim - 1)


def moments(flow):
    parts = [flow(i) for i in range(VELS)]
    density = parts[0]
    for part in parts[1:]:
        density = density + part
    speeds = []
    for table in (VELOCITY_X, VELOCITY_Y, VELOCITY_Z):
        plus = [parts[i] for i in range(VELS) if table[i] == 1]
        minus = [parts[i] for i in range(VELS) if table[i] == -1]
        total = plus[0] - minus[0]
        for a, b in zip(plus[1:], minus[1:]):
            total = total + (a - b)
        speeds.append(total)
    return density, speeds


def potential_of(phase, neighbours):
    around = neighbours[0]
    for cells in neighbours[1:]:
        around = around + cells
    bulk = BULK_COEFF * (phase * phase * phase - phase)
    return bulk - SURFACE_COEFF * (around - 6.0 * phase)


def dot_velocity(i, vector):
    total = None
    for sign, part in zip((VELOCITY_X[i], VELOCITY_Y[i], VELOCITY_Z[i]), vector):
        if sign == 0:
            continue
        if total is None:
            total = part if sign == 1 else -part
        else:
            total = total + part if sign == 1 else total - part
    return total


def collide(wanted, flow, order, density, momentum, phase, potential, force):
    inverse = 1.0 / density
    speed = [(momentum[d] + 0.5 * force[d]) * inverse for d in range(3)]
    source = 1.0 - 0.5 / RELAX_FLOW
    relaxed = density * (1.0 / RELAX_FLOW)
    speed_sq = speed[0] * speed[0] + speed[1] * speed[1] + speed[2] * speed[2]
    work = speed[0] * force[0] + speed[1] * force[1] + speed[2] * force[2]
    even = relaxed * (1.0 - 1.5 * speed_sq) - (3.0 * source) * work
    odd = [3.0 * (relaxed * speed[d] + source * force[d]) for d in range(3)]
    quad = [4.5 * relaxed * speed[d] + (9.0 * source) * force[d] for d in range(3)]
    order_even = (3.0 * MOBILITY / RELAX_ORDER) * potential
    carried = (3.0 / RELAX_ORDER) * phase
    order_odd = [carried * speed[d] for d in range(3)]
    flow_out, order_out = {}, {}
    keep_flow = 1.0 - 1.0 / RELAX_FLOW
    keep_order = 1.0 - 1.0 / RELAX_ORDER
    done = set()
    for i in wanted:
        if i in done:
            continue
        weight = WEIGHT_TABLE[i]
        if i == 0:
            flow_out[0] = keep_flow * flow(0) + weight * even
            rest = phase - (2.0 * MOBILITY) * potential
            order_out[0] = keep_order * order(0) + (1.0 / RELAX_ORDER) * rest
            continue
        first = i if i % 2 == 1 else i - 1
        pair_even = weight * (even + dot_velocity(first, speed) * dot_velocity(first, quad))
        pair_odd = weight * dot_velocity(first, odd)
        pair_order = weight * dot_velocity(first, order_odd)
        for member, sign in ((first, 1), (first + 1, -1)):
            if member not in wanted:
                continue
            done.add(member)
            both = pair_even + pair_odd if sign == 1 else pair_even - pair_odd
            flow_out[member] = keep_flow * flow(member) + both
            both = weight * order_even
            both = both + pair_order if sign == 1 else both - pair_order
            order_out[member] = keep_order * order(member) + both
    return flow_out, order_out


def add_phase(phase_ref, order_ref, x):
    total = order_ref[0, x]
    for i in range(1, VELS):
        total = total + order_ref[i, x]
    phase_ref[x] = total


def plane_copies(source, target, sems, pieces):
    return [
        pltpu.make_async_copy(source.at[:, pl.ds(first, count)], target.at[:, pl.ds(first, count)], sems.at[index])
        for index, (first, count) in enumerate(pieces)
    ]


SENT_ROWS = 11
SENT_SKIP = 2
SENT = ROWS + AT_PHASE * SENT_ROWS + 3 * (WINDOW - 1) + 1


def window_row(index):
    if index < AT_PHASE:
        return ROWS - SENT_SKIP + index * SENT_ROWS
    return ROWS + AT_PHASE * SENT_ROWS + (index - AT_PHASE) * (WINDOW - 1)


STORES = ((3, 5), (8, 5), (0, 3), (PLANES - 3, 3))


def even_boundary(slab):
    return slab + 1 - slab % 2


def odd_boundary(slab, slabs):
    return lax.rem(slab + slab % 2, slabs)


PACKED = PAYLOAD * (ROWS + PLANES)


def block_rows(index):
    return pl.ds(index * ROWS, ROWS)


def side_rows(index):
    return pl.ds(PAYLOAD * ROWS + index * PLANES, PLANES)


def side_row(ref, index, x):
    return ref[pl.ds(PAYLOAD * ROWS + index * PLANES + x, 1), :]


def payload_kernel(flow_ref, order_ref, even_ref, odd_ref, low_ref, high_ref, phase_ref):
    is_even = lax.axis_index("gx") % 2 == 0
    for x in range(PLANES):
        add_phase(phase_ref, order_ref, x)
    sides = []
    for plane, inward, comps in ((PLANES - 1, -1, UP_X), (0, 1, DOWN_X)):
        density, momentum = moments(lambda i: flow_ref[i, plane])
        parts = [flow_ref[i, plane] for i in comps] + [density] + momentum
        parts += [order_ref[i, plane] for i in comps]
        parts += [phase_ref[plane + inward * d] for d in range(3)]
        sides.append(parts)
    for index, (last, first) in enumerate(zip(*sides)):
        even_ref[index] = jnp.where(is_even, last, first)
        odd = jnp.where(is_even, first, last)
        odd_ref[index] = odd
        low_ref[block_rows(index), :] = odd
        high_ref[block_rows(index), :] = odd
    for out_ref, row, inward, comps in ((high_ref, ROWS - 1, -1, UP_Y), (low_ref, 0, 1, DOWN_Y)):
        density, momentum = moments(lambda i: flow_ref[i, :, row, :])
        parts = [flow_ref[i, :, row, :] for i in comps] + [density] + momentum
        parts += [order_ref[i, :, row, :] for i in comps]
        parts += [phase_ref[:, row + inward * d, :] for d in range(3)]
        for index, part in enumerate(parts):
            out_ref[side_rows(index), :] = part


def window_kernel(offset_ref, before_ref, own_ref, after_ref, out_ref, window_ref):
    slab = lax.axis_index("gx")
    inner = lax.rem(offset_ref[odd_boundary(slab, offset_ref.shape[0])] + 5, ROWS)

    blocks = [
        lambda index: before_ref[block_rows(index), :],
        lambda index: own_ref[index],
        lambda index: after_ref[block_rows(index), :],
    ]
    cut_window(blocks, jnp.where(slab % 2 == 0, inner, 9 - inner), window_ref)
    out_ref[0:ROWS, :] = window_ref[0, 0:ROWS]
    for index in range(PAYLOAD):
        first, count = (SENT_SKIP, SENT_ROWS) if index < AT_PHASE else (0, WINDOW)
        start = window_row(index) + first
        out_ref[start : start + count, :] = window_ref[index, first : first + count, :]


def cut_window(blocks, start, window_ref):
    row = lax.broadcasted_iota(jnp.int32, (ROWS, LANES), 0)
    inner = lax.rem(start, ROWS)
    back = lax.rem(ROWS - inner, ROWS)
    early = row < ROWS - inner
    near = start < ROWS
    for index in range(PAYLOAD):
        rolled = [pltpu.roll(block(index), back, 0) for block in blocks]
        first = jnp.where(near, rolled[0], rolled[1])
        second = jnp.where(near, rolled[1], rolled[2])
        window_ref[index, 0:ROWS] = jnp.where(early, first, second)
        window_ref[index, ROWS : 2 * ROWS] = jnp.where(early, second, rolled[2])


def ghost_plane(window_ref, comps, own, own_next, weight, kick_speed):
    other = 1.0 - weight

    def sheared(cells):
        return weight * cells + other * roll_rows(cells, 1)

    def seen(cells):
        return other * roll_rows(cells, -1) + weight * cells

    def sides(cells):
        return [roll_rows(cells, 1), roll_rows(cells, -1), roll_lanes(cells, 1), roll_lanes(cells, -1)]

    near, second, third = [window_ref[AT_PHASE + d] for d in range(3)]
    ghost_phase = sheared(near)
    own_potential = potential_of(own, [own_next, ghost_phase] + sides(own))
    near_potential = potential_of(near, [second, seen(own)] + sides(near))
    second_potential = potential_of(second, [third, near] + sides(second))
    beyond = seen(own_potential)
    outward = 1.0 if VELOCITY_X[comps[0]] == 1 else -1.0
    half = -0.5 * near
    force = [
        outward * half * (beyond - second_potential),
        half * (roll_rows(near_potential, -1) - roll_rows(near_potential, 1)),
        half * (roll_lanes(near_potential, -1) - roll_lanes(near_potential, 1)),
    ]
    density = window_ref[AT_MOMENTS]
    momentum = [window_ref[AT_MOMENTS + 1 + d] for d in range(3)]
    flow_out, order_out = collide(
        comps,
        lambda i: window_ref[comps.index(i)],
        lambda i: window_ref[AT_ORDER + comps.index(i)],
        density,
        momentum,
        near,
        near_potential,
        force,
    )
    flow_ghost = []
    for i in comps:
        cells = flow_out[i]
        if VELOCITY_Y[i] != 0:
            cells = cells + (WEIGHT_TABLE[i] * 3.0 * VELOCITY_Y[i] * kick_speed) * density
        flow_ghost.append(sheared(cells))
    order_ghost = [sheared(order_out[i]) for i in comps]
    return ghost_phase, own_potential, sheared(near_potential), flow_ghost, order_ghost


def rows_before(cells, line):
    row = lax.broadcasted_iota(jnp.int32, (ROWS, LANES), 0)
    return jnp.where(row == 0, line, roll_rows(cells, 1))


def rows_after(cells, line):
    row = lax.broadcasted_iota(jnp.int32, (ROWS, LANES), 0)
    return jnp.where(row == ROWS - 1, line, roll_rows(cells, -1))


def collide_sides(phase_ref, low_ref, high_ref, below, above, low_side, high_side, edge_ref):
    plane_at = lax.broadcasted_iota(jnp.int32, (PLANES, LANES), 0)

    def across(cells, which, own_row):
        before, after = roll_rows(cells, 1), roll_rows(cells, -1)
        if below is not None:
            before = jnp.where(plane_at == 0, below(which, own_row), before)
            after = jnp.where(plane_at == PLANES - 1, above(which, own_row), after)
        return before, after

    for side_ref, out_ref, edge, beside, inward, comps in (
        (low_ref, low_side, 0, -1, 1, UP_Y),
        (high_ref, high_side, ROWS - 1, ROWS, -1, DOWN_Y),
    ):
        own = [phase_ref[:, edge + inward * d, :] for d in range(2)]
        outer = [side_ref[side_rows(AT_PHASE + d), :] for d in range(3)]
        lines = [own[1], own[0]] + outer
        potentials = []
        for index in range(1, 4):
            cells = lines[index]
            around = list(across(cells, 0, edge + inward * (1 - index)))
            around += [lines[index - 1], lines[index + 1], roll_lanes(cells, 1), roll_lanes(cells, -1)]
            potentials.append(potential_of(cells, around))
        inside, here, outside = potentials
        before, after = across(here, 1, beside)
        half = -0.5 * outer[0]
        force = [
            half * (after - before),
            (inward * half) * (inside - outside),
            half * (roll_lanes(here, -1) - roll_lanes(here, 1)),
        ]
        flow_post, order_post = collide(
            comps,
            lambda i: side_ref[side_rows(comps.index(i)), :],
            lambda i: side_ref[side_rows(AT_ORDER + comps.index(i)), :],
            side_ref[side_rows(AT_MOMENTS), :],
            [side_ref[side_rows(AT_MOMENTS + 1 + d), :] for d in range(3)],
            outer[0],
            here,
            force,
        )
        for index, i in enumerate(comps):
            out_ref[index] = flow_post[i]
            out_ref[5 + index] = order_post[i]
        edge_ref[0 if inward == 1 else 1] = here


def plane_potential(phase_ref, low_ref, high_ref, x):
    cells = phase_ref[x]
    around = [
        phase_ref[x - 1],
        phase_ref[x + 1],
        rows_before(cells, side_row(low_ref, AT_PHASE, x)),
        rows_after(cells, side_row(high_ref, AT_PHASE, x)),
        roll_lanes(cells, 1),
        roll_lanes(cells, -1),
    ]
    return potential_of(cells, around)


def collide_plane(x, skip, flow_ref, order_ref, phase_ref, potential_ref, edge_ref, low_side, high_side, flow_out, order_out):
    here = potential_ref[x + 1]
    phase = phase_ref[x]
    half = -0.5 * phase
    along_y = rows_after(here, edge_ref[1, pl.ds(x, 1), :]) - rows_before(here, edge_ref[0, pl.ds(x, 1), :])
    force = [
        half * (potential_ref[x + 2] - potential_ref[x]),
        half * along_y,
        half * (roll_lanes(here, -1) - roll_lanes(here, 1)),
    ]
    density, momentum = moments(lambda i: flow_ref[i, x])
    flow_post, order_post = collide(
        tuple(i for i in range(VELS) if VELOCITY_X[i] == 0 or VELOCITY_X[i] != skip),
        lambda i: flow_ref[i, x],
        lambda i: order_ref[i, x],
        density,
        momentum,
        phase,
        here,
        force,
    )

    def moved(i, cells, first):
        if VELOCITY_Y[i] == 1:
            cells = rows_before(cells, low_side[first + UP_Y.index(i), pl.ds(x, 1), :])
        elif VELOCITY_Y[i] == -1:
            cells = rows_after(cells, high_side[first + DOWN_Y.index(i), pl.ds(x, 1), :])
        if VELOCITY_Z[i] != 0:
            cells = roll_lanes(cells, VELOCITY_Z[i])
        return cells

    for i in flow_post:
        target = x + VELOCITY_X[i]
        flow_out[i, target] = moved(i, flow_post[i], 0)
        order_out[i, target] = moved(i, order_post[i], 5)


def main_kernel(
    offset_ref, flow_ref, order_ref, low_ref, high_ref, minus_hbm, same_hbm, plus_hbm, odd_hbm, flow_hbm_out, order_hbm_out,
    minus_ref, same_ref, plus_ref, odd_ref, flow_out, order_out, phase_ref, below_ref, above_ref, wide_ref, ghost_ref, potential_ref, low_side, high_side, edge_ref,
    arrival_sems, flow_out_sems, order_out_sems,
):
    pairs = ((minus_hbm, minus_ref), (same_hbm, same_ref), (plus_hbm, plus_ref), (odd_hbm, odd_ref))
    arrivals = [pltpu.make_async_copy(a, b, arrival_sems.at[index]) for index, (a, b) in enumerate(pairs)]
    for copy in arrivals:
        copy.start()
    flow_writes = plane_copies(flow_out, flow_hbm_out, flow_out_sems, STORES)
    order_writes = plane_copies(order_out, order_hbm_out, order_out_sems, STORES)

    def one_plane(x, skip):
        collide_plane(
            x, skip, flow_ref, order_ref, phase_ref, potential_ref, edge_ref, low_side, high_side, flow_out, order_out
        )

    for x in range(PLANES):
        add_phase(phase_ref, order_ref, x)
    collide_sides(phase_ref, low_ref, high_ref, None, None, low_side, high_side, edge_ref)
    for x in range(1, PLANES - 1):
        potential_ref[x + 1] = plane_potential(phase_ref, low_ref, high_ref, x)

    def step(x, carry):
        one_plane(x, 0)
        for part, (first, count) in enumerate(STORES[:-2]):

            @pl.when(x == first + count)
            def _(part=part):
                flow_writes[part].start()
                order_writes[part].start()

        return carry

    lax.fori_loop(2, PLANES - 2, step, 0)
    for copy in arrivals:
        copy.wait()
    slab = lax.axis_index("gx")
    is_even = slab % 2 == 0
    inner = lax.rem(offset_ref[even_boundary(slab)] + 5, ROWS)
    blocks = [
        lambda at: jnp.where(is_even, minus_ref[at], plus_ref[at]),
        lambda at: same_ref[at],
        lambda at: jnp.where(is_even, plus_ref[at], minus_ref[at]),
    ]
    cut_window(blocks, jnp.where(is_even, inner, 9 - inner), above_ref)
    for index in range(PAYLOAD):
        start = window_row(index)
        even, odd = above_ref[index], odd_ref[start : start + WINDOW, :]
        below_ref[index] = jnp.where(is_even, odd, even)
        above_ref[index] = jnp.where(is_even, even, odd)

    for index, plane in enumerate((0, 1, PLANES - 1, PLANES - 2)):
        wide_ref[index] = jnp.zeros((WINDOW, LANES), jnp.float32)
        for d in range(3):
            wide_ref[index, 3 - d : 4 - d, :] = side_row(low_ref, AT_PHASE + d, plane)
            wide_ref[index, 12 + d : 13 + d, :] = side_row(high_ref, AT_PHASE + d, plane)
        wide_ref[index, 4:12, :] = phase_ref[plane]
    below = ghost_plane(below_ref, UP_X, wide_ref[0], wide_ref[1], 1.0 - SHIFT_FRACTION, WALL_SPEED)
    above = ghost_plane(above_ref, DOWN_X, wide_ref[2], wide_ref[3], SHIFT_FRACTION, -WALL_SPEED)
    for index in range(5):
        ghost_ref[index] = below[3][index]
        ghost_ref[5 + index] = below[4][index]
        ghost_ref[10 + index] = above[3][index]
        ghost_ref[15 + index] = above[4][index]

    def ghost_row(ghost):
        return lambda which, own_row: ghost[2 * which][own_row + WINDOW_PAD : own_row + WINDOW_PAD + 1, :]

    collide_sides(
        phase_ref, low_ref, high_ref, ghost_row(below), ghost_row(above), low_side, high_side, edge_ref
    )
    wide_ref[0] = below[1]
    wide_ref[1] = below[2]
    wide_ref[2] = above[1]
    wide_ref[3] = above[2]
    potential_ref[1] = wide_ref[0, 4:12, :]
    potential_ref[0] = wide_ref[1, 4:12, :]
    potential_ref[PLANES] = wide_ref[2, 4:12, :]
    potential_ref[PLANES + 1] = wide_ref[3, 4:12, :]
    for comps, first, target in ((UP_X, 0, 0), (DOWN_X, 10, PLANES - 1)):
        for index, i in enumerate(comps):
            start = WINDOW_PAD - VELOCITY_Y[i]
            for out_ref, at in ((flow_out, first + index), (order_out, first + 5 + index)):
                cells = ghost_ref[at, start : start + ROWS, :]
                if VELOCITY_Z[i] != 0:
                    cells = roll_lanes(cells, VELOCITY_Z[i])
                out_ref[i, target] = cells
    one_plane(0, -1)
    one_plane(1, 0)
    flow_writes[-2].start()
    order_writes[-2].start()
    one_plane(PLANES - 2, 0)
    one_plane(PLANES - 1, 1)
    flow_writes[-1].start()
    order_writes[-1].start()
    for copy in flow_writes + order_writes:
        copy.wait()


def vmem(count):
    return [pl.BlockSpec(memory_space=pltpu.VMEM)] * count


def params(limit):
    return pltpu.CompilerParams(vmem_limit_bytes=limit)


def f32(*shape):
    return jax.ShapeDtypeStruct(shape, jnp.float32)


def shift_pairs(count, step):
    return [(i, (i + step) % count) for i in range(count)]


def swap_pairs(slabs, strips, first, step):
    pairs = []
    for low in range(first, slabs, 2):
        high = (low + 1) % slabs
        for strip in range(strips):
            other = (strip + step) % strips
            pairs.append((low * strips + strip, high * strips + other))
            pairs.append((high * strips + other, low * strips + strip))
    return pairs


def hbm(count):
    return [pl.BlockSpec(memory_space=pltpu.HBM)] * count


def smem():
    return [pl.BlockSpec(memory_space=pltpu.SMEM)]


def scratch(*shape):
    return pltpu.VMEM(shape, jnp.float32)


def sems(count):
    return pltpu.SemaphoreType.DMA((count,))


def main_planes(plane_offsets, flow, order, from_low, from_high, blocks, odd):
    return pl.pallas_call(
        main_kernel,
        out_shape=(f32(*flow.shape), f32(*order.shape)),
        in_specs=smem() + vmem(4) + hbm(4),
        out_specs=tuple(hbm(2)),
        scratch_shapes=[
            scratch(PAYLOAD, ROWS, LANES),
            scratch(PAYLOAD, ROWS, LANES),
            scratch(PAYLOAD, ROWS, LANES),
            scratch(SENT, LANES),
            scratch(*flow.shape),
            scratch(*order.shape),
            scratch(PLANES, ROWS, LANES),
            scratch(PAYLOAD, WINDOW, LANES),
            scratch(PAYLOAD, WINDOW, LANES),
            scratch(4, WINDOW, LANES),
            scratch(20, WINDOW, LANES),
            scratch(PLANES + 2, ROWS, LANES),
            scratch(10, PLANES, LANES),
            scratch(10, PLANES, LANES),
            scratch(2, PLANES, LANES),
            sems(4),
            sems(len(STORES)),
            sems(len(STORES)),
        ],
        compiler_params=params(MAIN_VMEM),
        name="collide_stream",
    )(plane_offsets, flow, order, from_low, from_high, *blocks, odd)


def shards(populations, order_pops, plane_offsets):
    slabs, strips = lax.axis_size("gx"), lax.axis_size("gy")
    slab = lax.axis_index("gx")
    shifts = ((plane_offsets + 5) // ROWS) % strips
    boundary = lax.iota(jnp.int32, slabs)
    at_even = jnp.where(boundary == (slab | 1), strips, 0)
    at_odd = jnp.where(boundary == ((slab + (slab & 1)) & (slabs - 1)), 1, 0)
    code = jnp.sum(shifts * (at_even + at_odd)).astype(jnp.uint32)
    even_step = (code // jnp.uint32(strips)).astype(jnp.int32)
    odd_step = lax.rem(code, jnp.uint32(strips)).astype(jnp.int32)

    even, own, to_low, to_high = pl.pallas_call(
        payload_kernel,
        out_shape=(
            f32(PAYLOAD, ROWS, LANES),
            f32(PAYLOAD, ROWS, LANES),
            f32(PACKED, LANES),
            f32(PACKED, LANES),
        ),
        in_specs=vmem(2),
        out_specs=tuple(vmem(4)),
        scratch_shapes=[scratch(PLANES, ROWS, LANES)],
        compiler_params=params(SMALL_VMEM),
        name="payloads",
    )(populations, order_pops)

    from_low = lax.ppermute(to_high, "gy", shift_pairs(strips, 1))
    from_high = lax.ppermute(to_low, "gy", shift_pairs(strips, -1))

    def even_branch(step):
        def run(mine):
            return tuple(
                lax.ppermute(mine, ("gx", "gy"), swap_pairs(slabs, strips, 0, step + d)) for d in (-1, 0, 1)
            )

        return run

    blocks = lax.switch(even_step, [even_branch(step) for step in range(strips)], even)
    from_low, from_high, blocks = lax.optimization_barrier((from_low, from_high, blocks))
    window = pl.pallas_call(
        window_kernel,
        out_shape=f32(SENT, LANES),
        in_specs=smem() + vmem(3),
        out_specs=vmem(1)[0],
        scratch_shapes=[scratch(PAYLOAD, WINDOW, LANES)],
        compiler_params=params(SMALL_VMEM),
        name="window",
    )(plane_offsets, from_low, own, from_high)

    def odd_branch(step):
        return lambda mine: lax.ppermute(mine, ("gx", "gy"), swap_pairs(slabs, strips, 1, step))

    odd = lax.switch(odd_step, [odd_branch(step) for step in range(strips)], window)
    return main_planes(plane_offsets, populations, order_pops, from_low, from_high, blocks, odd)


def solution(mesh):
    return jax.shard_map(
        shards,
        mesh=mesh,
        in_specs=(P(None, "gx", "gy", None), P(None, "gx", "gy", None), P()),
        out_specs=(P(None, "gx", "gy", None), P(None, "gx", "gy", None)),
        check_vma=False,
    )
```

```python
import jax
import jax.numpy as jnp
from jax import lax
from jax.experimental import pallas as pl
from jax.experimental.pallas import tpu as pltpu
from jax.sharding import PartitionSpec as P

SHIFT_FRACTION = 0.375
WALL_SPEED = 0.05
RELAX_FLOW = 0.8
RELAX_ORDER = 0.9
BULK_COEFF = 0.05
SURFACE_COEFF = 0.04
MOBILITY = 1.0
VELOCITY_X = (0, 1, -1, 0, 0, 0, 0, 1, -1, 1, -1, 1, -1, 1, -1, 0, 0, 0, 0)
VELOCITY_Y = (0, 0, 0, 1, -1, 0, 0, 1, -1, -1, 1, 0, 0, 0, 0, 1, -1, 1, -1)
VELOCITY_Z = (0, 0, 0, 0, 0, 1, -1, 0, 0, 0, 0, 1, -1, -1, 1, 1, -1, -1, 1)
WEIGHT_TABLE = (1.0 / 3.0,) + (1.0 / 18.0,) * 6 + (1.0 / 36.0,) * 12

VELS = 19
PLANES = 16
ROWS = 8
LANES = 128
UP_X = tuple(i for i in range(VELS) if VELOCITY_X[i] == 1)
DOWN_X = tuple(i for i in range(VELS) if VELOCITY_X[i] == -1)
UP_Y = tuple(i for i in range(VELS) if VELOCITY_Y[i] == 1)
DOWN_Y = tuple(i for i in range(VELS) if VELOCITY_Y[i] == -1)
PAYLOAD = 17
AT_MOMENTS = 5
AT_ORDER = 9
AT_PHASE = 14
WINDOW = 16
WINDOW_PAD = 4

SMALL_VMEM = 16 * 1024 * 1024
MAIN_VMEM = 24 * 1024 * 1024


def roll_rows(cells, step):
    return pltpu.roll(cells, step % cells.shape[0], 0)


def roll_lanes(cells, step):
    return pltpu.roll(cells, step % LANES, cells.ndim - 1)


def moments(flow):
    parts = [flow(i) for i in range(VELS)]
    density = parts[0]
    for part in parts[1:]:
        density = density + part
    speeds = []
    for table in (VELOCITY_X, VELOCITY_Y, VELOCITY_Z):
        plus = [parts[i] for i in range(VELS) if table[i] == 1]
        minus = [parts[i] for i in range(VELS) if table[i] == -1]
        total = plus[0] - minus[0]
        for a, b in zip(plus[1:], minus[1:]):
            total = total + (a - b)
        speeds.append(total)
    return density, speeds


def potential_of(phase, neighbours):
    around = neighbours[0]
    for cells in neighbours[1:]:
        around = around + cells
    bulk = BULK_COEFF * (phase * phase * phase - phase)
    return bulk - SURFACE_COEFF * (around - 6.0 * phase)


def dot_velocity(i, vector):
    total = None
    for sign, part in zip((VELOCITY_X[i], VELOCITY_Y[i], VELOCITY_Z[i]), vector):
        if sign == 0:
            continue
        if total is None:
            total = part if sign == 1 else -part
        else:
            total = total + part if sign == 1 else total - part
    return total


def collide(wanted, flow, order, density, momentum, phase, potential, force):
    inverse = 1.0 / density
    speed = [(momentum[d] + 0.5 * force[d]) * inverse for d in range(3)]
    source = 1.0 - 0.5 / RELAX_FLOW
    relaxed = density * (1.0 / RELAX_FLOW)
    speed_sq = speed[0] * speed[0] + speed[1] * speed[1] + speed[2] * speed[2]
    work = speed[0] * force[0] + speed[1] * force[1] + speed[2] * force[2]
    even = relaxed * (1.0 - 1.5 * speed_sq) - (3.0 * source) * work
    odd = [3.0 * (relaxed * speed[d] + source * force[d]) for d in range(3)]
    quad = [4.5 * relaxed * speed[d] + (9.0 * source) * force[d] for d in range(3)]
    order_even = (3.0 * MOBILITY / RELAX_ORDER) * potential
    carried = (3.0 / RELAX_ORDER) * phase
    order_odd = [carried * speed[d] for d in range(3)]
    flow_out, order_out = {}, {}
    keep_flow = 1.0 - 1.0 / RELAX_FLOW
    keep_order = 1.0 - 1.0 / RELAX_ORDER
    done = set()
    for i in wanted:
        if i in done:
            continue
        weight = WEIGHT_TABLE[i]
        if i == 0:
            flow_out[0] = keep_flow * flow(0) + weight * even
            rest = phase - (2.0 * MOBILITY) * potential
            order_out[0] = keep_order * order(0) + (1.0 / RELAX_ORDER) * rest
            continue
        first = i if i % 2 == 1 else i - 1
        pair_even = weight * (even + dot_velocity(first, speed) * dot_velocity(first, quad))
        pair_odd = weight * dot_velocity(first, odd)
        pair_order = weight * dot_velocity(first, order_odd)
        for member, sign in ((first, 1), (first + 1, -1)):
            if member not in wanted:
                continue
            done.add(member)
            both = pair_even + pair_odd if sign == 1 else pair_even - pair_odd
            flow_out[member] = keep_flow * flow(member) + both
            both = weight * order_even
            both = both + pair_order if sign == 1 else both - pair_order
            order_out[member] = keep_order * order(member) + both
    return flow_out, order_out


def add_phase(phase_ref, order_ref, x):
    total = order_ref[0, x]
    for i in range(1, VELS):
        total = total + order_ref[i, x]
    phase_ref[x] = total


def plane_copies(source, target, sems, pieces):
    return [
        pltpu.make_async_copy(source.at[:, pl.ds(first, count)], target.at[:, pl.ds(first, count)], sems.at[index])
        for index, (first, count) in enumerate(pieces)
    ]


SENT_ROWS = 11
SENT_SKIP = 2
SENT = ROWS + AT_PHASE * SENT_ROWS + 3 * (WINDOW - 1) + 1


def window_row(index):
    if index < AT_PHASE:
        return ROWS - SENT_SKIP + index * SENT_ROWS
    return ROWS + AT_PHASE * SENT_ROWS + (index - AT_PHASE) * (WINDOW - 1)


STORES = ((3, 5), (8, 5), (0, 3), (PLANES - 3, 3))


def even_boundary(slab):
    return slab + 1 - slab % 2


def odd_boundary(slab, slabs):
    return lax.rem(slab + slab % 2, slabs)


PACKED = PAYLOAD * (ROWS + PLANES)


def block_rows(index):
    return pl.ds(index * ROWS, ROWS)


def side_rows(index):
    return pl.ds(PAYLOAD * ROWS + index * PLANES, PLANES)


def side_row(ref, index, x):
    return ref[pl.ds(PAYLOAD * ROWS + index * PLANES + x, 1), :]


def payload_kernel(flow_ref, order_ref, even_ref, odd_ref, low_ref, high_ref, phase_ref):
    is_even = lax.axis_index("gx") % 2 == 0
    for x in range(PLANES):
        add_phase(phase_ref, order_ref, x)
    sides = []
    for plane, inward, comps in ((PLANES - 1, -1, UP_X), (0, 1, DOWN_X)):
        density, momentum = moments(lambda i: flow_ref[i, plane])
        parts = [flow_ref[i, plane] for i in comps] + [density] + momentum
        parts += [order_ref[i, plane] for i in comps]
        parts += [phase_ref[plane + inward * d] for d in range(3)]
        sides.append(parts)
    for index, (last, first) in enumerate(zip(*sides)):
        even_ref[index] = jnp.where(is_even, last, first)
        odd = jnp.where(is_even, first, last)
        odd_ref[index] = odd
        low_ref[block_rows(index), :] = odd
        high_ref[block_rows(index), :] = odd
    for out_ref, row, inward, comps in ((high_ref, ROWS - 1, -1, UP_Y), (low_ref, 0, 1, DOWN_Y)):
        density, momentum = moments(lambda i: flow_ref[i, :, row, :])
        parts = [flow_ref[i, :, row, :] for i in comps] + [density] + momentum
        parts += [order_ref[i, :, row, :] for i in comps]
        parts += [phase_ref[:, row + inward * d, :] for d in range(3)]
        for index, part in enumerate(parts):
            out_ref[side_rows(index), :] = part


def window_kernel(offset_ref, before_ref, own_ref, after_ref, out_ref, window_ref):
    slab = lax.axis_index("gx")
    inner = lax.rem(offset_ref[odd_boundary(slab, offset_ref.shape[0])] + 5, ROWS)

    blocks = [
        lambda index: before_ref[block_rows(index), :],
        lambda index: own_ref[index],
        lambda index: after_ref[block_rows(index), :],
    ]
    cut_window(blocks, jnp.where(slab % 2 == 0, inner, 9 - inner), window_ref)
    out_ref[0:ROWS, :] = window_ref[0, 0:ROWS]
    for index in range(PAYLOAD):
        first, count = (SENT_SKIP, SENT_ROWS) if index < AT_PHASE else (0, WINDOW)
        start = window_row(index) + first
        out_ref[start : start + count, :] = window_ref[index, first : first + count, :]


def cut_window(blocks, start, window_ref):
    row = lax.broadcasted_iota(jnp.int32, (ROWS, LANES), 0)
    inner = lax.rem(start, ROWS)
    back = lax.rem(ROWS - inner, ROWS)
    early = row < ROWS - inner
    near = start < ROWS
    for index in range(PAYLOAD):
        rolled = [pltpu.roll(block(index), back, 0) for block in blocks]
        first = jnp.where(near, rolled[0], rolled[1])
        second = jnp.where(near, rolled[1], rolled[2])
        window_ref[index, 0:ROWS] = jnp.where(early, first, second)
        window_ref[index, ROWS : 2 * ROWS] = jnp.where(early, second, rolled[2])


def ghost_plane(window_ref, comps, own, own_next, weight, kick_speed):
    other = 1.0 - weight

    def sheared(cells):
        return weight * cells + other * roll_rows(cells, 1)

    def seen(cells):
        return other * roll_rows(cells, -1) + weight * cells

    def sides(cells):
        return [roll_rows(cells, 1), roll_rows(cells, -1), roll_lanes(cells, 1), roll_lanes(cells, -1)]

    near, second, third = [window_ref[AT_PHASE + d] for d in range(3)]
    ghost_phase = sheared(near)
    own_potential = potential_of(own, [own_next, ghost_phase] + sides(own))
    near_potential = potential_of(near, [second, seen(own)] + sides(near))
    second_potential = potential_of(second, [third, near] + sides(second))
    beyond = seen(own_potential)
    outward = 1.0 if VELOCITY_X[comps[0]] == 1 else -1.0
    half = -0.5 * near
    force = [
        outward * half * (beyond - second_potential),
        half * (roll_rows(near_potential, -1) - roll_rows(near_potential, 1)),
        half * (roll_lanes(near_potential, -1) - roll_lanes(near_potential, 1)),
    ]
    density = window_ref[AT_MOMENTS]
    momentum = [window_ref[AT_MOMENTS + 1 + d] for d in range(3)]
    flow_out, order_out = collide(
        comps,
        lambda i: window_ref[comps.index(i)],
        lambda i: window_ref[AT_ORDER + comps.index(i)],
        density,
        momentum,
        near,
        near_potential,
        force,
    )
    flow_ghost = []
    for i in comps:
        cells = flow_out[i]
        if VELOCITY_Y[i] != 0:
            cells = cells + (WEIGHT_TABLE[i] * 3.0 * VELOCITY_Y[i] * kick_speed) * density
        flow_ghost.append(sheared(cells))
    order_ghost = [sheared(order_out[i]) for i in comps]
    return ghost_phase, own_potential, sheared(near_potential), flow_ghost, order_ghost


def rows_before(cells, line):
    row = lax.broadcasted_iota(jnp.int32, (ROWS, LANES), 0)
    return jnp.where(row == 0, line, roll_rows(cells, 1))


def rows_after(cells, line):
    row = lax.broadcasted_iota(jnp.int32, (ROWS, LANES), 0)
    return jnp.where(row == ROWS - 1, line, roll_rows(cells, -1))


def collide_sides(phase_ref, low_ref, high_ref, below, above, low_side, high_side, edge_ref):
    plane_at = lax.broadcasted_iota(jnp.int32, (PLANES, LANES), 0)

    def across(cells, which, own_row):
        before, after = roll_rows(cells, 1), roll_rows(cells, -1)
        if below is not None:
            before = jnp.where(plane_at == 0, below(which, own_row), before)
            after = jnp.where(plane_at == PLANES - 1, above(which, own_row), after)
        return before, after

    for side_ref, out_ref, edge, beside, inward, comps in (
        (low_ref, low_side, 0, -1, 1, UP_Y),
        (high_ref, high_side, ROWS - 1, ROWS, -1, DOWN_Y),
    ):
        own = [phase_ref[:, edge + inward * d, :] for d in range(2)]
        outer = [side_ref[side_rows(AT_PHASE + d), :] for d in range(3)]
        lines = [own[1], own[0]] + outer
        potentials = []
        for index in range(1, 4):
            cells = lines[index]
            around = list(across(cells, 0, edge + inward * (1 - index)))
            around += [lines[index - 1], lines[index + 1], roll_lanes(cells, 1), roll_lanes(cells, -1)]
            potentials.append(potential_of(cells, around))
        inside, here, outside = potentials
        before, after = across(here, 1, beside)
        half = -0.5 * outer[0]
        force = [
            half * (after - before),
            (inward * half) * (inside - outside),
            half * (roll_lanes(here, -1) - roll_lanes(here, 1)),
        ]
        flow_post, order_post = collide(
            comps,
            lambda i: side_ref[side_rows(comps.index(i)), :],
            lambda i: side_ref[side_rows(AT_ORDER + comps.index(i)), :],
            side_ref[side_rows(AT_MOMENTS), :],
            [side_ref[side_rows(AT_MOMENTS + 1 + d), :] for d in range(3)],
            outer[0],
            here,
            force,
        )
        for index, i in enumerate(comps):
            out_ref[index] = flow_post[i]
            out_ref[5 + index] = order_post[i]
        edge_ref[0 if inward == 1 else 1] = here


def plane_potential(phase_ref, low_ref, high_ref, x):
    cells = phase_ref[x]
    around = [
        phase_ref[x - 1],
        phase_ref[x + 1],
        rows_before(cells, side_row(low_ref, AT_PHASE, x)),
        rows_after(cells, side_row(high_ref, AT_PHASE, x)),
        roll_lanes(cells, 1),
        roll_lanes(cells, -1),
    ]
    return potential_of(cells, around)


def collide_plane(x, skip, flow_ref, order_ref, phase_ref, potential_ref, edge_ref, low_side, high_side, flow_out, order_out):
    here = potential_ref[x + 1]
    phase = phase_ref[x]
    half = -0.5 * phase
    along_y = rows_after(here, edge_ref[1, pl.ds(x, 1), :]) - rows_before(here, edge_ref[0, pl.ds(x, 1), :])
    force = [
        half * (potential_ref[x + 2] - potential_ref[x]),
        half * along_y,
        half * (roll_lanes(here, -1) - roll_lanes(here, 1)),
    ]
    density, momentum = moments(lambda i: flow_ref[i, x])
    flow_post, order_post = collide(
        tuple(i for i in range(VELS) if VELOCITY_X[i] == 0 or VELOCITY_X[i] != skip),
        lambda i: flow_ref[i, x],
        lambda i: order_ref[i, x],
        density,
        momentum,
        phase,
        here,
        force,
    )

    def moved(i, cells, first):
        if VELOCITY_Y[i] == 1:
            cells = rows_before(cells, low_side[first + UP_Y.index(i), pl.ds(x, 1), :])
        elif VELOCITY_Y[i] == -1:
            cells = rows_after(cells, high_side[first + DOWN_Y.index(i), pl.ds(x, 1), :])
        if VELOCITY_Z[i] != 0:
            cells = roll_lanes(cells, VELOCITY_Z[i])
        return cells

    for i in flow_post:
        target = x + VELOCITY_X[i]
        flow_out[i, target] = moved(i, flow_post[i], 0)
        order_out[i, target] = moved(i, order_post[i], 5)


def main_kernel(
    offset_hbm, flow_ref, order_ref, low_ref, high_ref, minus_hbm, same_hbm, plus_hbm, odd_hbm, flow_hbm_out, order_hbm_out,
    offset_ref, minus_ref, same_ref, plus_ref, odd_ref, flow_out, order_out, phase_ref, below_ref, above_ref, wide_ref, ghost_ref, potential_ref, low_side, high_side, edge_ref,
    arrival_sems, flow_out_sems, order_out_sems,
):
    pairs = ((minus_hbm, minus_ref), (same_hbm, same_ref), (plus_hbm, plus_ref), (odd_hbm, odd_ref))
    pairs += ((offset_hbm, offset_ref),)
    arrivals = [pltpu.make_async_copy(a, b, arrival_sems.at[index]) for index, (a, b) in enumerate(pairs)]
    for copy in arrivals:
        copy.start()
    flow_writes = plane_copies(flow_out, flow_hbm_out, flow_out_sems, STORES)
    order_writes = plane_copies(order_out, order_hbm_out, order_out_sems, STORES)

    def one_plane(x, skip):
        collide_plane(
            x, skip, flow_ref, order_ref, phase_ref, potential_ref, edge_ref, low_side, high_side, flow_out, order_out
        )

    for x in range(PLANES):
        add_phase(phase_ref, order_ref, x)
    collide_sides(phase_ref, low_ref, high_ref, None, None, low_side, high_side, edge_ref)
    for x in range(1, PLANES - 1):
        potential_ref[x + 1] = plane_potential(phase_ref, low_ref, high_ref, x)

    def step(x, carry):
        one_plane(x, 0)
        for part, (first, count) in enumerate(STORES[:-2]):

            @pl.when(x == first + count)
            def _(part=part):
                flow_writes[part].start()
                order_writes[part].start()

        return carry

    lax.fori_loop(2, PLANES - 2, step, 0)
    for copy in arrivals:
        copy.wait()
    slab = lax.axis_index("gx")
    is_even = slab % 2 == 0
    inner = lax.rem(offset_ref[even_boundary(slab)] + 5, ROWS)
    blocks = [
        lambda at: jnp.where(is_even, minus_ref[at], plus_ref[at]),
        lambda at: same_ref[at],
        lambda at: jnp.where(is_even, plus_ref[at], minus_ref[at]),
    ]
    cut_window(blocks, jnp.where(is_even, inner, 9 - inner), above_ref)
    for index in range(PAYLOAD):
        start = window_row(index)
        even, odd = above_ref[index], odd_ref[start : start + WINDOW, :]
        below_ref[index] = jnp.where(is_even, odd, even)
        above_ref[index] = jnp.where(is_even, even, odd)

    for index, plane in enumerate((0, 1, PLANES - 1, PLANES - 2)):
        wide_ref[index] = jnp.zeros((WINDOW, LANES), jnp.float32)
        for d in range(3):
            wide_ref[index, 3 - d : 4 - d, :] = side_row(low_ref, AT_PHASE + d, plane)
            wide_ref[index, 12 + d : 13 + d, :] = side_row(high_ref, AT_PHASE + d, plane)
        wide_ref[index, 4:12, :] = phase_ref[plane]
    below = ghost_plane(below_ref, UP_X, wide_ref[0], wide_ref[1], 1.0 - SHIFT_FRACTION, WALL_SPEED)
    above = ghost_plane(above_ref, DOWN_X, wide_ref[2], wide_ref[3], SHIFT_FRACTION, -WALL_SPEED)
    for index in range(5):
        ghost_ref[index] = below[3][index]
        ghost_ref[5 + index] = below[4][index]
        ghost_ref[10 + index] = above[3][index]
        ghost_ref[15 + index] = above[4][index]

    def ghost_row(ghost):
        return lambda which, own_row: ghost[2 * which][own_row + WINDOW_PAD : own_row + WINDOW_PAD + 1, :]

    collide_sides(
        phase_ref, low_ref, high_ref, ghost_row(below), ghost_row(above), low_side, high_side, edge_ref
    )
    wide_ref[0] = below[1]
    wide_ref[1] = below[2]
    wide_ref[2] = above[1]
    wide_ref[3] = above[2]
    potential_ref[1] = wide_ref[0, 4:12, :]
    potential_ref[0] = wide_ref[1, 4:12, :]
    potential_ref[PLANES] = wide_ref[2, 4:12, :]
    potential_ref[PLANES + 1] = wide_ref[3, 4:12, :]
    for comps, first, target in ((UP_X, 0, 0), (DOWN_X, 10, PLANES - 1)):
        for index, i in enumerate(comps):
            start = WINDOW_PAD - VELOCITY_Y[i]
            for out_ref, at in ((flow_out, first + index), (order_out, first + 5 + index)):
                cells = ghost_ref[at, start : start + ROWS, :]
                if VELOCITY_Z[i] != 0:
                    cells = roll_lanes(cells, VELOCITY_Z[i])
                out_ref[i, target] = cells
    one_plane(0, -1)
    one_plane(1, 0)
    flow_writes[-2].start()
    order_writes[-2].start()
    one_plane(PLANES - 2, 0)
    one_plane(PLANES - 1, 1)
    flow_writes[-1].start()
    order_writes[-1].start()
    for copy in flow_writes + order_writes:
        copy.wait()


def vmem(count):
    return [pl.BlockSpec(memory_space=pltpu.VMEM)] * count


def params(limit):
    return pltpu.CompilerParams(vmem_limit_bytes=limit)


def f32(*shape):
    return jax.ShapeDtypeStruct(shape, jnp.float32)


def shift_pairs(count, step):
    return [(i, (i + step) % count) for i in range(count)]


def swap_pairs(slabs, strips, first, step):
    pairs = []
    for low in range(first, slabs, 2):
        high = (low + 1) % slabs
        for strip in range(strips):
            other = (strip + step) % strips
            pairs.append((low * strips + strip, high * strips + other))
            pairs.append((high * strips + other, low * strips + strip))
    return pairs


def hbm(count):
    return [pl.BlockSpec(memory_space=pltpu.HBM)] * count


def smem():
    return [pl.BlockSpec(memory_space=pltpu.SMEM)]


def scratch(*shape):
    return pltpu.VMEM(shape, jnp.float32)


def sems(count):
    return pltpu.SemaphoreType.DMA((count,))


def main_planes(plane_offsets, flow, order, from_low, from_high, blocks, odd):
    return pl.pallas_call(
        main_kernel,
        out_shape=(f32(*flow.shape), f32(*order.shape)),
        in_specs=hbm(1) + vmem(4) + hbm(4),
        out_specs=tuple(hbm(2)),
        scratch_shapes=[
            pltpu.SMEM(plane_offsets.shape, jnp.int32),
            scratch(PAYLOAD, ROWS, LANES),
            scratch(PAYLOAD, ROWS, LANES),
            scratch(PAYLOAD, ROWS, LANES),
            scratch(SENT, LANES),
            scratch(*flow.shape),
            scratch(*order.shape),
            scratch(PLANES, ROWS, LANES),
            scratch(PAYLOAD, WINDOW, LANES),
            scratch(PAYLOAD, WINDOW, LANES),
            scratch(4, WINDOW, LANES),
            scratch(20, WINDOW, LANES),
            scratch(PLANES + 2, ROWS, LANES),
            scratch(10, PLANES, LANES),
            scratch(10, PLANES, LANES),
            scratch(2, PLANES, LANES),
            sems(5),
            sems(len(STORES)),
            sems(len(STORES)),
        ],
        compiler_params=params(MAIN_VMEM),
        name="collide_stream",
    )(plane_offsets, flow, order, from_low, from_high, *blocks, odd)


def shards(populations, order_pops, plane_offsets):
    slabs, strips = lax.axis_size("gx"), lax.axis_size("gy")
    slab = lax.axis_index("gx")
    shifts = ((plane_offsets + 5) // ROWS) % strips
    boundary = lax.iota(jnp.int32, slabs)
    at_even = jnp.where(boundary == (slab | 1), strips, 0)
    at_odd = jnp.where(boundary == ((slab + (slab & 1)) & (slabs - 1)), 1, 0)
    code = jnp.sum(shifts * (at_even + at_odd)).astype(jnp.uint32)
    even_step = (code // jnp.uint32(strips)).astype(jnp.int32)
    odd_step = lax.rem(code, jnp.uint32(strips)).astype(jnp.int32)

    even, own, to_low, to_high = pl.pallas_call(
        payload_kernel,
        out_shape=(
            f32(PAYLOAD, ROWS, LANES),
            f32(PAYLOAD, ROWS, LANES),
            f32(PACKED, LANES),
            f32(PACKED, LANES),
        ),
        in_specs=vmem(2),
        out_specs=tuple(vmem(4)),
        scratch_shapes=[scratch(PLANES, ROWS, LANES)],
        compiler_params=params(SMALL_VMEM),
        name="payloads",
    )(populations, order_pops)

    from_low = lax.ppermute(to_high, "gy", shift_pairs(strips, 1))
    from_high = lax.ppermute(to_low, "gy", shift_pairs(strips, -1))

    def even_branch(step):
        def run(mine):
            return tuple(
                lax.ppermute(mine, ("gx", "gy"), swap_pairs(slabs, strips, 0, step + d)) for d in (-1, 0, 1)
            )

        return run

    blocks = lax.switch(even_step, [even_branch(step) for step in range(strips)], even)
    from_low, from_high, blocks = lax.optimization_barrier((from_low, from_high, blocks))
    window = pl.pallas_call(
        window_kernel,
        out_shape=f32(SENT, LANES),
        in_specs=smem() + vmem(3),
        out_specs=vmem(1)[0],
        scratch_shapes=[scratch(PAYLOAD, WINDOW, LANES)],
        compiler_params=params(SMALL_VMEM),
        name="window",
    )(plane_offsets, from_low, own, from_high)

    def odd_branch(step):
        return lambda mine: lax.ppermute(mine, ("gx", "gy"), swap_pairs(slabs, strips, 1, step))

    odd = lax.switch(odd_step, [odd_branch(step) for step in range(strips)], window)
    return main_planes(plane_offsets, populations, order_pops, from_low, from_high, blocks, odd)


def solution(mesh):
    return jax.shard_map(
        shards,
        mesh=mesh,
        in_specs=(P(None, "gx", "gy", None), P(None, "gx", "gy", None), P()),
        out_specs=(P(None, "gx", "gy", None), P(None, "gx", "gy", None)),
        check_vma=False,
    )
```

```python
import jax
import jax.numpy as jnp
from jax import lax
from jax.experimental import pallas as pl
from jax.experimental.pallas import tpu as pltpu
from jax.sharding import PartitionSpec as P

SHIFT_FRACTION = 0.375
WALL_SPEED = 0.05
RELAX_FLOW = 0.8
RELAX_ORDER = 0.9
BULK_COEFF = 0.05
SURFACE_COEFF = 0.04
MOBILITY = 1.0
VELOCITY_X = (0, 1, -1, 0, 0, 0, 0, 1, -1, 1, -1, 1, -1, 1, -1, 0, 0, 0, 0)
VELOCITY_Y = (0, 0, 0, 1, -1, 0, 0, 1, -1, -1, 1, 0, 0, 0, 0, 1, -1, 1, -1)
VELOCITY_Z = (0, 0, 0, 0, 0, 1, -1, 0, 0, 0, 0, 1, -1, -1, 1, 1, -1, -1, 1)
WEIGHT_TABLE = (1.0 / 3.0,) + (1.0 / 18.0,) * 6 + (1.0 / 36.0,) * 12

VELS = 19
PLANES = 16
ROWS = 8
LANES = 128
UP_X = tuple(i for i in range(VELS) if VELOCITY_X[i] == 1)
DOWN_X = tuple(i for i in range(VELS) if VELOCITY_X[i] == -1)
UP_Y = tuple(i for i in range(VELS) if VELOCITY_Y[i] == 1)
DOWN_Y = tuple(i for i in range(VELS) if VELOCITY_Y[i] == -1)
PAYLOAD = 17
AT_MOMENTS = 5
AT_ORDER = 9
AT_PHASE = 14
WINDOW = 16
WINDOW_PAD = 4

SMALL_VMEM = 16 * 1024 * 1024
MAIN_VMEM = 24 * 1024 * 1024


def roll_rows(cells, step):
    return pltpu.roll(cells, step % cells.shape[0], 0)


def roll_lanes(cells, step):
    return pltpu.roll(cells, step % LANES, cells.ndim - 1)


def moments(flow):
    parts = [flow(i) for i in range(VELS)]
    density = parts[0]
    for part in parts[1:]:
        density = density + part
    speeds = []
    for table in (VELOCITY_X, VELOCITY_Y, VELOCITY_Z):
        plus = [parts[i] for i in range(VELS) if table[i] == 1]
        minus = [parts[i] for i in range(VELS) if table[i] == -1]
        total = plus[0] - minus[0]
        for a, b in zip(plus[1:], minus[1:]):
            total = total + (a - b)
        speeds.append(total)
    return density, speeds


def potential_of(phase, neighbours):
    around = neighbours[0]
    for cells in neighbours[1:]:
        around = around + cells
    bulk = BULK_COEFF * (phase * phase * phase - phase)
    return bulk - SURFACE_COEFF * (around - 6.0 * phase)


def dot_velocity(i, vector):
    total = None
    for sign, part in zip((VELOCITY_X[i], VELOCITY_Y[i], VELOCITY_Z[i]), vector):
        if sign == 0:
            continue
        if total is None:
            total = part if sign == 1 else -part
        else:
            total = total + part if sign == 1 else total - part
    return total


def collide(wanted, flow, order, density, momentum, phase, potential, force):
    inverse = 1.0 / density
    speed = [(momentum[d] + 0.5 * force[d]) * inverse for d in range(3)]
    source = 1.0 - 0.5 / RELAX_FLOW
    relaxed = density * (1.0 / RELAX_FLOW)
    speed_sq = speed[0] * speed[0] + speed[1] * speed[1] + speed[2] * speed[2]
    work = speed[0] * force[0] + speed[1] * force[1] + speed[2] * force[2]
    even = relaxed * (1.0 - 1.5 * speed_sq) - (3.0 * source) * work
    odd = [3.0 * (relaxed * speed[d] + source * force[d]) for d in range(3)]
    quad = [4.5 * relaxed * speed[d] + (9.0 * source) * force[d] for d in range(3)]
    order_even = (3.0 * MOBILITY / RELAX_ORDER) * potential
    carried = (3.0 / RELAX_ORDER) * phase
    order_odd = [carried * speed[d] for d in range(3)]
    flow_out, order_out = {}, {}
    keep_flow = 1.0 - 1.0 / RELAX_FLOW
    keep_order = 1.0 - 1.0 / RELAX_ORDER
    done = set()
    for i in wanted:
        if i in done:
            continue
        weight = WEIGHT_TABLE[i]
        if i == 0:
            flow_out[0] = keep_flow * flow(0) + weight * even
            rest = phase - (2.0 * MOBILITY) * potential
            order_out[0] = keep_order * order(0) + (1.0 / RELAX_ORDER) * rest
            continue
        first = i if i % 2 == 1 else i - 1
        pair_even = weight * (even + dot_velocity(first, speed) * dot_velocity(first, quad))
        pair_odd = weight * dot_velocity(first, odd)
        pair_order = weight * dot_velocity(first, order_odd)
        for member, sign in ((first, 1), (first + 1, -1)):
            if member not in wanted:
                continue
            done.add(member)
            both = pair_even + pair_odd if sign == 1 else pair_even - pair_odd
            flow_out[member] = keep_flow * flow(member) + both
            both = weight * order_even
            both = both + pair_order if sign == 1 else both - pair_order
            order_out[member] = keep_order * order(member) + both
    return flow_out, order_out


def add_phase(phase_ref, order_ref, x):
    total = order_ref[0, x]
    for i in range(1, VELS):
        total = total + order_ref[i, x]
    phase_ref[x] = total


def plane_copies(source, target, sems, pieces):
    return [
        pltpu.make_async_copy(source.at[:, pl.ds(first, count)], target.at[:, pl.ds(first, count)], sems.at[index])
        for index, (first, count) in enumerate(pieces)
    ]


SENT_ROWS = 11
SENT_SKIP = 2
SENT = ROWS + AT_PHASE * SENT_ROWS + 3 * (WINDOW - 1) + 1


def window_row(index):
    if index < AT_PHASE:
        return ROWS - SENT_SKIP + index * SENT_ROWS
    return ROWS + AT_PHASE * SENT_ROWS + (index - AT_PHASE) * (WINDOW - 1)


STORES = ((3, 5), (8, 5), (0, 3), (PLANES - 3, 3))


def even_boundary(slab):
    return slab + 1 - slab % 2


def odd_boundary(slab, slabs):
    return lax.rem(slab + slab % 2, slabs)


WIDE_ROWS, NARROW_ROWS = 6, 4
WIDE_PACK, NARROW_PACK = 112, 88


def pack_row(index, rows):
    return (index - AT_PHASE) * ROWS if index >= AT_PHASE else 3 * ROWS + index * rows


def put_rows(pack_ref, index, rows, block_ref, kept_from):
    start = pack_row(index, rows)
    if index >= AT_PHASE:
        pack_ref[start : start + ROWS, :] = block_ref[index]
    else:
        pack_ref[start : start + rows, :] = block_ref[index, kept_from : kept_from + rows, :]


def packed_block(pack_ref, index, rows, kept_from):
    start = pack_row(index, rows) - (0 if index >= AT_PHASE else kept_from)
    return pack_ref[start : start + ROWS, :]


PACKED = WIDE_PACK + PAYLOAD * PLANES


def side_rows(index):
    return pl.ds(WIDE_PACK + index * PLANES, PLANES)


def side_row(ref, index, x):
    return ref[pl.ds(WIDE_PACK + index * PLANES + x, 1), :]


def payload_kernel(flow_ref, order_ref, minus_ref, even_ref, plus_ref, odd_ref, low_ref, high_ref, phase_ref):
    is_even = lax.axis_index("gx") % 2 == 0
    for x in range(PLANES):
        add_phase(phase_ref, order_ref, x)
    sides = []
    for plane, inward, comps in ((PLANES - 1, -1, UP_X), (0, 1, DOWN_X)):
        density, momentum = moments(lambda i: flow_ref[i, plane])
        parts = [flow_ref[i, plane] for i in comps] + [density] + momentum
        parts += [order_ref[i, plane] for i in comps]
        parts += [phase_ref[plane + inward * d] for d in range(3)]
        sides.append(parts)
    for index, (last, first) in enumerate(zip(*sides)):
        even_ref[index] = jnp.where(is_even, last, first)
        odd_ref[index] = jnp.where(is_even, first, last)
        put_rows(low_ref, index, WIDE_ROWS, odd_ref, 0)
        put_rows(high_ref, index, WIDE_ROWS, odd_ref, ROWS - WIDE_ROWS)
        for pack_ref, rows, when_even, when_odd in (
            (minus_ref, WIDE_ROWS, 0, ROWS - WIDE_ROWS),
            (plus_ref, NARROW_ROWS, ROWS - NARROW_ROWS, 0),
        ):
            start = pack_row(index, rows)
            if index >= AT_PHASE:
                pack_ref[start : start + ROWS, :] = even_ref[index]
            else:
                pack_ref[start : start + rows, :] = jnp.where(
                    is_even, even_ref[index, when_even : when_even + rows, :], even_ref[index, when_odd : when_odd + rows, :]
                )
    for out_ref, row, inward, comps in ((high_ref, ROWS - 1, -1, UP_Y), (low_ref, 0, 1, DOWN_Y)):
        density, momentum = moments(lambda i: flow_ref[i, :, row, :])
        parts = [flow_ref[i, :, row, :] for i in comps] + [density] + momentum
        parts += [order_ref[i, :, row, :] for i in comps]
        parts += [phase_ref[:, row + inward * d, :] for d in range(3)]
        for index, part in enumerate(parts):
            out_ref[side_rows(index), :] = part


def window_kernel(offset_ref, before_ref, own_ref, after_ref, out_ref, window_ref):
    slab = lax.axis_index("gx")
    inner = lax.rem(offset_ref[odd_boundary(slab, offset_ref.shape[0])] + 5, ROWS)

    blocks = [
        lambda index: packed_block(before_ref, index, WIDE_ROWS, ROWS - WIDE_ROWS),
        lambda index: own_ref[index],
        lambda index: packed_block(after_ref, index, WIDE_ROWS, 0),
    ]
    cut_window(blocks, jnp.where(slab % 2 == 0, inner, 9 - inner), window_ref)
    out_ref[0:ROWS, :] = window_ref[0, 0:ROWS]
    for index in range(PAYLOAD):
        first, count = (SENT_SKIP, SENT_ROWS) if index < AT_PHASE else (0, WINDOW)
        start = window_row(index) + first
        out_ref[start : start + count, :] = window_ref[index, first : first + count, :]


def cut_window(blocks, start, window_ref):
    row = lax.broadcasted_iota(jnp.int32, (ROWS, LANES), 0)
    inner = lax.rem(start, ROWS)
    back = lax.rem(ROWS - inner, ROWS)
    early = row < ROWS - inner
    near = start < ROWS
    for index in range(PAYLOAD):
        rolled = [pltpu.roll(block(index), back, 0) for block in blocks]
        first = jnp.where(near, rolled[0], rolled[1])
        second = jnp.where(near, rolled[1], rolled[2])
        window_ref[index, 0:ROWS] = jnp.where(early, first, second)
        window_ref[index, ROWS : 2 * ROWS] = jnp.where(early, second, rolled[2])


def ghost_plane(window_ref, comps, own, own_next, weight, kick_speed):
    other = 1.0 - weight

    def sheared(cells):
        return weight * cells + other * roll_rows(cells, 1)

    def seen(cells):
        return other * roll_rows(cells, -1) + weight * cells

    def sides(cells):
        return [roll_rows(cells, 1), roll_rows(cells, -1), roll_lanes(cells, 1), roll_lanes(cells, -1)]

    near, second, third = [window_ref[AT_PHASE + d] for d in range(3)]
    ghost_phase = sheared(near)
    own_potential = potential_of(own, [own_next, ghost_phase] + sides(own))
    near_potential = potential_of(near, [second, seen(own)] + sides(near))
    second_potential = potential_of(second, [third, near] + sides(second))
    beyond = seen(own_potential)
    outward = 1.0 if VELOCITY_X[comps[0]] == 1 else -1.0
    half = -0.5 * near
    force = [
        outward * half * (beyond - second_potential),
        half * (roll_rows(near_potential, -1) - roll_rows(near_potential, 1)),
        half * (roll_lanes(near_potential, -1) - roll_lanes(near_potential, 1)),
    ]
    density = window_ref[AT_MOMENTS]
    momentum = [window_ref[AT_MOMENTS + 1 + d] for d in range(3)]
    flow_out, order_out = collide(
        comps,
        lambda i: window_ref[comps.index(i)],
        lambda i: window_ref[AT_ORDER + comps.index(i)],
        density,
        momentum,
        near,
        near_potential,
        force,
    )
    flow_ghost = []
    for i in comps:
        cells = flow_out[i]
        if VELOCITY_Y[i] != 0:
            cells = cells + (WEIGHT_TABLE[i] * 3.0 * VELOCITY_Y[i] * kick_speed) * density
        flow_ghost.append(sheared(cells))
    order_ghost = [sheared(order_out[i]) for i in comps]
    return ghost_phase, own_potential, sheared(near_potential), flow_ghost, order_ghost


def rows_before(cells, line):
    row = lax.broadcasted_iota(jnp.int32, (ROWS, LANES), 0)
    return jnp.where(row == 0, line, roll_rows(cells, 1))


def rows_after(cells, line):
    row = lax.broadcasted_iota(jnp.int32, (ROWS, LANES), 0)
    return jnp.where(row == ROWS - 1, line, roll_rows(cells, -1))


def collide_sides(phase_ref, low_ref, high_ref, below, above, low_side, high_side, edge_ref):
    plane_at = lax.broadcasted_iota(jnp.int32, (PLANES, LANES), 0)

    def across(cells, which, own_row):
        before, after = roll_rows(cells, 1), roll_rows(cells, -1)
        if below is not None:
            before = jnp.where(plane_at == 0, below(which, own_row), before)
            after = jnp.where(plane_at == PLANES - 1, above(which, own_row), after)
        return before, after

    for side_ref, out_ref, edge, beside, inward, comps in (
        (low_ref, low_side, 0, -1, 1, UP_Y),
        (high_ref, high_side, ROWS - 1, ROWS, -1, DOWN_Y),
    ):
        own = [phase_ref[:, edge + inward * d, :] for d in range(2)]
        outer = [side_ref[side_rows(AT_PHASE + d), :] for d in range(3)]
        lines = [own[1], own[0]] + outer
        potentials = []
        for index in range(1, 4):
            cells = lines[index]
            around = list(across(cells, 0, edge + inward * (1 - index)))
            around += [lines[index - 1], lines[index + 1], roll_lanes(cells, 1), roll_lanes(cells, -1)]
            potentials.append(potential_of(cells, around))
        inside, here, outside = potentials
        before, after = across(here, 1, beside)
        half = -0.5 * outer[0]
        force = [
            half * (after - before),
            (inward * half) * (inside - outside),
            half * (roll_lanes(here, -1) - roll_lanes(here, 1)),
        ]
        flow_post, order_post = collide(
            comps,
            lambda i: side_ref[side_rows(comps.index(i)), :],
            lambda i: side_ref[side_rows(AT_ORDER + comps.index(i)), :],
            side_ref[side_rows(AT_MOMENTS), :],
            [side_ref[side_rows(AT_MOMENTS + 1 + d), :] for d in range(3)],
            outer[0],
            here,
            force,
        )
        for index, i in enumerate(comps):
            out_ref[index] = flow_post[i]
            out_ref[5 + index] = order_post[i]
        edge_ref[0 if inward == 1 else 1] = here


def plane_potential(phase_ref, low_ref, high_ref, x):
    cells = phase_ref[x]
    around = [
        phase_ref[x - 1],
        phase_ref[x + 1],
        rows_before(cells, side_row(low_ref, AT_PHASE, x)),
        rows_after(cells, side_row(high_ref, AT_PHASE, x)),
        roll_lanes(cells, 1),
        roll_lanes(cells, -1),
    ]
    return potential_of(cells, around)


def collide_plane(x, skip, flow_ref, order_ref, phase_ref, potential_ref, edge_ref, low_side, high_side, flow_out, order_out):
    here = potential_ref[x + 1]
    phase = phase_ref[x]
    half = -0.5 * phase
    along_y = rows_after(here, edge_ref[1, pl.ds(x, 1), :]) - rows_before(here, edge_ref[0, pl.ds(x, 1), :])
    force = [
        half * (potential_ref[x + 2] - potential_ref[x]),
        half * along_y,
        half * (roll_lanes(here, -1) - roll_lanes(here, 1)),
    ]
    density, momentum = moments(lambda i: flow_ref[i, x])
    flow_post, order_post = collide(
        tuple(i for i in range(VELS) if VELOCITY_X[i] == 0 or VELOCITY_X[i] != skip),
        lambda i: flow_ref[i, x],
        lambda i: order_ref[i, x],
        density,
        momentum,
        phase,
        here,
        force,
    )

    def moved(i, cells, first):
        if VELOCITY_Y[i] == 1:
            cells = rows_before(cells, low_side[first + UP_Y.index(i), pl.ds(x, 1), :])
        elif VELOCITY_Y[i] == -1:
            cells = rows_after(cells, high_side[first + DOWN_Y.index(i), pl.ds(x, 1), :])
        if VELOCITY_Z[i] != 0:
            cells = roll_lanes(cells, VELOCITY_Z[i])
        return cells

    for i in flow_post:
        target = x + VELOCITY_X[i]
        flow_out[i, target] = moved(i, flow_post[i], 0)
        order_out[i, target] = moved(i, order_post[i], 5)


def main_kernel(
    offset_hbm, flow_ref, order_ref, low_ref, high_ref, minus_hbm, same_hbm, plus_hbm, odd_hbm, flow_hbm_out, order_hbm_out,
    offset_ref, minus_ref, same_ref, plus_ref, odd_ref, flow_out, order_out, phase_ref, below_ref, above_ref, wide_ref, ghost_ref, potential_ref, low_side, high_side, edge_ref,
    arrival_sems, flow_out_sems, order_out_sems,
):
    pairs = ((minus_hbm, minus_ref), (same_hbm, same_ref), (plus_hbm, plus_ref), (odd_hbm, odd_ref))
    pairs += ((offset_hbm, offset_ref),)
    arrivals = [pltpu.make_async_copy(a, b, arrival_sems.at[index]) for index, (a, b) in enumerate(pairs)]
    for copy in arrivals:
        copy.start()
    flow_writes = plane_copies(flow_out, flow_hbm_out, flow_out_sems, STORES)
    order_writes = plane_copies(order_out, order_hbm_out, order_out_sems, STORES)

    def one_plane(x, skip):
        collide_plane(
            x, skip, flow_ref, order_ref, phase_ref, potential_ref, edge_ref, low_side, high_side, flow_out, order_out
        )

    for x in range(PLANES):
        add_phase(phase_ref, order_ref, x)
    collide_sides(phase_ref, low_ref, high_ref, None, None, low_side, high_side, edge_ref)
    for x in range(1, PLANES - 1):
        potential_ref[x + 1] = plane_potential(phase_ref, low_ref, high_ref, x)

    def step(x, carry):
        one_plane(x, 0)
        for part, (first, count) in enumerate(STORES[:-2]):

            @pl.when(x == first + count)
            def _(part=part):
                flow_writes[part].start()
                order_writes[part].start()

        return carry

    lax.fori_loop(2, PLANES - 2, step, 0)
    for copy in arrivals:
        copy.wait()
    slab = lax.axis_index("gx")
    is_even = slab % 2 == 0
    inner = lax.rem(offset_ref[even_boundary(slab)] + 5, ROWS)
    blocks = [
        lambda at: jnp.where(
            is_even,
            packed_block(minus_ref, at, WIDE_ROWS, ROWS - WIDE_ROWS),
            packed_block(plus_ref, at, NARROW_ROWS, ROWS - NARROW_ROWS),
        ),
        lambda at: same_ref[at],
        lambda at: jnp.where(
            is_even, packed_block(plus_ref, at, NARROW_ROWS, 0), packed_block(minus_ref, at, WIDE_ROWS, 0)
        ),
    ]
    cut_window(blocks, jnp.where(is_even, inner, 9 - inner), above_ref)
    for index in range(PAYLOAD):
        start = window_row(index)
        even, odd = above_ref[index], odd_ref[start : start + WINDOW, :]
        below_ref[index] = jnp.where(is_even, odd, even)
        above_ref[index] = jnp.where(is_even, even, odd)

    for index, plane in enumerate((0, 1, PLANES - 1, PLANES - 2)):
        wide_ref[index] = jnp.zeros((WINDOW, LANES), jnp.float32)
        for d in range(3):
            wide_ref[index, 3 - d : 4 - d, :] = side_row(low_ref, AT_PHASE + d, plane)
            wide_ref[index, 12 + d : 13 + d, :] = side_row(high_ref, AT_PHASE + d, plane)
        wide_ref[index, 4:12, :] = phase_ref[plane]
    below = ghost_plane(below_ref, UP_X, wide_ref[0], wide_ref[1], 1.0 - SHIFT_FRACTION, WALL_SPEED)
    above = ghost_plane(above_ref, DOWN_X, wide_ref[2], wide_ref[3], SHIFT_FRACTION, -WALL_SPEED)
    for index in range(5):
        ghost_ref[index] = below[3][index]
        ghost_ref[5 + index] = below[4][index]
        ghost_ref[10 + index] = above[3][index]
        ghost_ref[15 + index] = above[4][index]

    def ghost_row(ghost):
        return lambda which, own_row: ghost[2 * which][own_row + WINDOW_PAD : own_row + WINDOW_PAD + 1, :]

    collide_sides(
        phase_ref, low_ref, high_ref, ghost_row(below), ghost_row(above), low_side, high_side, edge_ref
    )
    wide_ref[0] = below[1]
    wide_ref[1] = below[2]
    wide_ref[2] = above[1]
    wide_ref[3] = above[2]
    potential_ref[1] = wide_ref[0, 4:12, :]
    potential_ref[0] = wide_ref[1, 4:12, :]
    potential_ref[PLANES] = wide_ref[2, 4:12, :]
    potential_ref[PLANES + 1] = wide_ref[3, 4:12, :]
    for comps, first, target in ((UP_X, 0, 0), (DOWN_X, 10, PLANES - 1)):
        for index, i in enumerate(comps):
            start = WINDOW_PAD - VELOCITY_Y[i]
            for out_ref, at in ((flow_out, first + index), (order_out, first + 5 + index)):
                cells = ghost_ref[at, start : start + ROWS, :]
                if VELOCITY_Z[i] != 0:
                    cells = roll_lanes(cells, VELOCITY_Z[i])
                out_ref[i, target] = cells
    one_plane(0, -1)
    one_plane(1, 0)
    flow_writes[-2].start()
    order_writes[-2].start()
    one_plane(PLANES - 2, 0)
    one_plane(PLANES - 1, 1)
    flow_writes[-1].start()
    order_writes[-1].start()
    for copy in flow_writes + order_writes:
        copy.wait()


def vmem(count):
    return [pl.BlockSpec(memory_space=pltpu.VMEM)] * count


def params(limit):
    return pltpu.CompilerParams(vmem_limit_bytes=limit)


def f32(*shape):
    return jax.ShapeDtypeStruct(shape, jnp.float32)


def shift_pairs(count, step):
    return [(i, (i + step) % count) for i in range(count)]


def swap_pairs(slabs, strips, first, step):
    pairs = []
    for low in range(first, slabs, 2):
        high = (low + 1) % slabs
        for strip in range(strips):
            other = (strip + step) % strips
            pairs.append((low * strips + strip, high * strips + other))
            pairs.append((high * strips + other, low * strips + strip))
    return pairs


def hbm(count):
    return [pl.BlockSpec(memory_space=pltpu.HBM)] * count


def smem():
    return [pl.BlockSpec(memory_space=pltpu.SMEM)]


def scratch(*shape):
    return pltpu.VMEM(shape, jnp.float32)


def sems(count):
    return pltpu.SemaphoreType.DMA((count,))


def main_planes(plane_offsets, flow, order, from_low, from_high, blocks, odd):
    return pl.pallas_call(
        main_kernel,
        out_shape=(f32(*flow.shape), f32(*order.shape)),
        in_specs=hbm(1) + vmem(4) + hbm(4),
        out_specs=tuple(hbm(2)),
        scratch_shapes=[
            pltpu.SMEM(plane_offsets.shape, jnp.int32),
            scratch(WIDE_PACK, LANES),
            scratch(PAYLOAD, ROWS, LANES),
            scratch(NARROW_PACK, LANES),
            scratch(SENT, LANES),
            scratch(*flow.shape),
            scratch(*order.shape),
            scratch(PLANES, ROWS, LANES),
            scratch(PAYLOAD, WINDOW, LANES),
            scratch(PAYLOAD, WINDOW, LANES),
            scratch(4, WINDOW, LANES),
            scratch(20, WINDOW, LANES),
            scratch(PLANES + 2, ROWS, LANES),
            scratch(10, PLANES, LANES),
            scratch(10, PLANES, LANES),
            scratch(2, PLANES, LANES),
            sems(5),
            sems(len(STORES)),
            sems(len(STORES)),
        ],
        compiler_params=params(MAIN_VMEM),
        name="collide_stream",
    )(plane_offsets, flow, order, from_low, from_high, *blocks, odd)


def shards(populations, order_pops, plane_offsets):
    slabs, strips = lax.axis_size("gx"), lax.axis_size("gy")
    slab = lax.axis_index("gx")
    shifts = ((plane_offsets + 5) // ROWS) % strips
    boundary = lax.iota(jnp.int32, slabs)
    at_even = jnp.where(boundary == (slab | 1), strips, 0)
    at_odd = jnp.where(boundary == ((slab + (slab & 1)) & (slabs - 1)), 1, 0)
    code = jnp.sum(shifts * (at_even + at_odd)).astype(jnp.uint32)
    even_step = (code // jnp.uint32(strips)).astype(jnp.int32)
    odd_step = lax.rem(code, jnp.uint32(strips)).astype(jnp.int32)

    minus, same, plus, own, to_low, to_high = pl.pallas_call(
        payload_kernel,
        out_shape=(
            f32(WIDE_PACK, LANES),
            f32(PAYLOAD, ROWS, LANES),
            f32(NARROW_PACK, LANES),
            f32(PAYLOAD, ROWS, LANES),
            f32(PACKED, LANES),
            f32(PACKED, LANES),
        ),
        in_specs=vmem(2),
        out_specs=tuple(vmem(6)),
        scratch_shapes=[scratch(PLANES, ROWS, LANES)],
        compiler_params=params(SMALL_VMEM),
        name="payloads",
    )(populations, order_pops)

    from_low = lax.ppermute(to_high, "gy", shift_pairs(strips, 1))
    from_high = lax.ppermute(to_low, "gy", shift_pairs(strips, -1))

    def even_branch(step):
        def run(*payloads):
            return tuple(
                lax.ppermute(mine, ("gx", "gy"), swap_pairs(slabs, strips, 0, step + d))
                for d, mine in zip((-1, 0, 1), payloads)
            )

        return run

    blocks = lax.switch(even_step, [even_branch(step) for step in range(strips)], minus, same, plus)
    from_low, from_high, blocks = lax.optimization_barrier((from_low, from_high, blocks))
    window = pl.pallas_call(
        window_kernel,
        out_shape=f32(SENT, LANES),
        in_specs=smem() + vmem(3),
        out_specs=vmem(1)[0],
        scratch_shapes=[scratch(PAYLOAD, WINDOW, LANES)],
        compiler_params=params(SMALL_VMEM),
        name="window",
    )(plane_offsets, from_low, own, from_high)

    def odd_branch(step):
        return lambda mine: lax.ppermute(mine, ("gx", "gy"), swap_pairs(slabs, strips, 1, step))

    odd = lax.switch(odd_step, [odd_branch(step) for step in range(strips)], window)
    return main_planes(plane_offsets, populations, order_pops, from_low, from_high, blocks, odd)


def solution(mesh):
    return jax.shard_map(
        shards,
        mesh=mesh,
        in_specs=(P(None, "gx", "gy", None), P(None, "gx", "gy", None), P()),
        out_specs=(P(None, "gx", "gy", None), P(None, "gx", "gy", None)),
        check_vma=False,
    )
```

```python
import jax
import jax.numpy as jnp
from jax import lax
from jax.experimental import pallas as pl
from jax.experimental.pallas import tpu as pltpu
from jax.sharding import PartitionSpec as P

SHIFT_FRACTION = 0.375
WALL_SPEED = 0.05
RELAX_FLOW = 0.8
RELAX_ORDER = 0.9
BULK_COEFF = 0.05
SURFACE_COEFF = 0.04
MOBILITY = 1.0
VELOCITY_X = (0, 1, -1, 0, 0, 0, 0, 1, -1, 1, -1, 1, -1, 1, -1, 0, 0, 0, 0)
VELOCITY_Y = (0, 0, 0, 1, -1, 0, 0, 1, -1, -1, 1, 0, 0, 0, 0, 1, -1, 1, -1)
VELOCITY_Z = (0, 0, 0, 0, 0, 1, -1, 0, 0, 0, 0, 1, -1, -1, 1, 1, -1, -1, 1)
WEIGHT_TABLE = (1.0 / 3.0,) + (1.0 / 18.0,) * 6 + (1.0 / 36.0,) * 12

VELS = 19
PLANES = 16
ROWS = 8
LANES = 128
UP_X = tuple(i for i in range(VELS) if VELOCITY_X[i] == 1)
DOWN_X = tuple(i for i in range(VELS) if VELOCITY_X[i] == -1)
UP_Y = tuple(i for i in range(VELS) if VELOCITY_Y[i] == 1)
DOWN_Y = tuple(i for i in range(VELS) if VELOCITY_Y[i] == -1)
PAYLOAD = 17
AT_MOMENTS = 5
AT_ORDER = 9
AT_PHASE = 14
WINDOW = 16
WINDOW_PAD = 4

SMALL_VMEM = 16 * 1024 * 1024
MAIN_VMEM = 24 * 1024 * 1024


def roll_rows(cells, step):
    return pltpu.roll(cells, step % cells.shape[0], 0)


def roll_lanes(cells, step):
    return pltpu.roll(cells, step % LANES, cells.ndim - 1)


def moments(flow):
    parts = [flow(i) for i in range(VELS)]
    density = parts[0]
    for part in parts[1:]:
        density = density + part
    speeds = []
    for table in (VELOCITY_X, VELOCITY_Y, VELOCITY_Z):
        plus = [parts[i] for i in range(VELS) if table[i] == 1]
        minus = [parts[i] for i in range(VELS) if table[i] == -1]
        total = plus[0] - minus[0]
        for a, b in zip(plus[1:], minus[1:]):
            total = total + (a - b)
        speeds.append(total)
    return density, speeds


def potential_of(phase, neighbours):
    around = neighbours[0]
    for cells in neighbours[1:]:
        around = around + cells
    bulk = BULK_COEFF * (phase * phase * phase - phase)
    return bulk - SURFACE_COEFF * (around - 6.0 * phase)


def dot_velocity(i, vector):
    total = None
    for sign, part in zip((VELOCITY_X[i], VELOCITY_Y[i], VELOCITY_Z[i]), vector):
        if sign == 0:
            continue
        if total is None:
            total = part if sign == 1 else -part
        else:
            total = total + part if sign == 1 else total - part
    return total


def collide(wanted, flow, order, density, momentum, phase, potential, force):
    inverse = 1.0 / density
    speed = [(momentum[d] + 0.5 * force[d]) * inverse for d in range(3)]
    source = 1.0 - 0.5 / RELAX_FLOW
    relaxed = density * (1.0 / RELAX_FLOW)
    speed_sq = speed[0] * speed[0] + speed[1] * speed[1] + speed[2] * speed[2]
    work = speed[0] * force[0] + speed[1] * force[1] + speed[2] * force[2]
    even = relaxed * (1.0 - 1.5 * speed_sq) - (3.0 * source) * work
    odd = [3.0 * (relaxed * speed[d] + source * force[d]) for d in range(3)]
    quad = [4.5 * relaxed * speed[d] + (9.0 * source) * force[d] for d in range(3)]
    order_even = (3.0 * MOBILITY / RELAX_ORDER) * potential
    carried = (3.0 / RELAX_ORDER) * phase
    order_odd = [carried * speed[d] for d in range(3)]
    flow_out, order_out = {}, {}
    keep_flow = 1.0 - 1.0 / RELAX_FLOW
    keep_order = 1.0 - 1.0 / RELAX_ORDER
    done = set()
    for i in wanted:
        if i in done:
            continue
        weight = WEIGHT_TABLE[i]
        if i == 0:
            flow_out[0] = keep_flow * flow(0) + weight * even
            rest = phase - (2.0 * MOBILITY) * potential
            order_out[0] = keep_order * order(0) + (1.0 / RELAX_ORDER) * rest
            continue
        first = i if i % 2 == 1 else i - 1
        pair_even = weight * (even + dot_velocity(first, speed) * dot_velocity(first, quad))
        pair_odd = weight * dot_velocity(first, odd)
        pair_order = weight * dot_velocity(first, order_odd)
        for member, sign in ((first, 1), (first + 1, -1)):
            if member not in wanted:
                continue
            done.add(member)
            both = pair_even + pair_odd if sign == 1 else pair_even - pair_odd
            flow_out[member] = keep_flow * flow(member) + both
            both = weight * order_even
            both = both + pair_order if sign == 1 else both - pair_order
            order_out[member] = keep_order * order(member) + both
    return flow_out, order_out


def add_phase(phase_ref, order_ref, x):
    total = order_ref[0, x]
    for i in range(1, VELS):
        total = total + order_ref[i, x]
    phase_ref[x] = total


def plane_copies(source, target, sems, pieces):
    return [
        pltpu.make_async_copy(source.at[:, pl.ds(first, count)], target.at[:, pl.ds(first, count)], sems.at[index])
        for index, (first, count) in enumerate(pieces)
    ]


SENT_ROWS = 11
SENT_SKIP = 2
SENT = ROWS + AT_PHASE * SENT_ROWS + 3 * (WINDOW - 1) + 1


def window_row(index):
    if index < AT_PHASE:
        return ROWS - SENT_SKIP + index * SENT_ROWS
    return ROWS + AT_PHASE * SENT_ROWS + (index - AT_PHASE) * (WINDOW - 1)


STORES = ((3, 5), (8, 5), (0, 3), (PLANES - 3, 3))


def even_boundary(slab):
    return slab + 1 - slab % 2


def odd_boundary(slab, slabs):
    return lax.rem(slab + slab % 2, slabs)


WIDE_ROWS, NARROW_ROWS = 6, 4
WIDE_PACK, NARROW_PACK = 112, 88


def pack_row(index, rows):
    return (index - AT_PHASE) * ROWS if index >= AT_PHASE else 3 * ROWS + index * rows


def put_rows(pack_ref, index, rows, block_ref, is_even, when_even, when_odd):
    start = pack_row(index, rows)
    if index >= AT_PHASE:
        pack_ref[start : start + ROWS, :] = block_ref[index]
    else:
        pack_ref[start : start + rows, :] = jnp.where(
            is_even, block_ref[index, when_even : when_even + rows, :], block_ref[index, when_odd : when_odd + rows, :]
        )


def packed_block(pack_ref, index, rows, kept_from):
    start = pack_row(index, rows) - (0 if index >= AT_PHASE else kept_from)
    return pack_ref[start : start + ROWS, :]


SIDE = PAYLOAD * PLANES


def side_rows(index, base=0):
    return pl.ds(base + index * PLANES, PLANES)


def side_row(ref, index, x):
    return ref[pl.ds(index * PLANES + x, 1), :]


def payload_kernel(flow_ref, order_ref, minus_ref, even_ref, plus_ref, odd_ref, wide_ref, narrow_ref, phase_ref):
    is_even = lax.axis_index("gx") % 2 == 0
    for x in range(PLANES):
        add_phase(phase_ref, order_ref, x)
    sides = []
    for plane, inward, comps in ((PLANES - 1, -1, UP_X), (0, 1, DOWN_X)):
        density, momentum = moments(lambda i: flow_ref[i, plane])
        parts = [flow_ref[i, plane] for i in comps] + [density] + momentum
        parts += [order_ref[i, plane] for i in comps]
        parts += [phase_ref[plane + inward * d] for d in range(3)]
        sides.append(parts)
    for index, (last, first) in enumerate(zip(*sides)):
        even_ref[index] = jnp.where(is_even, last, first)
        odd_ref[index] = jnp.where(is_even, first, last)
        put_rows(minus_ref, index, WIDE_ROWS, even_ref, is_even, 0, ROWS - WIDE_ROWS)
        put_rows(plus_ref, index, NARROW_ROWS, even_ref, is_even, ROWS - NARROW_ROWS, 0)
        put_rows(wide_ref, index, WIDE_ROWS, odd_ref, is_even, ROWS - WIDE_ROWS, 0)
        put_rows(narrow_ref, index, NARROW_ROWS, odd_ref, is_even, 0, ROWS - NARROW_ROWS)
    edges = []
    for row, inward, comps in ((ROWS - 1, -1, UP_Y), (0, 1, DOWN_Y)):
        density, momentum = moments(lambda i: flow_ref[i, :, row, :])
        parts = [flow_ref[i, :, row, :] for i in comps] + [density] + momentum
        parts += [order_ref[i, :, row, :] for i in comps]
        parts += [phase_ref[:, row + inward * d, :] for d in range(3)]
        edges.append(parts)
    for index, (high, low) in enumerate(zip(*edges)):
        wide_ref[side_rows(index, WIDE_PACK), :] = jnp.where(is_even, high, low)
        narrow_ref[side_rows(index, NARROW_PACK), :] = jnp.where(is_even, low, high)


def window_kernel(offset_ref, wide_ref, own_ref, narrow_ref, out_ref, window_ref):
    slab = lax.axis_index("gx")
    is_even = slab % 2 == 0
    inner = lax.rem(offset_ref[odd_boundary(slab, offset_ref.shape[0])] + 5, ROWS)

    blocks = [
        lambda index: jnp.where(
            is_even,
            packed_block(wide_ref, index, WIDE_ROWS, ROWS - WIDE_ROWS),
            packed_block(narrow_ref, index, NARROW_ROWS, ROWS - NARROW_ROWS),
        ),
        lambda index: own_ref[index],
        lambda index: jnp.where(
            is_even, packed_block(narrow_ref, index, NARROW_ROWS, 0), packed_block(wide_ref, index, WIDE_ROWS, 0)
        ),
    ]
    cut_window(blocks, jnp.where(is_even, inner, 9 - inner), window_ref)
    out_ref[0:ROWS, :] = window_ref[0, 0:ROWS]
    for index in range(PAYLOAD):
        first, count = (SENT_SKIP, SENT_ROWS) if index < AT_PHASE else (0, WINDOW)
        start = window_row(index) + first
        out_ref[start : start + count, :] = window_ref[index, first : first + count, :]


def cut_window(blocks, start, window_ref):
    row = lax.broadcasted_iota(jnp.int32, (ROWS, LANES), 0)
    inner = lax.rem(start, ROWS)
    back = lax.rem(ROWS - inner, ROWS)
    early = row < ROWS - inner
    near = start < ROWS
    for index in range(PAYLOAD):
        rolled = [pltpu.roll(block(index), back, 0) for block in blocks]
        first = jnp.where(near, rolled[0], rolled[1])
        second = jnp.where(near, rolled[1], rolled[2])
        window_ref[index, 0:ROWS] = jnp.where(early, first, second)
        window_ref[index, ROWS : 2 * ROWS] = jnp.where(early, second, rolled[2])


def ghost_plane(window_ref, comps, own, own_next, weight, kick_speed):
    other = 1.0 - weight

    def sheared(cells):
        return weight * cells + other * roll_rows(cells, 1)

    def seen(cells):
        return other * roll_rows(cells, -1) + weight * cells

    def sides(cells):
        return [roll_rows(cells, 1), roll_rows(cells, -1), roll_lanes(cells, 1), roll_lanes(cells, -1)]

    near, second, third = [window_ref[AT_PHASE + d] for d in range(3)]
    ghost_phase = sheared(near)
    own_potential = potential_of(own, [own_next, ghost_phase] + sides(own))
    near_potential = potential_of(near, [second, seen(own)] + sides(near))
    second_potential = potential_of(second, [third, near] + sides(second))
    beyond = seen(own_potential)
    outward = 1.0 if VELOCITY_X[comps[0]] == 1 else -1.0
    half = -0.5 * near
    force = [
        outward * half * (beyond - second_potential),
        half * (roll_rows(near_potential, -1) - roll_rows(near_potential, 1)),
        half * (roll_lanes(near_potential, -1) - roll_lanes(near_potential, 1)),
    ]
    density = window_ref[AT_MOMENTS]
    momentum = [window_ref[AT_MOMENTS + 1 + d] for d in range(3)]
    flow_out, order_out = collide(
        comps,
        lambda i: window_ref[comps.index(i)],
        lambda i: window_ref[AT_ORDER + comps.index(i)],
        density,
        momentum,
        near,
        near_potential,
        force,
    )
    flow_ghost = []
    for i in comps:
        cells = flow_out[i]
        if VELOCITY_Y[i] != 0:
            cells = cells + (WEIGHT_TABLE[i] * 3.0 * VELOCITY_Y[i] * kick_speed) * density
        flow_ghost.append(sheared(cells))
    order_ghost = [sheared(order_out[i]) for i in comps]
    return ghost_phase, own_potential, sheared(near_potential), flow_ghost, order_ghost


def rows_before(cells, line):
    row = lax.broadcasted_iota(jnp.int32, (ROWS, LANES), 0)
    return jnp.where(row == 0, line, roll_rows(cells, 1))


def rows_after(cells, line):
    row = lax.broadcasted_iota(jnp.int32, (ROWS, LANES), 0)
    return jnp.where(row == ROWS - 1, line, roll_rows(cells, -1))


def collide_sides(phase_ref, low_ref, high_ref, below, above, low_side, high_side, edge_ref):
    plane_at = lax.broadcasted_iota(jnp.int32, (PLANES, LANES), 0)

    def across(cells, which, own_row):
        before, after = roll_rows(cells, 1), roll_rows(cells, -1)
        if below is not None:
            before = jnp.where(plane_at == 0, below(which, own_row), before)
            after = jnp.where(plane_at == PLANES - 1, above(which, own_row), after)
        return before, after

    for side_ref, out_ref, edge, beside, inward, comps in (
        (low_ref, low_side, 0, -1, 1, UP_Y),
        (high_ref, high_side, ROWS - 1, ROWS, -1, DOWN_Y),
    ):
        own = [phase_ref[:, edge + inward * d, :] for d in range(2)]
        outer = [side_ref[side_rows(AT_PHASE + d), :] for d in range(3)]
        lines = [own[1], own[0]] + outer
        potentials = []
        for index in range(1, 4):
            cells = lines[index]
            around = list(across(cells, 0, edge + inward * (1 - index)))
            around += [lines[index - 1], lines[index + 1], roll_lanes(cells, 1), roll_lanes(cells, -1)]
            potentials.append(potential_of(cells, around))
        inside, here, outside = potentials
        before, after = across(here, 1, beside)
        half = -0.5 * outer[0]
        force = [
            half * (after - before),
            (inward * half) * (inside - outside),
            half * (roll_lanes(here, -1) - roll_lanes(here, 1)),
        ]
        flow_post, order_post = collide(
            comps,
            lambda i: side_ref[side_rows(comps.index(i)), :],
            lambda i: side_ref[side_rows(AT_ORDER + comps.index(i)), :],
            side_ref[side_rows(AT_MOMENTS), :],
            [side_ref[side_rows(AT_MOMENTS + 1 + d), :] for d in range(3)],
            outer[0],
            here,
            force,
        )
        for index, i in enumerate(comps):
            out_ref[index] = flow_post[i]
            out_ref[5 + index] = order_post[i]
        edge_ref[0 if inward == 1 else 1] = here


def plane_potential(phase_ref, low_ref, high_ref, x):
    cells = phase_ref[x]
    around = [
        phase_ref[x - 1],
        phase_ref[x + 1],
        rows_before(cells, side_row(low_ref, AT_PHASE, x)),
        rows_after(cells, side_row(high_ref, AT_PHASE, x)),
        roll_lanes(cells, 1),
        roll_lanes(cells, -1),
    ]
    return potential_of(cells, around)


def collide_plane(x, skip, flow_ref, order_ref, phase_ref, potential_ref, edge_ref, low_side, high_side, flow_out, order_out):
    here = potential_ref[x + 1]
    phase = phase_ref[x]
    half = -0.5 * phase
    along_y = rows_after(here, edge_ref[1, pl.ds(x, 1), :]) - rows_before(here, edge_ref[0, pl.ds(x, 1), :])
    force = [
        half * (potential_ref[x + 2] - potential_ref[x]),
        half * along_y,
        half * (roll_lanes(here, -1) - roll_lanes(here, 1)),
    ]
    density, momentum = moments(lambda i: flow_ref[i, x])
    flow_post, order_post = collide(
        tuple(i for i in range(VELS) if VELOCITY_X[i] == 0 or VELOCITY_X[i] != skip),
        lambda i: flow_ref[i, x],
        lambda i: order_ref[i, x],
        density,
        momentum,
        phase,
        here,
        force,
    )

    def moved(i, cells, first):
        if VELOCITY_Y[i] == 1:
            cells = rows_before(cells, low_side[first + UP_Y.index(i), pl.ds(x, 1), :])
        elif VELOCITY_Y[i] == -1:
            cells = rows_after(cells, high_side[first + DOWN_Y.index(i), pl.ds(x, 1), :])
        if VELOCITY_Z[i] != 0:
            cells = roll_lanes(cells, VELOCITY_Z[i])
        return cells

    for i in flow_post:
        target = x + VELOCITY_X[i]
        flow_out[i, target] = moved(i, flow_post[i], 0)
        order_out[i, target] = moved(i, order_post[i], 5)


def main_kernel(
    offset_hbm, flow_ref, order_ref, wide_pack, narrow_pack, minus_hbm, same_hbm, plus_hbm, odd_hbm, flow_hbm_out, order_hbm_out,
    offset_ref, minus_ref, same_ref, plus_ref, odd_ref, low_ref, high_ref, flow_out, order_out, phase_ref, below_ref, above_ref, wide_ref, ghost_ref, potential_ref, low_side, high_side, edge_ref,
    arrival_sems, flow_out_sems, order_out_sems,
):
    pairs = ((minus_hbm, minus_ref), (same_hbm, same_ref), (plus_hbm, plus_ref), (odd_hbm, odd_ref))
    pairs += ((offset_hbm, offset_ref),)
    arrivals = [pltpu.make_async_copy(a, b, arrival_sems.at[index]) for index, (a, b) in enumerate(pairs)]
    for copy in arrivals:
        copy.start()
    flow_writes = plane_copies(flow_out, flow_hbm_out, flow_out_sems, STORES)
    order_writes = plane_copies(order_out, order_hbm_out, order_out_sems, STORES)

    def one_plane(x, skip):
        collide_plane(
            x, skip, flow_ref, order_ref, phase_ref, potential_ref, edge_ref, low_side, high_side, flow_out, order_out
        )

    slab = lax.axis_index("gx")
    is_even = slab % 2 == 0
    for index in range(PAYLOAD):
        wide, narrow = wide_pack[side_rows(index, WIDE_PACK), :], narrow_pack[side_rows(index, NARROW_PACK), :]
        low_ref[side_rows(index), :] = jnp.where(is_even, wide, narrow)
        high_ref[side_rows(index), :] = jnp.where(is_even, narrow, wide)
    for x in range(PLANES):
        add_phase(phase_ref, order_ref, x)
    collide_sides(phase_ref, low_ref, high_ref, None, None, low_side, high_side, edge_ref)
    for x in range(1, PLANES - 1):
        potential_ref[x + 1] = plane_potential(phase_ref, low_ref, high_ref, x)

    def step(x, carry):
        one_plane(x, 0)
        for part, (first, count) in enumerate(STORES[:-2]):

            @pl.when(x == first + count)
            def _(part=part):
                flow_writes[part].start()
                order_writes[part].start()

        return carry

    lax.fori_loop(2, PLANES - 2, step, 0, unroll=2)
    for copy in arrivals:
        copy.wait()
    inner = lax.rem(offset_ref[even_boundary(slab)] + 5, ROWS)
    blocks = [
        lambda at: jnp.where(
            is_even,
            packed_block(minus_ref, at, WIDE_ROWS, ROWS - WIDE_ROWS),
            packed_block(plus_ref, at, NARROW_ROWS, ROWS - NARROW_ROWS),
        ),
        lambda at: same_ref[at],
        lambda at: jnp.where(
            is_even, packed_block(plus_ref, at, NARROW_ROWS, 0), packed_block(minus_ref, at, WIDE_ROWS, 0)
        ),
    ]
    cut_window(blocks, jnp.where(is_even, inner, 9 - inner), above_ref)
    for index in range(PAYLOAD):
        start = window_row(index)
        even, odd = above_ref[index], odd_ref[start : start + WINDOW, :]
        below_ref[index] = jnp.where(is_even, odd, even)
        above_ref[index] = jnp.where(is_even, even, odd)

    for index, plane in enumerate((0, 1, PLANES - 1, PLANES - 2)):
        wide_ref[index] = jnp.zeros((WINDOW, LANES), jnp.float32)
        for d in range(3):
            wide_ref[index, 3 - d : 4 - d, :] = side_row(low_ref, AT_PHASE + d, plane)
            wide_ref[index, 12 + d : 13 + d, :] = side_row(high_ref, AT_PHASE + d, plane)
        wide_ref[index, 4:12, :] = phase_ref[plane]
    below = ghost_plane(below_ref, UP_X, wide_ref[0], wide_ref[1], 1.0 - SHIFT_FRACTION, WALL_SPEED)
    above = ghost_plane(above_ref, DOWN_X, wide_ref[2], wide_ref[3], SHIFT_FRACTION, -WALL_SPEED)
    for index in range(5):
        ghost_ref[index] = below[3][index]
        ghost_ref[5 + index] = below[4][index]
        ghost_ref[10 + index] = above[3][index]
        ghost_ref[15 + index] = above[4][index]

    def ghost_row(ghost):
        return lambda which, own_row: ghost[2 * which][own_row + WINDOW_PAD : own_row + WINDOW_PAD + 1, :]

    collide_sides(
        phase_ref, low_ref, high_ref, ghost_row(below), ghost_row(above), low_side, high_side, edge_ref
    )
    wide_ref[0] = below[1]
    wide_ref[1] = below[2]
    wide_ref[2] = above[1]
    wide_ref[3] = above[2]
    potential_ref[1] = wide_ref[0, 4:12, :]
    potential_ref[0] = wide_ref[1, 4:12, :]
    potential_ref[PLANES] = wide_ref[2, 4:12, :]
    potential_ref[PLANES + 1] = wide_ref[3, 4:12, :]
    for comps, first, target in ((UP_X, 0, 0), (DOWN_X, 10, PLANES - 1)):
        for index, i in enumerate(comps):
            start = WINDOW_PAD - VELOCITY_Y[i]
            for out_ref, at in ((flow_out, first + index), (order_out, first + 5 + index)):
                cells = ghost_ref[at, start : start + ROWS, :]
                if VELOCITY_Z[i] != 0:
                    cells = roll_lanes(cells, VELOCITY_Z[i])
                out_ref[i, target] = cells
    one_plane(0, -1)
    one_plane(1, 0)
    flow_writes[-2].start()
    order_writes[-2].start()
    one_plane(PLANES - 2, 0)
    one_plane(PLANES - 1, 1)
    flow_writes[-1].start()
    order_writes[-1].start()
    for copy in flow_writes + order_writes:
        copy.wait()


def vmem(count):
    return [pl.BlockSpec(memory_space=pltpu.VMEM)] * count


def params(limit):
    return pltpu.CompilerParams(vmem_limit_bytes=limit)


def f32(*shape):
    return jax.ShapeDtypeStruct(shape, jnp.float32)


def turn_pairs(slabs, strips, step):
    pairs = []
    for slab in range(slabs):
        for strip in range(strips):
            other = (strip + (step if slab % 2 == 0 else -step)) % strips
            pairs.append((slab * strips + strip, slab * strips + other))
    return pairs


def swap_pairs(slabs, strips, first, step):
    pairs = []
    for low in range(first, slabs, 2):
        high = (low + 1) % slabs
        for strip in range(strips):
            other = (strip + step) % strips
            pairs.append((low * strips + strip, high * strips + other))
            pairs.append((high * strips + other, low * strips + strip))
    return pairs


def hbm(count):
    return [pl.BlockSpec(memory_space=pltpu.HBM)] * count


def smem():
    return [pl.BlockSpec(memory_space=pltpu.SMEM)]


def scratch(*shape):
    return pltpu.VMEM(shape, jnp.float32)


def sems(count):
    return pltpu.SemaphoreType.DMA((count,))


def main_planes(plane_offsets, flow, order, wide, narrow, blocks, odd):
    return pl.pallas_call(
        main_kernel,
        out_shape=(f32(*flow.shape), f32(*order.shape)),
        in_specs=hbm(1) + vmem(4) + hbm(4),
        out_specs=tuple(hbm(2)),
        scratch_shapes=[
            pltpu.SMEM(plane_offsets.shape, jnp.int32),
            scratch(WIDE_PACK, LANES),
            scratch(PAYLOAD, ROWS, LANES),
            scratch(NARROW_PACK, LANES),
            scratch(SENT, LANES),
            scratch(SIDE, LANES),
            scratch(SIDE, LANES),
            scratch(*flow.shape),
            scratch(*order.shape),
            scratch(PLANES, ROWS, LANES),
            scratch(PAYLOAD, WINDOW, LANES),
            scratch(PAYLOAD, WINDOW, LANES),
            scratch(4, WINDOW, LANES),
            scratch(20, WINDOW, LANES),
            scratch(PLANES + 2, ROWS, LANES),
            scratch(10, PLANES, LANES),
            scratch(10, PLANES, LANES),
            scratch(2, PLANES, LANES),
            sems(5),
            sems(len(STORES)),
            sems(len(STORES)),
        ],
        compiler_params=params(MAIN_VMEM),
        name="collide_stream",
    )(plane_offsets, flow, order, wide, narrow, *blocks, odd)


def shards(populations, order_pops, plane_offsets):
    slabs, strips = lax.axis_size("gx"), lax.axis_size("gy")
    slab = lax.axis_index("gx")
    shifts = ((plane_offsets + 5) // ROWS) % strips
    boundary = lax.iota(jnp.int32, slabs)
    at_even = jnp.where(boundary == (slab | 1), strips, 0)
    at_odd = jnp.where(boundary == ((slab + (slab & 1)) & (slabs - 1)), 1, 0)
    code = jnp.sum(shifts * (at_even + at_odd)).astype(jnp.uint32)
    even_step = (code // jnp.uint32(strips)).astype(jnp.int32)
    odd_step = lax.rem(code, jnp.uint32(strips)).astype(jnp.int32)

    minus, same, plus, own, wide, narrow = pl.pallas_call(
        payload_kernel,
        out_shape=(
            f32(WIDE_PACK, LANES),
            f32(PAYLOAD, ROWS, LANES),
            f32(NARROW_PACK, LANES),
            f32(PAYLOAD, ROWS, LANES),
            f32(WIDE_PACK + SIDE, LANES),
            f32(NARROW_PACK + SIDE, LANES),
        ),
        in_specs=vmem(2),
        out_specs=tuple(vmem(6)),
        scratch_shapes=[scratch(PLANES, ROWS, LANES)],
        compiler_params=params(SMALL_VMEM),
        name="payloads",
    )(populations, order_pops)

    wide = lax.ppermute(wide, ("gx", "gy"), turn_pairs(slabs, strips, 1))
    narrow = lax.ppermute(narrow, ("gx", "gy"), turn_pairs(slabs, strips, -1))

    def even_branch(step):
        def run(*payloads):
            return tuple(
                lax.ppermute(mine, ("gx", "gy"), swap_pairs(slabs, strips, 0, step + d))
                for d, mine in zip((-1, 0, 1), payloads)
            )

        return run

    blocks = lax.switch(even_step, [even_branch(step) for step in range(strips)], minus, same, plus)
    wide, narrow, blocks = lax.optimization_barrier((wide, narrow, blocks))
    window = pl.pallas_call(
        window_kernel,
        out_shape=f32(SENT, LANES),
        in_specs=smem() + vmem(3),
        out_specs=vmem(1)[0],
        scratch_shapes=[scratch(PAYLOAD, WINDOW, LANES)],
        compiler_params=params(SMALL_VMEM),
        name="window",
    )(plane_offsets, wide, own, narrow)

    def odd_branch(step):
        return lambda mine: lax.ppermute(mine, ("gx", "gy"), swap_pairs(slabs, strips, 1, step))

    odd = lax.switch(odd_step, [odd_branch(step) for step in range(strips)], window)
    return main_planes(plane_offsets, populations, order_pops, wide, narrow, blocks, odd)


def solution(mesh):
    return jax.shard_map(
        shards,
        mesh=mesh,
        in_specs=(P(None, "gx", "gy", None), P(None, "gx", "gy", None), P()),
        out_specs=(P(None, "gx", "gy", None), P(None, "gx", "gy", None)),
        check_vma=False,
    )
```

```python
import jax
import jax.numpy as jnp
from jax import lax
from jax.experimental import pallas as pl
from jax.experimental.pallas import tpu as pltpu
from jax.sharding import PartitionSpec as P

SHIFT_FRACTION = 0.375
WALL_SPEED = 0.05
RELAX_FLOW = 0.8
RELAX_ORDER = 0.9
BULK_COEFF = 0.05
SURFACE_COEFF = 0.04
MOBILITY = 1.0
VELOCITY_X = (0, 1, -1, 0, 0, 0, 0, 1, -1, 1, -1, 1, -1, 1, -1, 0, 0, 0, 0)
VELOCITY_Y = (0, 0, 0, 1, -1, 0, 0, 1, -1, -1, 1, 0, 0, 0, 0, 1, -1, 1, -1)
VELOCITY_Z = (0, 0, 0, 0, 0, 1, -1, 0, 0, 0, 0, 1, -1, -1, 1, 1, -1, -1, 1)
WEIGHT_TABLE = (1.0 / 3.0,) + (1.0 / 18.0,) * 6 + (1.0 / 36.0,) * 12

VELS = 19
PLANES = 16
ROWS = 8
LANES = 128
UP_X = tuple(i for i in range(VELS) if VELOCITY_X[i] == 1)
DOWN_X = tuple(i for i in range(VELS) if VELOCITY_X[i] == -1)
UP_Y = tuple(i for i in range(VELS) if VELOCITY_Y[i] == 1)
DOWN_Y = tuple(i for i in range(VELS) if VELOCITY_Y[i] == -1)
PAYLOAD = 17
AT_MOMENTS = 5
AT_ORDER = 9
AT_PHASE = 14
WINDOW = 16
WINDOW_PAD = 4

SMALL_VMEM = 16 * 1024 * 1024
MAIN_VMEM = 24 * 1024 * 1024


def roll_rows(cells, step):
    return pltpu.roll(cells, step % cells.shape[0], 0)


def roll_lanes(cells, step):
    return pltpu.roll(cells, step % LANES, cells.ndim - 1)


def moments(flow):
    parts = [flow(i) for i in range(VELS)]
    density = parts[0]
    for part in parts[1:]:
        density = density + part
    speeds = []
    for table in (VELOCITY_X, VELOCITY_Y, VELOCITY_Z):
        plus = [parts[i] for i in range(VELS) if table[i] == 1]
        minus = [parts[i] for i in range(VELS) if table[i] == -1]
        total = plus[0] - minus[0]
        for a, b in zip(plus[1:], minus[1:]):
            total = total + (a - b)
        speeds.append(total)
    return density, speeds


def potential_of(phase, neighbours):
    around = neighbours[0]
    for cells in neighbours[1:]:
        around = around + cells
    bulk = BULK_COEFF * (phase * phase * phase - phase)
    return bulk - SURFACE_COEFF * (around - 6.0 * phase)


def dot_velocity(i, vector):
    total = None
    for sign, part in zip((VELOCITY_X[i], VELOCITY_Y[i], VELOCITY_Z[i]), vector):
        if sign == 0:
            continue
        if total is None:
            total = part if sign == 1 else -part
        else:
            total = total + part if sign == 1 else total - part
    return total


def collide(wanted, flow, order, density, momentum, phase, potential, force):
    inverse = 1.0 / density
    speed = [(momentum[d] + 0.5 * force[d]) * inverse for d in range(3)]
    source = 1.0 - 0.5 / RELAX_FLOW
    relaxed = density * (1.0 / RELAX_FLOW)
    speed_sq = speed[0] * speed[0] + speed[1] * speed[1] + speed[2] * speed[2]
    work = speed[0] * force[0] + speed[1] * force[1] + speed[2] * force[2]
    even = relaxed * (1.0 - 1.5 * speed_sq) - (3.0 * source) * work
    odd = [3.0 * (relaxed * speed[d] + source * force[d]) for d in range(3)]
    quad = [4.5 * relaxed * speed[d] + (9.0 * source) * force[d] for d in range(3)]
    order_even = (3.0 * MOBILITY / RELAX_ORDER) * potential
    carried = (3.0 / RELAX_ORDER) * phase
    order_odd = [carried * speed[d] for d in range(3)]
    flow_out, order_out = {}, {}
    keep_flow = 1.0 - 1.0 / RELAX_FLOW
    keep_order = 1.0 - 1.0 / RELAX_ORDER
    done = set()
    for i in wanted:
        if i in done:
            continue
        weight = WEIGHT_TABLE[i]
        if i == 0:
            flow_out[0] = keep_flow * flow(0) + weight * even
            rest = phase - (2.0 * MOBILITY) * potential
            order_out[0] = keep_order * order(0) + (1.0 / RELAX_ORDER) * rest
            continue
        first = i if i % 2 == 1 else i - 1
        pair_even = weight * (even + dot_velocity(first, speed) * dot_velocity(first, quad))
        pair_odd = weight * dot_velocity(first, odd)
        pair_order = weight * dot_velocity(first, order_odd)
        for member, sign in ((first, 1), (first + 1, -1)):
            if member not in wanted:
                continue
            done.add(member)
            both = pair_even + pair_odd if sign == 1 else pair_even - pair_odd
            flow_out[member] = keep_flow * flow(member) + both
            both = weight * order_even
            both = both + pair_order if sign == 1 else both - pair_order
            order_out[member] = keep_order * order(member) + both
    return flow_out, order_out


def add_phase(phase_ref, order_ref, x):
    total = order_ref[0, x]
    for i in range(1, VELS):
        total = total + order_ref[i, x]
    phase_ref[x] = total


def plane_copies(source, target, sems, pieces):
    return [
        pltpu.make_async_copy(source.at[:, pl.ds(first, count)], target.at[:, pl.ds(first, count)], sems.at[index])
        for index, (first, count) in enumerate(pieces)
    ]


SENT_ROWS = 11
SENT_SKIP = 2
SENT = ROWS + AT_PHASE * SENT_ROWS + 3 * (WINDOW - 1) + 1


def window_row(index):
    if index < AT_PHASE:
        return ROWS - SENT_SKIP + index * SENT_ROWS
    return ROWS + AT_PHASE * SENT_ROWS + (index - AT_PHASE) * (WINDOW - 1)


STORES = ((3, 4), (7, 6), (0, 3), (PLANES - 3, 3))


def even_boundary(slab):
    return slab + 1 - slab % 2


def odd_boundary(slab, slabs):
    return lax.rem(slab + slab % 2, slabs)


WIDE_ROWS, NARROW_ROWS = 6, 4
WIDE_PACK, NARROW_PACK = 112, 88


def pack_row(index, rows):
    return (index - AT_PHASE) * ROWS if index >= AT_PHASE else 3 * ROWS + index * rows


def put_rows(pack_ref, index, rows, block_ref, is_even, when_even, when_odd):
    start = pack_row(index, rows)
    if index >= AT_PHASE:
        pack_ref[start : start + ROWS, :] = block_ref[index]
    else:
        pack_ref[start : start + rows, :] = jnp.where(
            is_even, block_ref[index, when_even : when_even + rows, :], block_ref[index, when_odd : when_odd + rows, :]
        )


def packed_block(pack_ref, index, rows, kept_from):
    start = pack_row(index, rows) - (0 if index >= AT_PHASE else kept_from)
    return pack_ref[start : start + ROWS, :]


SIDE = PAYLOAD * PLANES


def side_rows(index, base=0):
    return pl.ds(base + index * PLANES, PLANES)


def side_row(ref, index, x):
    return ref[pl.ds(index * PLANES + x, 1), :]


def payload_kernel(flow_ref, order_ref, minus_ref, even_ref, plus_ref, odd_ref, wide_ref, narrow_ref, phase_ref):
    is_even = lax.axis_index("gx") % 2 == 0
    for x in range(PLANES):
        add_phase(phase_ref, order_ref, x)
    sides = []
    for plane, inward, comps in ((PLANES - 1, -1, UP_X), (0, 1, DOWN_X)):
        density, momentum = moments(lambda i: flow_ref[i, plane])
        parts = [flow_ref[i, plane] for i in comps] + [density] + momentum
        parts += [order_ref[i, plane] for i in comps]
        parts += [phase_ref[plane + inward * d] for d in range(3)]
        sides.append(parts)
    for index, (last, first) in enumerate(zip(*sides)):
        even_ref[index] = jnp.where(is_even, last, first)
        odd_ref[index] = jnp.where(is_even, first, last)
        put_rows(minus_ref, index, WIDE_ROWS, even_ref, is_even, 0, ROWS - WIDE_ROWS)
        put_rows(plus_ref, index, NARROW_ROWS, even_ref, is_even, ROWS - NARROW_ROWS, 0)
        put_rows(wide_ref, index, WIDE_ROWS, odd_ref, is_even, ROWS - WIDE_ROWS, 0)
        put_rows(narrow_ref, index, NARROW_ROWS, odd_ref, is_even, 0, ROWS - NARROW_ROWS)
    edges = []
    for row, inward, comps in ((ROWS - 1, -1, UP_Y), (0, 1, DOWN_Y)):
        density, momentum = moments(lambda i: flow_ref[i, :, row, :])
        parts = [flow_ref[i, :, row, :] for i in comps] + [density] + momentum
        parts += [order_ref[i, :, row, :] for i in comps]
        parts += [phase_ref[:, row + inward * d, :] for d in range(3)]
        edges.append(parts)
    for index, (high, low) in enumerate(zip(*edges)):
        wide_ref[side_rows(index, WIDE_PACK), :] = jnp.where(is_even, high, low)
        narrow_ref[side_rows(index, NARROW_PACK), :] = jnp.where(is_even, low, high)


def window_kernel(offset_ref, wide_ref, own_ref, narrow_ref, out_ref, window_ref):
    slab = lax.axis_index("gx")
    is_even = slab % 2 == 0
    inner = lax.rem(offset_ref[odd_boundary(slab, offset_ref.shape[0])] + 5, ROWS)

    blocks = [
        lambda index: jnp.where(
            is_even,
            packed_block(wide_ref, index, WIDE_ROWS, ROWS - WIDE_ROWS),
            packed_block(narrow_ref, index, NARROW_ROWS, ROWS - NARROW_ROWS),
        ),
        lambda index: own_ref[index],
        lambda index: jnp.where(
            is_even, packed_block(narrow_ref, index, NARROW_ROWS, 0), packed_block(wide_ref, index, WIDE_ROWS, 0)
        ),
    ]
    cut_window(blocks, jnp.where(is_even, inner, 9 - inner), window_ref)
    out_ref[0:ROWS, :] = window_ref[0, 0:ROWS]
    for index in range(PAYLOAD):
        first, count = (SENT_SKIP, SENT_ROWS) if index < AT_PHASE else (0, WINDOW)
        start = window_row(index) + first
        out_ref[start : start + count, :] = window_ref[index, first : first + count, :]


def cut_window(blocks, start, window_ref):
    row = lax.broadcasted_iota(jnp.int32, (ROWS, LANES), 0)
    inner = lax.rem(start, ROWS)
    back = lax.rem(ROWS - inner, ROWS)
    early = row < ROWS - inner
    near = start < ROWS
    for index in range(PAYLOAD):
        rolled = [pltpu.roll(block(index), back, 0) for block in blocks]
        first = jnp.where(near, rolled[0], rolled[1])
        second = jnp.where(near, rolled[1], rolled[2])
        window_ref[index, 0:ROWS] = jnp.where(early, first, second)
        window_ref[index, ROWS : 2 * ROWS] = jnp.where(early, second, rolled[2])


def ghost_plane(window_ref, comps, own, own_next, weight, kick_speed):
    other = 1.0 - weight

    def sheared(cells):
        return weight * cells + other * roll_rows(cells, 1)

    def seen(cells):
        return other * roll_rows(cells, -1) + weight * cells

    def sides(cells):
        return [roll_rows(cells, 1), roll_rows(cells, -1), roll_lanes(cells, 1), roll_lanes(cells, -1)]

    near, second, third = [window_ref[AT_PHASE + d] for d in range(3)]
    ghost_phase = sheared(near)
    own_potential = potential_of(own, [own_next, ghost_phase] + sides(own))
    near_potential = potential_of(near, [second, seen(own)] + sides(near))
    second_potential = potential_of(second, [third, near] + sides(second))
    beyond = seen(own_potential)
    outward = 1.0 if VELOCITY_X[comps[0]] == 1 else -1.0
    half = -0.5 * near
    force = [
        outward * half * (beyond - second_potential),
        half * (roll_rows(near_potential, -1) - roll_rows(near_potential, 1)),
        half * (roll_lanes(near_potential, -1) - roll_lanes(near_potential, 1)),
    ]
    density = window_ref[AT_MOMENTS]
    momentum = [window_ref[AT_MOMENTS + 1 + d] for d in range(3)]
    flow_out, order_out = collide(
        comps,
        lambda i: window_ref[comps.index(i)],
        lambda i: window_ref[AT_ORDER + comps.index(i)],
        density,
        momentum,
        near,
        near_potential,
        force,
    )
    flow_ghost = []
    for i in comps:
        cells = flow_out[i]
        if VELOCITY_Y[i] != 0:
            cells = cells + (WEIGHT_TABLE[i] * 3.0 * VELOCITY_Y[i] * kick_speed) * density
        flow_ghost.append(sheared(cells))
    order_ghost = [sheared(order_out[i]) for i in comps]
    return ghost_phase, own_potential, sheared(near_potential), flow_ghost, order_ghost


def rows_before(cells, line):
    row = lax.broadcasted_iota(jnp.int32, (ROWS, LANES), 0)
    return jnp.where(row == 0, line, roll_rows(cells, 1))


def rows_after(cells, line):
    row = lax.broadcasted_iota(jnp.int32, (ROWS, LANES), 0)
    return jnp.where(row == ROWS - 1, line, roll_rows(cells, -1))


def collide_sides(phase_ref, low_ref, high_ref, below, above, low_side, high_side, edge_ref):
    plane_at = lax.broadcasted_iota(jnp.int32, (PLANES, LANES), 0)

    def across(cells, which, own_row):
        before, after = roll_rows(cells, 1), roll_rows(cells, -1)
        if below is not None:
            before = jnp.where(plane_at == 0, below(which, own_row), before)
            after = jnp.where(plane_at == PLANES - 1, above(which, own_row), after)
        return before, after

    for side_ref, out_ref, edge, beside, inward, comps in (
        (low_ref, low_side, 0, -1, 1, UP_Y),
        (high_ref, high_side, ROWS - 1, ROWS, -1, DOWN_Y),
    ):
        own = [phase_ref[:, edge + inward * d, :] for d in range(2)]
        outer = [side_ref[side_rows(AT_PHASE + d), :] for d in range(3)]
        lines = [own[1], own[0]] + outer
        potentials = []
        for index in range(1, 4):
            cells = lines[index]
            around = list(across(cells, 0, edge + inward * (1 - index)))
            around += [lines[index - 1], lines[index + 1], roll_lanes(cells, 1), roll_lanes(cells, -1)]
            potentials.append(potential_of(cells, around))
        inside, here, outside = potentials
        before, after = across(here, 1, beside)
        half = -0.5 * outer[0]
        force = [
            half * (after - before),
            (inward * half) * (inside - outside),
            half * (roll_lanes(here, -1) - roll_lanes(here, 1)),
        ]
        flow_post, order_post = collide(
            comps,
            lambda i: side_ref[side_rows(comps.index(i)), :],
            lambda i: side_ref[side_rows(AT_ORDER + comps.index(i)), :],
            side_ref[side_rows(AT_MOMENTS), :],
            [side_ref[side_rows(AT_MOMENTS + 1 + d), :] for d in range(3)],
            outer[0],
            here,
            force,
        )
        for index, i in enumerate(comps):
            out_ref[index] = flow_post[i]
            out_ref[5 + index] = order_post[i]
        edge_ref[0 if inward == 1 else 1] = here


def plane_potential(phase_ref, low_ref, high_ref, x):
    cells = phase_ref[x]
    around = [
        phase_ref[x - 1],
        phase_ref[x + 1],
        rows_before(cells, side_row(low_ref, AT_PHASE, x)),
        rows_after(cells, side_row(high_ref, AT_PHASE, x)),
        roll_lanes(cells, 1),
        roll_lanes(cells, -1),
    ]
    return potential_of(cells, around)


def collide_plane(x, skip, flow_ref, order_ref, phase_ref, potential_ref, edge_ref, low_side, high_side, flow_out, order_out):
    here = potential_ref[x + 1]
    phase = phase_ref[x]
    half = -0.5 * phase
    along_y = rows_after(here, edge_ref[1, pl.ds(x, 1), :]) - rows_before(here, edge_ref[0, pl.ds(x, 1), :])
    force = [
        half * (potential_ref[x + 2] - potential_ref[x]),
        half * along_y,
        half * (roll_lanes(here, -1) - roll_lanes(here, 1)),
    ]
    density, momentum = moments(lambda i: flow_ref[i, x])
    flow_post, order_post = collide(
        tuple(i for i in range(VELS) if VELOCITY_X[i] == 0 or VELOCITY_X[i] != skip),
        lambda i: flow_ref[i, x],
        lambda i: order_ref[i, x],
        density,
        momentum,
        phase,
        here,
        force,
    )

    def moved(i, cells, first):
        if VELOCITY_Y[i] == 1:
            cells = rows_before(cells, low_side[first + UP_Y.index(i), pl.ds(x, 1), :])
        elif VELOCITY_Y[i] == -1:
            cells = rows_after(cells, high_side[first + DOWN_Y.index(i), pl.ds(x, 1), :])
        if VELOCITY_Z[i] != 0:
            cells = roll_lanes(cells, VELOCITY_Z[i])
        return cells

    for i in flow_post:
        target = x + VELOCITY_X[i]
        flow_out[i, target] = moved(i, flow_post[i], 0)
        order_out[i, target] = moved(i, order_post[i], 5)


def main_kernel(
    offset_hbm, flow_ref, order_ref, wide_pack, narrow_pack, minus_hbm, same_hbm, plus_hbm, odd_hbm, flow_hbm_out, order_hbm_out,
    offset_ref, minus_ref, same_ref, plus_ref, odd_ref, low_ref, high_ref, flow_out, order_out, phase_ref, below_ref, above_ref, wide_ref, ghost_ref, potential_ref, low_side, high_side, edge_ref,
    arrival_sems, flow_out_sems, order_out_sems,
):
    pairs = ((minus_hbm, minus_ref), (same_hbm, same_ref), (plus_hbm, plus_ref), (odd_hbm, odd_ref))
    pairs += ((offset_hbm, offset_ref),)
    arrivals = [pltpu.make_async_copy(a, b, arrival_sems.at[index]) for index, (a, b) in enumerate(pairs)]
    for copy in arrivals:
        copy.start()
    flow_writes = plane_copies(flow_out, flow_hbm_out, flow_out_sems, STORES)
    order_writes = plane_copies(order_out, order_hbm_out, order_out_sems, STORES)

    def one_plane(x, skip):
        collide_plane(
            x, skip, flow_ref, order_ref, phase_ref, potential_ref, edge_ref, low_side, high_side, flow_out, order_out
        )

    slab = lax.axis_index("gx")
    is_even = slab % 2 == 0
    for index in range(PAYLOAD):
        wide, narrow = wide_pack[side_rows(index, WIDE_PACK), :], narrow_pack[side_rows(index, NARROW_PACK), :]
        low_ref[side_rows(index), :] = jnp.where(is_even, wide, narrow)
        high_ref[side_rows(index), :] = jnp.where(is_even, narrow, wide)
    for x in range(PLANES):
        add_phase(phase_ref, order_ref, x)
    collide_sides(phase_ref, low_ref, high_ref, None, None, low_side, high_side, edge_ref)
    for x in range(1, PLANES - 1):
        potential_ref[x + 1] = plane_potential(phase_ref, low_ref, high_ref, x)

    def step(x, carry):
        one_plane(x, 0)
        return carry

    for part, (first, last) in enumerate(((2, 8), (8, PLANES - 2))):
        lax.fori_loop(first, last, step, 0, unroll=3)
        flow_writes[part].start()
        order_writes[part].start()
    for copy in arrivals:
        copy.wait()
    inner = lax.rem(offset_ref[even_boundary(slab)] + 5, ROWS)
    blocks = [
        lambda at: jnp.where(
            is_even,
            packed_block(minus_ref, at, WIDE_ROWS, ROWS - WIDE_ROWS),
            packed_block(plus_ref, at, NARROW_ROWS, ROWS - NARROW_ROWS),
        ),
        lambda at: same_ref[at],
        lambda at: jnp.where(
            is_even, packed_block(plus_ref, at, NARROW_ROWS, 0), packed_block(minus_ref, at, WIDE_ROWS, 0)
        ),
    ]
    cut_window(blocks, jnp.where(is_even, inner, 9 - inner), above_ref)
    for index in range(PAYLOAD):
        start = window_row(index)
        even, odd = above_ref[index], odd_ref[start : start + WINDOW, :]
        below_ref[index] = jnp.where(is_even, odd, even)
        above_ref[index] = jnp.where(is_even, even, odd)

    for index, plane in enumerate((0, 1, PLANES - 1, PLANES - 2)):
        wide_ref[index] = jnp.zeros((WINDOW, LANES), jnp.float32)
        for d in range(3):
            wide_ref[index, 3 - d : 4 - d, :] = side_row(low_ref, AT_PHASE + d, plane)
            wide_ref[index, 12 + d : 13 + d, :] = side_row(high_ref, AT_PHASE + d, plane)
        wide_ref[index, 4:12, :] = phase_ref[plane]
    below = ghost_plane(below_ref, UP_X, wide_ref[0], wide_ref[1], 1.0 - SHIFT_FRACTION, WALL_SPEED)
    above = ghost_plane(above_ref, DOWN_X, wide_ref[2], wide_ref[3], SHIFT_FRACTION, -WALL_SPEED)
    for index in range(5):
        ghost_ref[index] = below[3][index]
        ghost_ref[5 + index] = below[4][index]
        ghost_ref[10 + index] = above[3][index]
        ghost_ref[15 + index] = above[4][index]

    def ghost_row(ghost):
        return lambda which, own_row: ghost[2 * which][own_row + WINDOW_PAD : own_row + WINDOW_PAD + 1, :]

    collide_sides(
        phase_ref, low_ref, high_ref, ghost_row(below), ghost_row(above), low_side, high_side, edge_ref
    )
    wide_ref[0] = below[1]
    wide_ref[1] = below[2]
    wide_ref[2] = above[1]
    wide_ref[3] = above[2]
    potential_ref[1] = wide_ref[0, 4:12, :]
    potential_ref[0] = wide_ref[1, 4:12, :]
    potential_ref[PLANES] = wide_ref[2, 4:12, :]
    potential_ref[PLANES + 1] = wide_ref[3, 4:12, :]
    for comps, first, target in ((UP_X, 0, 0), (DOWN_X, 10, PLANES - 1)):
        for index, i in enumerate(comps):
            start = WINDOW_PAD - VELOCITY_Y[i]
            for out_ref, at in ((flow_out, first + index), (order_out, first + 5 + index)):
                cells = ghost_ref[at, start : start + ROWS, :]
                if VELOCITY_Z[i] != 0:
                    cells = roll_lanes(cells, VELOCITY_Z[i])
                out_ref[i, target] = cells
    one_plane(0, -1)
    one_plane(1, 0)
    flow_writes[-2].start()
    order_writes[-2].start()
    one_plane(PLANES - 2, 0)
    one_plane(PLANES - 1, 1)
    flow_writes[-1].start()
    order_writes[-1].start()
    for copy in flow_writes + order_writes:
        copy.wait()


def vmem(count):
    return [pl.BlockSpec(memory_space=pltpu.VMEM)] * count


def params(limit):
    return pltpu.CompilerParams(vmem_limit_bytes=limit)


def f32(*shape):
    return jax.ShapeDtypeStruct(shape, jnp.float32)


def turn_pairs(slabs, strips, step):
    pairs = []
    for slab in range(slabs):
        for strip in range(strips):
            other = (strip + (step if slab % 2 == 0 else -step)) % strips
            pairs.append((slab * strips + strip, slab * strips + other))
    return pairs


def swap_pairs(slabs, strips, first, step):
    pairs = []
    for low in range(first, slabs, 2):
        high = (low + 1) % slabs
        for strip in range(strips):
            other = (strip + step) % strips
            pairs.append((low * strips + strip, high * strips + other))
            pairs.append((high * strips + other, low * strips + strip))
    return pairs


def hbm(count):
    return [pl.BlockSpec(memory_space=pltpu.HBM)] * count


def smem():
    return [pl.BlockSpec(memory_space=pltpu.SMEM)]


def scratch(*shape):
    return pltpu.VMEM(shape, jnp.float32)


def sems(count):
    return pltpu.SemaphoreType.DMA((count,))


def main_planes(plane_offsets, flow, order, wide, narrow, blocks, odd):
    return pl.pallas_call(
        main_kernel,
        out_shape=(f32(*flow.shape), f32(*order.shape)),
        in_specs=hbm(1) + vmem(4) + hbm(4),
        out_specs=tuple(hbm(2)),
        scratch_shapes=[
            pltpu.SMEM(plane_offsets.shape, jnp.int32),
            scratch(WIDE_PACK, LANES),
            scratch(PAYLOAD, ROWS, LANES),
            scratch(NARROW_PACK, LANES),
            scratch(SENT, LANES),
            scratch(SIDE, LANES),
            scratch(SIDE, LANES),
            scratch(*flow.shape),
            scratch(*order.shape),
            scratch(PLANES, ROWS, LANES),
            scratch(PAYLOAD, WINDOW, LANES),
            scratch(PAYLOAD, WINDOW, LANES),
            scratch(4, WINDOW, LANES),
            scratch(20, WINDOW, LANES),
            scratch(PLANES + 2, ROWS, LANES),
            scratch(10, PLANES, LANES),
            scratch(10, PLANES, LANES),
            scratch(2, PLANES, LANES),
            sems(5),
            sems(len(STORES)),
            sems(len(STORES)),
        ],
        compiler_params=params(MAIN_VMEM),
        name="collide_stream",
    )(plane_offsets, flow, order, wide, narrow, *blocks, odd)


def shards(populations, order_pops, plane_offsets):
    slabs, strips = lax.axis_size("gx"), lax.axis_size("gy")
    slab = lax.axis_index("gx")
    shifts = ((plane_offsets + 5) // ROWS) % strips
    boundary = lax.iota(jnp.int32, slabs)
    at_even = jnp.where(boundary == (slab | 1), strips, 0)
    at_odd = jnp.where(boundary == ((slab + (slab & 1)) & (slabs - 1)), 1, 0)
    code = jnp.sum(shifts * (at_even + at_odd)).astype(jnp.uint32)
    even_step = (code // jnp.uint32(strips)).astype(jnp.int32)
    odd_step = lax.rem(code, jnp.uint32(strips)).astype(jnp.int32)

    minus, same, plus, own, wide, narrow = pl.pallas_call(
        payload_kernel,
        out_shape=(
            f32(WIDE_PACK, LANES),
            f32(PAYLOAD, ROWS, LANES),
            f32(NARROW_PACK, LANES),
            f32(PAYLOAD, ROWS, LANES),
            f32(WIDE_PACK + SIDE, LANES),
            f32(NARROW_PACK + SIDE, LANES),
        ),
        in_specs=vmem(2),
        out_specs=tuple(vmem(6)),
        scratch_shapes=[scratch(PLANES, ROWS, LANES)],
        compiler_params=params(SMALL_VMEM),
        name="payloads",
    )(populations, order_pops)

    wide = lax.ppermute(wide, ("gx", "gy"), turn_pairs(slabs, strips, 1))
    narrow = lax.ppermute(narrow, ("gx", "gy"), turn_pairs(slabs, strips, -1))

    def even_branch(step):
        def run(*payloads):
            return tuple(
                lax.ppermute(mine, ("gx", "gy"), swap_pairs(slabs, strips, 0, step + d))
                for d, mine in zip((-1, 0, 1), payloads)
            )

        return run

    blocks = lax.switch(even_step, [even_branch(step) for step in range(strips)], minus, same, plus)
    wide, narrow, blocks = lax.optimization_barrier((wide, narrow, blocks))
    window = pl.pallas_call(
        window_kernel,
        out_shape=f32(SENT, LANES),
        in_specs=smem() + vmem(3),
        out_specs=vmem(1)[0],
        scratch_shapes=[scratch(PAYLOAD, WINDOW, LANES)],
        compiler_params=params(SMALL_VMEM),
        name="window",
    )(plane_offsets, wide, own, narrow)

    def odd_branch(step):
        return lambda mine: lax.ppermute(mine, ("gx", "gy"), swap_pairs(slabs, strips, 1, step))

    odd = lax.switch(odd_step, [odd_branch(step) for step in range(strips)], window)
    return main_planes(plane_offsets, populations, order_pops, wide, narrow, blocks, odd)


def solution(mesh):
    return jax.shard_map(
        shards,
        mesh=mesh,
        in_specs=(P(None, "gx", "gy", None), P(None, "gx", "gy", None), P()),
        out_specs=(P(None, "gx", "gy", None), P(None, "gx", "gy", None)),
        check_vma=False,
    )
```
